128 devices in a mesh: led: 32 (over y, x, core), tile: 4 (over z).
Axes of the slice: x: 4, y: 4, z: 4, core: 2. Of those that a mesh axis runs over, the one named last changes fastest.
Arguments:
- spectrum: bfloat16 [1024, 2048], replicated, may hold values from -6 to 6
- pupils: bfloat16 [4, 512, 1024], replicated, may hold values from -1.5 to 1.5
- offsets: int32 [128, 2], P(('led', 'tile')), may hold values from 0 to 512
- measured: bfloat16 [128, 512, 512], P(('led', 'tile')), may hold values from 0.099609375 to 4
Outputs:
- spectrum_grad: float32 [4, 256, 2048], P('tile', 'led')
- pupil_grad: float32 [4, 512, 1024], P(None, 'led')
The draws below stay inside these ranges and needn't reach their ends.
Inputs may be any that keep to these rules, and one draw needn't show every extreme that they name: `offsets`: each patch lies inside the spectrum.
All inputs are finite; a program needn't handle non-finite values.
Results may differ from the reference program's by a relative error of at most 0.011.
Values sent between devices are 32-bit elements; how exact they have to be, the bound alone decides.
A program may use at most 128 MiB of HBM per device.

```python
import math
import jax
import jax.numpy as jnp
from jax import lax

PATCH = 512
MODES = 4
LEDS = 128
STRIP = 256
SPEC = 1024
N_TILE = 4


def touch_ends(values, own_key, low, largest):
    index_at = [jax.random.randint(jax.random.fold_in(own_key, axis), (), 0, length) for axis, length in enumerate(values.shape)]
    main_axis = values.shape.index(max(values.shape))
    beside = index_at[:main_axis] + [(index_at[main_axis] + 1) % values.shape[main_axis]] + index_at[main_axis + 1:]
    return values.at[tuple(index_at)].set(low).at[tuple(beside)].set(largest)


def block_levels(rng, dims, shards, smallest, top_value):
    loudness, own = 1.0, jax.random.fold_in(rng, 6)
    for position, blocks in shards:
        heights = jnp.exp(jax.random.uniform(jax.random.fold_in(own, position), (blocks,), jnp.float32, smallest / len(shards), top_value / len(shards)))
        loudness = loudness * jnp.repeat(heights, dims[position] // blocks).reshape([-1 if axis == position else 1 for axis in range(len(dims))])
    return loudness


def bell_draw(own_key, shape, spread, most, held_as=jnp.bfloat16):
    drawn = jax.random.normal(own_key, shape, jnp.float32) * spread
    return jnp.minimum(jnp.maximum(drawn, -most), most).astype(held_as)


def setup_inputs(seed: int = 0) -> dict:
    seeds = jax.random.split(jax.random.key(seed), 5)
    spectrum = bell_draw(seeds[0], (SPEC, 2 * SPEC), 1.0, 6.0)
    pupils = bell_draw(seeds[1], (MODES, PATCH, 2 * PATCH), 0.25, 1.5)
    offsets = touch_ends(jax.random.randint(seeds[2], (LEDS, 2), 0, SPEC - PATCH + 1), jax.random.fold_in(seeds[2], 1), 0, SPEC - PATCH).astype(jnp.int32)
    measured = jnp.clip(jnp.exp(math.log(4.0) - 3.6927934 * jax.random.uniform(seeds[3], (LEDS, PATCH, PATCH), jnp.float32) ** block_levels(seeds[3], (LEDS, PATCH, PATCH), ((0, 128),), -0.2, 0.2)), 0.099609375, 4.0).astype(jnp.bfloat16)
    return dict(spectrum=spectrum, pupils=pupils, offsets=offsets, measured=measured)


def dft_tables(length):
    positions = jnp.arange(length, dtype=jnp.int32)
    angles = (positions[:, None] * positions[None, :] % length).astype(jnp.float32) * (2.0 * math.pi / length)
    factor = 1.0 / math.sqrt(length)
    return ((jnp.cos(angles) * factor).astype(jnp.bfloat16), (jnp.sin(angles) * factor).astype(jnp.bfloat16))

def product(form, left, right):
    return jnp.einsum(form, left.astype(jnp.float32), right.astype(jnp.float32), precision=lax.Precision.HIGHEST)

def emitter_model(patch_real, patch_imaginary, pupils, intensity_measurement, cosine_lookup, sine_lookup):
    length = patch_real.shape[0]
    pupil_re = pupils[:, :, :length].astype(jnp.float32)
    pupil_im = pupils[:, :, length:].astype(jnp.float32)
    real_part = patch_real.astype(jnp.float32)[None]
    imag_part = patch_imaginary.astype(jnp.float32)[None]
    exit_field = jnp.concatenate([real_part * pupil_re - imag_part * pupil_im, real_part * pupil_im + imag_part * pupil_re], axis=2).astype(jnp.bfloat16)
    cos_rows = product('jk,mkc->mjc', cosine_lookup, exit_field)
    sin_rows = product('jk,mkc->mjc', sine_lookup, exit_field)
    half_re = cos_rows[:, :, :length] - sin_rows[:, :, length:]
    half_im = cos_rows[:, :, length:] + sin_rows[:, :, :length]
    stacked = jnp.concatenate([half_re, half_im], axis=1).astype(jnp.bfloat16)
    cos_cols = product('mjk,kl->mjl', stacked, cosine_lookup)
    sin_cols = product('mjk,kl->mjl', stacked, sine_lookup)
    field_re = cos_cols[:, :length] - sin_cols[:, length:]
    field_im = cos_cols[:, length:] + sin_cols[:, :length]
    predicted_intensity = lax.optimization_barrier(jnp.sum(field_re * field_re + field_im * field_im, axis=0))
    mode_weight = 1.0 - jnp.sqrt(intensity_measurement.astype(jnp.float32) / jnp.maximum(predicted_intensity, 0.1))
    back_field = jnp.concatenate([mode_weight * field_re, mode_weight * field_im], axis=2).astype(jnp.bfloat16)
    cos_rows = product('jk,mkc->mjc', cosine_lookup, back_field)
    sin_rows = product('jk,mkc->mjc', sine_lookup, back_field)
    fore_re = cos_rows[:, :, :length] + sin_rows[:, :, length:]
    fore_im = cos_rows[:, :, length:] - sin_rows[:, :, :length]
    stacked = jnp.concatenate([fore_re, fore_im], axis=1).astype(jnp.bfloat16)
    cos_cols = product('mjk,kl->mjl', stacked, cosine_lookup)
    sin_cols = product('mjk,kl->mjl', stacked, sine_lookup)
    grad_re = cos_cols[:, :length] + sin_cols[:, length:]
    grad_im = cos_cols[:, length:] - sin_cols[:, :length]
    patch_grad = jnp.concatenate([lax.optimization_barrier(jnp.sum(pupil_re * grad_re + pupil_im * grad_im, axis=0)), lax.optimization_barrier(jnp.sum(pupil_re * grad_im - pupil_im * grad_re, axis=0))], axis=1)
    pupil_term = jnp.concatenate([real_part * grad_re + imag_part * grad_im, real_part * grad_im - imag_part * grad_re], axis=2)
    return (patch_grad, pupil_term)

def add_block(canvas, block, row_start, col_start):
    current = lax.dynamic_slice(canvas, (row_start, col_start), block.shape)
    return lax.dynamic_update_slice(canvas, current + block, (row_start, col_start))

def reference(spectrum, pupils, offsets, measured):
    cosine_lookup, sine_lookup = dft_tables(PATCH)

    def step(number, carry):
        canvas, pupil_sum = carry
        row_start = offsets[number, 0].astype(jnp.int32)
        col_start = offsets[number, 1].astype(jnp.int32)
        patch_real = lax.dynamic_slice(spectrum, (row_start, col_start), (PATCH, PATCH))
        patch_imaginary = lax.dynamic_slice(spectrum, (row_start, col_start + SPEC), (PATCH, PATCH))
        patch_grad, pupil_term = emitter_model(patch_real, patch_imaginary, pupils, measured[number], cosine_lookup, sine_lookup)
        canvas = add_block(canvas, patch_grad[:, :PATCH], row_start, col_start)
        canvas = add_block(canvas, patch_grad[:, PATCH:], row_start, col_start + SPEC)
        return (canvas, pupil_sum + pupil_term)
    start = (jnp.zeros((SPEC, 2 * SPEC), jnp.float32), jnp.zeros((MODES, PATCH, 2 * PATCH), jnp.float32))
    canvas, pupil_sum = lax.fori_loop(0, LEDS, step, start)
    return (canvas.reshape(N_TILE, STRIP, 2 * SPEC), pupil_sum)
```

```python
import math

import jax
import jax.numpy as jnp
import numpy as np
from jax import lax
from jax.experimental import pallas as pl
from jax.experimental.pallas import tpu as pltpu
from jax.sharding import PartitionSpec as P

MESH = pl.DeviceIdType.MESH
N = 512
H = 256
MODES = 4
SPEC = 1024
F32 = jnp.float32
BF16 = jnp.bfloat16

DIMS = (("y", 0), ("x", 0), ("z", 0), ("y", 1), ("x", 1), ("z", 1))

PUPIL_PHASES = (
    (0, 1, 2, 3),
    (4, 5, 0, 1),
    (2, 3, 4, 5),
    (0, 1, 2, 3),
)
CANVAS_PHASES = (
    (0, 1, 2, 3, 4, 4, 5, 5),
    (0, 1, 2, 2, 3, 3, 4, 5),
)
STREAMS = 6


def plan():
    counts = [0] * STREAMS
    place = {}
    groups = []
    for number, streams in enumerate(PUPIL_PHASES + CANVAS_PHASES):
        first = list(counts)
        for unit, stream in enumerate(streams):
            place[number, unit] = (stream, counts[stream])
            counts[stream] += 1
        for stream in range(STREAMS):
            if counts[stream] > first[stream]:
                groups.append((number, stream, first[stream], counts[stream]))
    return counts, place, groups


COUNTS, PLACE, GROUPS = plan()


def tables():
    positions = np.arange(N, dtype=np.int64)
    angles = (positions[:, None] * positions[None, :] % N).astype(np.float32) * np.float32(2.0 * math.pi / N)
    factor = np.float32(1.0 / math.sqrt(N))
    cosine = (np.cos(angles) * factor).astype(BF16)
    sine = (np.sin(angles) * factor).astype(BF16)
    half = np.concatenate([cosine[:H], sine[:H]], axis=0)
    half[H] = cosine[H]
    swap = np.zeros((H, H), np.float32)
    swap[(H - np.arange(H)) % H, np.arange(H)] = 1.0
    return half, np.ascontiguousarray(half.T), swap.astype(BF16)


def low_bit(position):
    return ((position + 1) // 2) % 2


def high_bit(position):
    return position // 2


def bits_of(y, x, z):
    return {
        ("y", 0): low_bit(y), ("y", 1): high_bit(y),
        ("x", 0): low_bit(x), ("x", 1): high_bit(x),
        ("z", 0): low_bit(z), ("z", 1): high_bit(z),
    }


def slot_of(bits, stream):
    slot = 0
    for step in range(6):
        slot = slot * 2 + bits[DIMS[(stream + step) % 6]]
    return slot


def dot(a, b):
    return jnp.dot(a, b, preferred_element_type=F32)


def kernel(mark, patch, pup, meas, tab, tabt, swap, out_spec, out_pup, *scratch):
    (half_s, field, inten, measp, xs, grads, folded, shift_rows, shift_cols, parts, parts_t, part, part_mark,
     peer, pupil_src, canvas_src) = scratch[:16]
    own = scratch[16:22]
    landed = scratch[22:28]
    (core_send, core_recv, send, recv, gather_send, gather_recv) = scratch[28:]

    led = lax.axis_index("led")
    z = lax.axis_index("tile")
    core = led % 2
    x = (led // 2) % 4
    y = led // 8
    other = 1 - core

    def device(yy, xx, cc, zz):
        return ((yy * 4 + xx) * 2 + cc, zz)

    def low(p):
        return p + 1 - 2 * (p % 2)

    def high(p):
        return 3 - p

    neighbour = {
        ("y", 0): device(low(y), x, core, z), ("y", 1): device(high(y), x, core, z),
        ("x", 0): device(y, low(x), core, z), ("x", 1): device(y, high(x), core, z),
        ("z", 0): device(y, x, core, low(z)), ("z", 1): device(y, x, core, high(z)),
    }
    partner = device(y, x, other, z)
    mine = bits_of(y, x, z)
    column = [(c, d) for d in range(4) for c in range(2) if (c, d) != (0, 0)]

    barrier = pltpu.get_barrier_semaphore()
    greeted = [neighbour["y", 0], neighbour["y", 1], neighbour["x", 0], neighbour["x", 1]]
    greeted += [device(y, x, (core + c) % 2, (z + d) % 4) for c, d in column]
    for target in greeted:
        pl.semaphore_signal(barrier, inc=1, device_id=target, device_id_type=MESH)

    measp[:, :H] = meas[0, :, :H]
    measp[:, H:] = dot(meas[0, :, H:], swap[...]).astype(BF16)
    measp[H:, :] = dot(swap[...], measp[H:, :]).astype(BF16)
    inten[...] = jnp.zeros_like(inten)

    lane0 = lax.broadcasted_iota(jnp.int32, (1, 128), 1) == 0
    row0 = lax.broadcasted_iota(jnp.int32, (16, 1), 0) == 0

    def forward(m, carry):
        for c in range(2):
            cols = slice(c * H, (c + 1) * H)
            cols_i = slice(N + c * H, N + (c + 1) * H)
            pr = patch[:, cols].astype(F32)
            pi = patch[:, cols_i].astype(F32)
            qr = pup[m, :, cols].astype(F32)
            qi = pup[m, :, cols_i].astype(F32)
            er = (pr * qr - pi * qi).astype(BF16)
            ei = (pr * qi + pi * qr).astype(BF16)
            u = dot(tab[...], er)
            v = dot(tab[...], ei)
            half_s[0, :H, cols] = (u[:H] - v[H:]).astype(BF16)
            half_s[0, H:, cols] = (u[:H] + v[H:]).astype(BF16)
            half_s[1, :H, cols] = (v[:H] + u[H:]).astype(BF16)
            half_s[1, H:, cols] = (v[:H] - u[H:]).astype(BF16)
            ut, ub, vt, vb = u[:16], u[H:H + 16], v[:16], v[H:H + 16]
            half_s[0, :16, cols] = jnp.where(row0, ut, ut - vb).astype(BF16)
            half_s[0, H:H + 16, cols] = jnp.where(row0, ub, ut + vb).astype(BF16)
            half_s[1, :16, cols] = jnp.where(row0, vt, vt + ub).astype(BF16)
            half_s[1, H:H + 16, cols] = jnp.where(row0, vb, vt - ub).astype(BF16)
        for r in range(2):
            rows = slice(r * H, (r + 1) * H)
            u = dot(half_s[0, rows, :], tabt[...])
            v = dot(half_s[1, rows, :], tabt[...])
            for b in range(2):
                left = slice(b * 128, (b + 1) * 128)
                right = slice(H + b * 128, H + (b + 1) * 128)
                uc, us, vc, vs = u[:, left], u[:, right], v[:, left], v[:, right]
                rl, il, rr, ir = uc - vs, vc + us, uc + vs, vc - us
                if b == 0:
                    rl = jnp.where(lane0, uc, rl)
                    il = jnp.where(lane0, vc, il)
                    rr = jnp.where(lane0, us, rr)
                    ir = jnp.where(lane0, vs, ir)
                field[0, m, rows, left] = rl
                field[1, m, rows, left] = il
                field[0, m, rows, right] = rr
                field[1, m, rows, right] = ir
                inten[rows, left] += rl * rl + il * il
                inten[rows, right] += rr * rr + ir * ir
        return carry

    lax.fori_loop(0, MODES, forward, 0)

    def weigh(i, carry):
        rows = pl.ds(pl.multiple_of(i * 64, 64), 64)
        level = measp[rows, :].astype(F32)
        inten[rows, :] = 1.0 - level * lax.rsqrt(level * jnp.maximum(inten[rows, :], 0.1))
        return carry

    lax.fori_loop(0, N // 64, weigh, 0)

    def backward(m):
        def fold(i, carry):
            top = pl.ds(pl.multiple_of(i * 32, 32), 32)
            bottom = pl.ds(pl.multiple_of(H + i * 32, 32), 32)
            wt, wb = inten[top, :], inten[bottom, :]
            rt, rb = wt * field[0, m, top, :], wb * field[0, m, bottom, :]
            it, ib = wt * field[1, m, top, :], wb * field[1, m, bottom, :]
            xs[0, top, :] = (rt + rb).astype(BF16)
            xs[0, bottom, :] = (it - ib).astype(BF16)
            xs[1, top, :] = (it + ib).astype(BF16)
            xs[1, bottom, :] = (rb - rt).astype(BF16)
            return carry

        lax.fori_loop(0, H // 32, fold, 0)
        wt, wb = inten[:16, :], inten[H:H + 16, :]
        rt, rb = wt * field[0, m, :16, :], wb * field[0, m, H:H + 16, :]
        it, ib = wt * field[1, m, :16, :], wb * field[1, m, H:H + 16, :]
        xs[0, :16, :] = jnp.where(row0, rt, rt + rb).astype(BF16)
        xs[0, H:H + 16, :] = jnp.where(row0, rb, it - ib).astype(BF16)
        xs[1, :16, :] = jnp.where(row0, it, it + ib).astype(BF16)
        xs[1, H:H + 16, :] = jnp.where(row0, ib, rb - rt).astype(BF16)

        def rows_of(i, carry):
            rows = pl.ds(pl.multiple_of(i * H, H), H)
            fr = dot(tabt[rows, :], xs[0])
            fi = dot(tabt[rows, :], xs[1])
            for b in range(2):
                left = slice(b * 128, (b + 1) * 128)
                right = slice(H + b * 128, H + (b + 1) * 128)
                rl, rr, il, ir = fr[:, left], fr[:, right], fi[:, left], fi[:, right]
                pr, mi, p_i, mr = rl + rr, il - ir, il + ir, rr - rl
                if b == 0:
                    pr = jnp.where(lane0, rl, pr)
                    mi = jnp.where(lane0, rr, mi)
                    p_i = jnp.where(lane0, il, p_i)
                    mr = jnp.where(lane0, ir, mr)
                half_s[0, rows, left] = pr.astype(BF16)
                half_s[0, rows, right] = mi.astype(BF16)
                half_s[1, rows, left] = p_i.astype(BF16)
                half_s[1, rows, right] = mr.astype(BF16)
            gr = dot(half_s[0, rows, :], tab[...])
            gi = dot(half_s[1, rows, :], tab[...])
            qr, qi = pup[m, rows, :N].astype(F32), pup[m, rows, N:].astype(F32)
            sr = qr * gr + qi * gi
            si = qr * gi - qi * gr
            if m == 0:
                grads[0, rows, :] = sr
                grads[1, rows, :] = si
            else:
                grads[0, rows, :] += sr
                grads[1, rows, :] += si
            pr, pi = patch[rows, :N].astype(F32), patch[rows, N:].astype(F32)
            field[0, m, rows, :] = pr * gr + pi * gi
            field[1, m, rows, :] = pr * gi - pi * gr
            return carry

        lax.fori_loop(0, 2, rows_of, 0)

    def core_copy(m):
        return pltpu.make_async_remote_copy(
            src_ref=field.at[other, m], dst_ref=peer.at[m], send_sem=core_send.at[m],
            recv_sem=core_recv.at[m], device_id=partner, device_id_type=MESH)

    def starts(stream):
        begin, out = 0, []
        for step in range(6):
            bit = mine[DIMS[(stream + step) % 6]]
            length = 32 >> step
            out.append((begin + bit * length, begin + (1 - bit) * length, length, 64 - 2 * length))
            begin = begin + bit * length
        return out, begin

    ranges = [starts(stream) for stream in range(STREAMS)]

    def hop(index, step):
        _, stream, first, last = GROUPS[index]
        _, away, length, offset = ranges[stream][0][step]
        units = pl.ds(first, last - first)
        return pltpu.make_async_remote_copy(
            src_ref=own[stream].at[units, pl.ds(away, length)],
            dst_ref=landed[stream].at[units, pl.ds(offset, length)],
            send_sem=send.at[index, step], recv_sem=recv.at[index, step],
            device_id=neighbour[DIMS[(stream + step) % 6]], device_id_type=MESH)

    def launch(phase):
        for index, group in enumerate(GROUPS):
            if group[0] == phase:
                hop(index, 0).start()

    def advance(phase, step):
        for index, (number, stream, first, last) in enumerate(GROUPS):
            if number != phase:
                continue
            hop(index, step).wait()
            keep, _, length, offset = ranges[stream][0][step]
            for unit in range(first, last):
                own[stream][unit, pl.ds(keep, length)] += landed[stream][unit, pl.ds(offset, length)]
            if step < 5:
                hop(index, step + 1).start()

    def spread_pupil(m):
        core_copy(m).wait()

        def body(yx, carry):
            for zz in range(4):
                bits = bits_of(yx // 4, yx % 4, zz)
                cols = slice(zz * 128, (zz + 1) * 128)
                for g in range(4):
                    stream, unit = PLACE[m, g]
                    rows = pl.ds(pl.multiple_of(yx * 32 + g * 8, 8), 8)
                    own[stream][unit, slot_of(bits, stream)] = field[core, m, rows, cols] + peer[m, rows, cols]
            return carry

        lax.fori_loop(0, 16, body, 0)
        launch(m)

    backward(0)
    pl.semaphore_wait(barrier, len(greeted))
    core_copy(0).start()
    backward(1)
    core_copy(1).start()
    spread_pupil(0)
    backward(2)
    core_copy(2).start()
    spread_pupil(1)
    advance(0, 0)
    backward(3)
    core_copy(3).start()
    advance(0, 1)
    advance(1, 0)
    spread_pupil(2)

    along = lax.broadcasted_iota(jnp.int32, (N, 128), 1).astype(F32)
    down = lax.broadcasted_iota(jnp.int32, (N, 128), 0).astype(F32)

    def wrap(value):
        return jnp.where(value >= float(N), value - float(N), value)

    for b in range(8):
        at = slice(b * 128, (b + 1) * 128)
        to = wrap(wrap(along + float(b % 4 * 128)) + mark[0, :1, :])
        shift_rows[:, at] = (down == wrap(to)).astype(F32).astype(BF16)
    for b in range(4):
        at = slice(b * 128, (b + 1) * 128)
        to = wrap(wrap(down + mark[1, :1, :]))
        hit = (along + float(b * 128) == to).astype(F32).astype(BF16)
        shift_cols[:N, at] = hit
        shift_cols[N:, at] = hit
    for part_no in range(2):
        whole = grads[part_no]
        coarse = whole.astype(BF16)
        parts[:N, :] = coarse
        parts[N:, :] = (whole - coarse.astype(F32)).astype(BF16)
        whole = dot(shift_rows[...], parts[...])
        coarse = whole.astype(BF16)
        parts_t[:, :N] = coarse
        parts_t[:, N:] = (whole - coarse.astype(F32)).astype(BF16)
        folded[part_no] = dot(parts_t[...], shift_cols[...])

    part_copy = pltpu.make_async_remote_copy(
        src_ref=folded.at[other], dst_ref=part, send_sem=core_send.at[4],
        recv_sem=core_recv.at[4], device_id=partner, device_id_type=MESH)
    mark_copy = pltpu.make_async_remote_copy(
        src_ref=mark, dst_ref=part_mark, send_sem=core_send.at[5],
        recv_sem=core_recv.at[5], device_id=partner, device_id_type=MESH)
    part_copy.start()
    mark_copy.start()
    spread_pupil(3)
    advance(0, 2)
    advance(1, 1)
    advance(2, 0)
    part_copy.wait()
    mark_copy.wait()

    iota_r = lax.broadcasted_iota(jnp.int32, (8, 128), 0).astype(F32)
    iota_c = lax.broadcasted_iota(jnp.int32, (8, 128), 1).astype(F32)

    def window(yx, carry):
        bit_sets = [bits_of(yx // 4, yx % 4, zz) for zz in range(4)]
        for zz in range(2):
            for g in range(2):
                base = 256 * zz + yx * 16 + g * 8
                rows = pl.ds(pl.multiple_of(base, 8), 8)
                row_no = iota_r + base.astype(F32)
                row_a = row_no < mark[0]
                row_b = row_no < part_mark[0]
                for block in range(4):
                    cols = slice(block * 128, (block + 1) * 128)
                    col_no = iota_c + float(block * 128)
                    col_a = col_no < mark[1]
                    col_b = col_no < part_mark[1]
                    value_a = folded[core, rows, cols]
                    value_b = part[rows, cols]
                    ra1 = jnp.where(row_a, value_a, 0.0)
                    ra0 = value_a - ra1
                    rb1 = jnp.where(row_b, value_b, 0.0)
                    rb0 = value_b - rb1
                    for upper, (va, vb) in enumerate(((ra0, rb0), (ra1, rb1))):
                        va1 = jnp.where(col_a, va, 0.0)
                        vb1 = jnp.where(col_b, vb, 0.0)
                        tiles = ((va - va1) + (vb - vb1), va1 + vb1)
                        bits = bit_sets[2 * upper + zz]
                        for later in range(2):
                            stream, unit = PLACE[4 + later, g * 4 + block]
                            own[stream][unit, slot_of(bits, stream)] = tiles[later]
        return carry

    lax.fori_loop(0, 16, window, 0)
    launch(4)
    launch(5)

    for phase, step in ((0, 3), (1, 2), (2, 1), (3, 0), (0, 4), (1, 3), (2, 2), (3, 1), (0, 5), (1, 4), (2, 3), (3, 2),
                        (1, 5), (2, 4), (4, 0), (3, 3), (2, 5), (5, 0), (3, 4), (4, 1), (3, 5)):
        advance(phase, step)

    for m in range(MODES):
        for g in range(4):
            stream, unit = PLACE[m, g]
            pupil_src[m, g * 8:(g + 1) * 8, :] = own[stream][unit, ranges[stream][1]]
    block = pl.ds(pl.multiple_of((core * 4 + z) * 128, 128), 128)
    copies = []
    for number, (c, d) in enumerate(column):
        to_core = (core + c) % 2
        copies.append(pltpu.make_async_remote_copy(
            src_ref=pupil_src.at[:, pl.ds(pl.multiple_of(to_core * 16, 16), 16), :],
            dst_ref=out_pup.at[:, :, block],
            send_sem=gather_send.at[number], recv_sem=gather_recv.at[number],
            device_id=device(y, x, to_core, (z + d) % 4), device_id_type=MESH))
        copies[-1].start()
    out_pup[:, :, block] = pupil_src[:, pl.ds(pl.multiple_of(core * 16, 16), 16), :]

    for phase, step in ((5, 1), (4, 2), (5, 2), (4, 3), (5, 3), (4, 4), (5, 4), (4, 5), (5, 5)):
        advance(phase, step)

    for phase in range(2):
        for g in range(2):
            for b in range(4):
                stream, unit = PLACE[4 + phase, g * 4 + b]
                at = (phase * 4 + b) * 128
                canvas_src[g, :, at:at + 128] = own[stream][unit, ranges[stream][1]]
    half_cols = pl.ds(pl.multiple_of(core * SPEC, SPEC), SPEC)
    last = pltpu.make_async_remote_copy(
        src_ref=canvas_src.at[other], dst_ref=out_spec.at[0, :, half_cols],
        send_sem=gather_send.at[7], recv_sem=gather_recv.at[7], device_id=partner, device_id_type=MESH)
    last.start()
    out_spec[0, :, half_cols] = canvas_src[core]
    for copy in copies:
        copy.wait()
    last.wait()


def local(spectrum, pupils, offsets, measured):
    row, col = offsets[0, 0], offsets[0, 1]
    patch = jnp.concatenate(
        [lax.dynamic_slice(spectrum, (row, col), (N, N)), lax.dynamic_slice(spectrum, (row, col + SPEC), (N, N))],
        axis=1)
    mark = jnp.broadcast_to(offsets.reshape(2, 1, 1).astype(F32), (2, 8, 128))
    half, half_t, swap = (jnp.asarray(table) for table in tables())
    vmem = pl.BlockSpec(memory_space=pltpu.VMEM)
    scratch = [
        pltpu.VMEM((2, N, N), BF16),
        pltpu.VMEM((2, MODES, N, N), F32),
        pltpu.VMEM((N, N), F32),
        pltpu.VMEM((N, N), BF16),
        pltpu.VMEM((2, N, N), BF16),
        pltpu.VMEM((2, N, N), F32),
        pltpu.VMEM((2, N, N), F32),
        pltpu.VMEM((N, 2 * N), BF16),
        pltpu.VMEM((2 * N, N), BF16),
        pltpu.VMEM((2 * N, N), BF16),
        pltpu.VMEM((N, 2 * N), BF16),
        pltpu.VMEM((N, N), F32),
        pltpu.VMEM((2, 8, 128), F32),
        pltpu.VMEM((MODES, N, N), F32),
        pltpu.VMEM((MODES, 32, 128), F32),
        pltpu.VMEM((2, 8, SPEC), F32),
    ]
    scratch += [pltpu.VMEM((count, 64, 8, 128), F32) for count in COUNTS]
    scratch += [pltpu.VMEM((count, 63, 8, 128), F32) for count in COUNTS]
    scratch += [pltpu.SemaphoreType.DMA((6,)), pltpu.SemaphoreType.DMA((6,))]
    scratch += [pltpu.SemaphoreType.DMA((len(GROUPS), 6)), pltpu.SemaphoreType.DMA((len(GROUPS), 6))]
    scratch += [pltpu.SemaphoreType.DMA((8,)), pltpu.SemaphoreType.DMA((8,))]
    return tuple(pl.pallas_call(
        kernel,
        out_shape=(
            jax.ShapeDtypeStruct((1, 8, 2 * SPEC), F32),
            jax.ShapeDtypeStruct((MODES, 16, 2 * N), F32),
        ),
        in_specs=[vmem] * 7,
        out_specs=(vmem, vmem),
        scratch_shapes=scratch,
        compiler_params=pltpu.CompilerParams(
            collective_id=0, has_side_effects=True, vmem_limit_bytes=60 * 2**20),
    )(mark, patch, pupils, measured, half, half_t, swap))


def solution(mesh):
    return jax.shard_map(
        local,
        mesh=mesh,
        in_specs=(P(), P(), P(("led", "tile"), None), P(("led", "tile"), None, None)),
        out_specs=(P("tile", "led", None), P(None, "led", None)),
        check_vma=False,
    )
```

```python
import math

import jax
import jax.numpy as jnp
import numpy as np
from jax import lax
from jax.experimental import pallas as pl
from jax.experimental.pallas import tpu as pltpu
from jax.sharding import PartitionSpec as P

MESH = pl.DeviceIdType.MESH
N = 512
H = 256
MODES = 4
SPEC = 1024
F32 = jnp.float32
BF16 = jnp.bfloat16

DIMS = (("y", 0), ("x", 0), ("z", 0), ("y", 1), ("x", 1), ("z", 1))

STREAMS = 6
PIECES = (
    (0, 1, 2, 3),
    (4, 5, 0, 1),
    (2, 3, 4, 5),
    (0, 1, 2, 3),
    (0, 1, 2, 3, 4, 4, 5, 5, 0, 1, 2, 2, 3, 3, 4, 5),
)
CANVAS = 4
PHASES = ((0, 1, 2, 3), (4,))


def plan():
    counts = [0] * STREAMS
    place, pieces, phases = {}, {}, {}
    for number, streams in enumerate(PIECES):
        first = list(counts)
        for unit, stream in enumerate(streams):
            place[number, unit] = (stream, counts[stream])
            counts[stream] += 1
        for stream in range(STREAMS):
            if counts[stream] > first[stream]:
                pieces[number, stream] = (first[stream], counts[stream])
    for number, members in enumerate(PHASES):
        for stream in range(STREAMS):
            spans = [pieces[member, stream] for member in members if (member, stream) in pieces]
            if spans:
                phases[number, stream] = (spans[0][0], spans[-1][1])
    return counts, place, pieces, phases


COUNTS, PLACE, PIECE_SPANS, PHASE_SPANS = plan()


def tables():
    positions = np.arange(N, dtype=np.int64)
    angles = (positions[:, None] * positions[None, :] % N).astype(np.float32) * np.float32(2.0 * math.pi / N)
    factor = np.float32(1.0 / math.sqrt(N))
    cosine = (np.cos(angles) * factor).astype(BF16)
    sine = (np.sin(angles) * factor).astype(BF16)
    half = np.concatenate([cosine[:H], sine[:H]], axis=0)
    half[H] = cosine[H]
    swap = np.zeros((H, H), np.float32)
    swap[(H - np.arange(H)) % H, np.arange(H)] = 1.0
    return half, np.ascontiguousarray(half.T), swap.astype(BF16)


def low_bit(position):
    return ((position + 1) // 2) % 2


def high_bit(position):
    return position // 2


def bits_of(y, x, z):
    return {
        ("y", 0): low_bit(y), ("y", 1): high_bit(y),
        ("x", 0): low_bit(x), ("x", 1): high_bit(x),
        ("z", 0): low_bit(z), ("z", 1): high_bit(z),
    }


def slot_of(bits, stream):
    slot = 0
    for step in range(6):
        slot = slot * 2 + bits[DIMS[(stream + step) % 6]]
    return slot


def dot(a, b):
    return jnp.dot(a, b, preferred_element_type=F32)


def extract(offs, spectrum, patch, mark, window, aligned, sem):
    row, col = offs[0, 0], offs[0, 1]
    row_from = pl.multiple_of(jnp.minimum(row // 16 * 16, N - 16), 16)
    col_from = pl.multiple_of(jnp.minimum(col // 128 * 128, N - 128), 128)
    copies = [
        pltpu.make_async_copy(
            spectrum.at[pl.ds(row_from, N + 16), pl.ds(part * SPEC + col_from, N + 128)],
            window.at[part], sem.at[part])
        for part in range(2)
    ]
    for copy in copies:
        copy.start()
    mark[0] = jnp.full((8, 128), row, jnp.int32).astype(F32)
    mark[1] = jnp.full((8, 128), col, jnp.int32).astype(F32)
    down = row - row_from
    up = (24 - down % 8) % 24
    turn = (N + 128 - (col - col_from)) % (N + 128)
    for part in range(2):
        copies[part].wait()

        def turn_rows(i, carry):
            rows = pl.ds(pl.multiple_of(i * 16, 16), 16)
            aligned[part, rows, :] = pltpu.roll(window[part, rows, :].astype(F32), turn, 1)[:, :N]
            return carry

        lax.fori_loop(0, N // 16 + 1, turn_rows, 0, unroll=3)

        def move_rows(i, carry):
            rows = pl.ds(pl.multiple_of(i * 16, 16), 16)
            source = pl.ds(pl.multiple_of((i * 2 + down // 8) * 8, 8), 24)
            patch[rows, part * N:(part + 1) * N] = pltpu.roll(aligned[part, source, :], up, 0)[:16].astype(BF16)
            return carry

        lax.fori_loop(0, N // 16, move_rows, 0, unroll=4)


def kernel(mark, patch, pup, meas, tab, tabt, swap, out_spec, out_pup, *scratch):
    (half_s, field, inten, measp, xs, grads, folded, shift_rows, shift_cols, parts, parts_t, part, part_mark,
     peer, pupil_src, canvas_src) = scratch[:16]
    own = scratch[16:22]
    landed = scratch[22:28]
    (core_send, core_recv, send0, recv0, send, recv, gather_send, gather_recv) = scratch[28:]

    led = lax.axis_index("led")
    z = lax.axis_index("tile")
    core = led % 2
    x = (led // 2) % 4
    y = led // 8
    other = 1 - core

    def device(yy, xx, cc, zz):
        return ((yy * 4 + xx) * 2 + cc, zz)

    def low(p):
        return p + 1 - 2 * (p % 2)

    def high(p):
        return 3 - p

    neighbour = {
        ("y", 0): device(low(y), x, core, z), ("y", 1): device(high(y), x, core, z),
        ("x", 0): device(y, low(x), core, z), ("x", 1): device(y, high(x), core, z),
        ("z", 0): device(y, x, core, low(z)), ("z", 1): device(y, x, core, high(z)),
    }
    partner = device(y, x, other, z)
    mine = bits_of(y, x, z)
    column = [(c, d) for d in range(4) for c in range(2) if (c, d) != (0, 0)]

    barrier = pltpu.get_barrier_semaphore()
    greeted = [neighbour["y", 0], neighbour["y", 1], neighbour["x", 0], neighbour["x", 1]]
    greeted += [device(y, x, (core + c) % 2, (z + d) % 4) for c, d in column]
    for target in greeted:
        pl.semaphore_signal(barrier, inc=1, device_id=target, device_id_type=MESH)

    measp[:, :H] = meas[0, :, :H]
    measp[:, H:] = dot(meas[0, :, H:], swap[...]).astype(BF16)
    measp[H:, :] = dot(swap[...], measp[H:, :]).astype(BF16)
    inten[...] = jnp.zeros_like(inten)

    lane0 = lax.broadcasted_iota(jnp.int32, (1, 128), 1) == 0
    row0 = lax.broadcasted_iota(jnp.int32, (16, 1), 0) == 0

    def forward(m, carry):
        for c in range(2):
            cols = slice(c * H, (c + 1) * H)
            cols_i = slice(N + c * H, N + (c + 1) * H)
            pr = patch[:, cols].astype(F32)
            pi = patch[:, cols_i].astype(F32)
            qr = pup[m, :, cols].astype(F32)
            qi = pup[m, :, cols_i].astype(F32)
            er = (pr * qr - pi * qi).astype(BF16)
            ei = (pr * qi + pi * qr).astype(BF16)
            u = dot(tab[...], er)
            v = dot(tab[...], ei)
            half_s[0, :H, cols] = (u[:H] - v[H:]).astype(BF16)
            half_s[0, H:, cols] = (u[:H] + v[H:]).astype(BF16)
            half_s[1, :H, cols] = (v[:H] + u[H:]).astype(BF16)
            half_s[1, H:, cols] = (v[:H] - u[H:]).astype(BF16)
            ut, ub, vt, vb = u[:16], u[H:H + 16], v[:16], v[H:H + 16]
            half_s[0, :16, cols] = jnp.where(row0, ut, ut - vb).astype(BF16)
            half_s[0, H:H + 16, cols] = jnp.where(row0, ub, ut + vb).astype(BF16)
            half_s[1, :16, cols] = jnp.where(row0, vt, vt + ub).astype(BF16)
            half_s[1, H:H + 16, cols] = jnp.where(row0, vb, vt - ub).astype(BF16)
        for r in range(2):
            rows = slice(r * H, (r + 1) * H)
            u = dot(half_s[0, rows, :], tabt[...])
            v = dot(half_s[1, rows, :], tabt[...])
            for b in range(2):
                left = slice(b * 128, (b + 1) * 128)
                right = slice(H + b * 128, H + (b + 1) * 128)
                uc, us, vc, vs = u[:, left], u[:, right], v[:, left], v[:, right]
                rl, il, rr, ir = uc - vs, vc + us, uc + vs, vc - us
                if b == 0:
                    rl = jnp.where(lane0, uc, rl)
                    il = jnp.where(lane0, vc, il)
                    rr = jnp.where(lane0, us, rr)
                    ir = jnp.where(lane0, vs, ir)
                field[0, m, rows, left] = rl
                field[1, m, rows, left] = il
                field[0, m, rows, right] = rr
                field[1, m, rows, right] = ir
                inten[rows, left] += rl * rl + il * il
                inten[rows, right] += rr * rr + ir * ir
        return carry

    lax.fori_loop(0, MODES, forward, 0)

    def weigh(i, carry):
        rows = pl.ds(pl.multiple_of(i * 64, 64), 64)
        level = measp[rows, :].astype(F32)
        inten[rows, :] = 1.0 - level * lax.rsqrt(level * jnp.maximum(inten[rows, :], 0.1))
        return carry

    lax.fori_loop(0, N // 64, weigh, 0)

    def backward(m):
        def fold(i, carry):
            top = pl.ds(pl.multiple_of(i * 32, 32), 32)
            bottom = pl.ds(pl.multiple_of(H + i * 32, 32), 32)
            wt, wb = inten[top, :], inten[bottom, :]
            rt, rb = wt * field[0, m, top, :], wb * field[0, m, bottom, :]
            it, ib = wt * field[1, m, top, :], wb * field[1, m, bottom, :]
            xs[0, top, :] = (rt + rb).astype(BF16)
            xs[0, bottom, :] = (it - ib).astype(BF16)
            xs[1, top, :] = (it + ib).astype(BF16)
            xs[1, bottom, :] = (rb - rt).astype(BF16)
            return carry

        lax.fori_loop(0, H // 32, fold, 0)
        wt, wb = inten[:16, :], inten[H:H + 16, :]
        rt, rb = wt * field[0, m, :16, :], wb * field[0, m, H:H + 16, :]
        it, ib = wt * field[1, m, :16, :], wb * field[1, m, H:H + 16, :]
        xs[0, :16, :] = jnp.where(row0, rt, rt + rb).astype(BF16)
        xs[0, H:H + 16, :] = jnp.where(row0, rb, it - ib).astype(BF16)
        xs[1, :16, :] = jnp.where(row0, it, it + ib).astype(BF16)
        xs[1, H:H + 16, :] = jnp.where(row0, ib, rb - rt).astype(BF16)

        def rows_of(i, carry):
            rows = pl.ds(pl.multiple_of(i * H, H), H)
            fr = dot(tabt[rows, :], xs[0])
            fi = dot(tabt[rows, :], xs[1])
            for b in range(2):
                left = slice(b * 128, (b + 1) * 128)
                right = slice(H + b * 128, H + (b + 1) * 128)
                rl, rr, il, ir = fr[:, left], fr[:, right], fi[:, left], fi[:, right]
                pr, mi, p_i, mr = rl + rr, il - ir, il + ir, rr - rl
                if b == 0:
                    pr = jnp.where(lane0, rl, pr)
                    mi = jnp.where(lane0, rr, mi)
                    p_i = jnp.where(lane0, il, p_i)
                    mr = jnp.where(lane0, ir, mr)
                half_s[0, rows, left] = pr.astype(BF16)
                half_s[0, rows, right] = mi.astype(BF16)
                half_s[1, rows, left] = p_i.astype(BF16)
                half_s[1, rows, right] = mr.astype(BF16)
            gr = dot(half_s[0, rows, :], tab[...])
            gi = dot(half_s[1, rows, :], tab[...])
            qr, qi = pup[m, rows, :N].astype(F32), pup[m, rows, N:].astype(F32)
            sr = qr * gr + qi * gi
            si = qr * gi - qi * gr
            if m == 0:
                grads[0, rows, :] = sr
                grads[1, rows, :] = si
            else:
                grads[0, rows, :] += sr
                grads[1, rows, :] += si
            pr, pi = patch[rows, :N].astype(F32), patch[rows, N:].astype(F32)
            field[0, m, rows, :] = pr * gr + pi * gi
            field[1, m, rows, :] = pr * gi - pi * gr
            return carry

        lax.fori_loop(0, 2, rows_of, 0)

    def core_copy(m):
        return pltpu.make_async_remote_copy(
            src_ref=field.at[other, m], dst_ref=peer.at[m], send_sem=core_send.at[m],
            recv_sem=core_recv.at[m], device_id=partner, device_id_type=MESH)

    def starts(stream):
        begin, out = 0, []
        for step in range(6):
            bit = mine[DIMS[(stream + step) % 6]]
            length = 32 >> step
            out.append((begin + bit * length, begin + (1 - bit) * length, length, 64 - 2 * length))
            begin = begin + bit * length
        return out, begin

    ranges = [starts(stream) for stream in range(STREAMS)]

    def copy_tiles(stream, span, step, send_one, recv_one):
        units = pl.ds(span[0], span[1] - span[0])
        _, away, length, offset = ranges[stream][0][step]
        return pltpu.make_async_remote_copy(
            src_ref=own[stream].at[units, pl.ds(away, length)],
            dst_ref=landed[stream].at[units, pl.ds(offset, length)],
            send_sem=send_one, recv_sem=recv_one,
            device_id=neighbour[DIMS[(stream + step) % 6]], device_id_type=MESH)

    def first_hop(piece, stream):
        return copy_tiles(stream, PIECE_SPANS[piece, stream], 0, send0.at[piece, stream], recv0.at[piece, stream])

    def hop(phase, stream, step):
        return copy_tiles(stream, PHASE_SPANS[phase, stream], step,
                          send.at[phase, stream, step], recv.at[phase, stream, step])

    def launch(piece):
        for stream in range(STREAMS):
            if (piece, stream) in PIECE_SPANS:
                first_hop(piece, stream).start()

    def add_landed(stream, span, step):
        keep, _, length, offset = ranges[stream][0][step]
        for unit in range(*span):
            own[stream][unit, pl.ds(keep, length)] += landed[stream][unit, pl.ds(offset, length)]

    def advance(phase, step):
        for stream in range(STREAMS):
            if (phase, stream) not in PHASE_SPANS:
                continue
            if step == 0:
                for piece in PHASES[phase]:
                    if (piece, stream) in PIECE_SPANS:
                        first_hop(piece, stream).wait()
                        add_landed(stream, PIECE_SPANS[piece, stream], 0)
            else:
                hop(phase, stream, step).wait()
                add_landed(stream, PHASE_SPANS[phase, stream], step)
            if step < 5:
                hop(phase, stream, step + 1).start()

    def spread_pupil(m):
        core_copy(m).wait()

        def body(yx, carry):
            for zz in range(4):
                bits = bits_of(yx // 4, yx % 4, zz)
                cols = slice(zz * 128, (zz + 1) * 128)
                for g in range(4):
                    stream, unit = PLACE[m, g]
                    rows = pl.ds(pl.multiple_of(yx * 32 + g * 8, 8), 8)
                    own[stream][unit, slot_of(bits, stream)] = field[core, m, rows, cols] + peer[m, rows, cols]
            return carry

        lax.fori_loop(0, 16, body, 0)
        launch(m)

    backward(0)
    pl.semaphore_wait(barrier, len(greeted))
    core_copy(0).start()
    backward(1)
    core_copy(1).start()
    spread_pupil(0)
    backward(2)
    core_copy(2).start()
    spread_pupil(1)
    backward(3)
    core_copy(3).start()
    spread_pupil(2)

    along = lax.broadcasted_iota(jnp.int32, (N, 128), 1).astype(F32)
    down = lax.broadcasted_iota(jnp.int32, (N, 128), 0).astype(F32)

    def wrap(value):
        return jnp.where(value >= float(N), value - float(N), value)

    for b in range(8):
        at = slice(b * 128, (b + 1) * 128)
        to = wrap(wrap(along + float(b % 4 * 128)) + mark[0, :1, :])
        shift_rows[:, at] = (down == wrap(to)).astype(F32).astype(BF16)
    for b in range(4):
        at = slice(b * 128, (b + 1) * 128)
        to = wrap(wrap(down + mark[1, :1, :]))
        hit = (along + float(b * 128) == to).astype(F32).astype(BF16)
        shift_cols[:N, at] = hit
        shift_cols[N:, at] = hit
    def roll(part_no):
        whole = grads[part_no]
        coarse = whole.astype(BF16)
        parts[:N, :] = coarse
        parts[N:, :] = (whole - coarse.astype(F32)).astype(BF16)
        whole = dot(shift_rows[...], parts[...])
        coarse = whole.astype(BF16)
        parts_t[:, :N] = coarse
        parts_t[:, N:] = (whole - coarse.astype(F32)).astype(BF16)
        folded[part_no] = dot(parts_t[...], shift_cols[...])

    part_copy = pltpu.make_async_remote_copy(
        src_ref=folded.at[other], dst_ref=part, send_sem=core_send.at[4],
        recv_sem=core_recv.at[4], device_id=partner, device_id_type=MESH)
    mark_copy = pltpu.make_async_remote_copy(
        src_ref=mark, dst_ref=part_mark, send_sem=core_send.at[5],
        recv_sem=core_recv.at[5], device_id=partner, device_id_type=MESH)
    mark_copy.start()
    roll(other)
    part_copy.start()
    spread_pupil(3)
    roll(core)
    part_copy.wait()
    mark_copy.wait()

    iota_r = lax.broadcasted_iota(jnp.int32, (8, 128), 0).astype(F32)
    iota_c = lax.broadcasted_iota(jnp.int32, (8, 128), 1).astype(F32)

    def window(yx, carry):
        bit_sets = [bits_of(yx // 4, yx % 4, zz) for zz in range(4)]
        for zz in range(2):
            for g in range(2):
                base = 256 * zz + yx * 16 + g * 8
                rows = pl.ds(pl.multiple_of(base, 8), 8)
                row_no = iota_r + base.astype(F32)
                row_a = row_no < mark[0]
                row_b = row_no < part_mark[0]
                for block in range(4):
                    cols = slice(block * 128, (block + 1) * 128)
                    col_no = iota_c + float(block * 128)
                    col_a = col_no < mark[1]
                    col_b = col_no < part_mark[1]
                    value_a = folded[core, rows, cols]
                    value_b = part[rows, cols]
                    ra1 = jnp.where(row_a, value_a, 0.0)
                    ra0 = value_a - ra1
                    rb1 = jnp.where(row_b, value_b, 0.0)
                    rb0 = value_b - rb1
                    for upper, (va, vb) in enumerate(((ra0, rb0), (ra1, rb1))):
                        va1 = jnp.where(col_a, va, 0.0)
                        vb1 = jnp.where(col_b, vb, 0.0)
                        tiles = ((va - va1) + (vb - vb1), va1 + vb1)
                        bits = bit_sets[2 * upper + zz]
                        for later in range(2):
                            stream, unit = PLACE[CANVAS, g * 8 + later * 4 + block]
                            own[stream][unit, slot_of(bits, stream)] = tiles[later]
        return carry

    lax.fori_loop(0, 16, window, 0)
    launch(CANVAS)

    for phase, step in ((0, 0), (0, 1), (1, 0), (0, 2), (1, 1), (0, 3), (1, 2), (0, 4), (1, 3), (0, 5)):
        advance(phase, step)

    for m in range(MODES):
        for g in range(4):
            stream, unit = PLACE[m, g]
            pupil_src[m, g * 8:(g + 1) * 8, :] = own[stream][unit, ranges[stream][1]]
    block = pl.ds(pl.multiple_of((core * 4 + z) * 128, 128), 128)
    copies = []
    for number, (c, d) in enumerate(column):
        to_core = (core + c) % 2
        copies.append(pltpu.make_async_remote_copy(
            src_ref=pupil_src.at[:, pl.ds(pl.multiple_of(to_core * 16, 16), 16), :],
            dst_ref=out_pup.at[:, :, block],
            send_sem=gather_send.at[number], recv_sem=gather_recv.at[number],
            device_id=device(y, x, to_core, (z + d) % 4), device_id_type=MESH))
        copies[-1].start()
    out_pup[:, :, block] = pupil_src[:, pl.ds(pl.multiple_of(core * 16, 16), 16), :]

    for step in (4, 5):
        advance(1, step)

    for g in range(2):
        for b in range(8):
            stream, unit = PLACE[CANVAS, g * 8 + b]
            canvas_src[g, :, b * 128:(b + 1) * 128] = own[stream][unit, ranges[stream][1]]
    half_cols = pl.ds(pl.multiple_of(core * SPEC, SPEC), SPEC)
    last = pltpu.make_async_remote_copy(
        src_ref=canvas_src.at[other], dst_ref=out_spec.at[0, :, half_cols],
        send_sem=gather_send.at[7], recv_sem=gather_recv.at[7], device_id=partner, device_id_type=MESH)
    last.start()
    out_spec[0, :, half_cols] = canvas_src[core]
    for copy in copies:
        copy.wait()
    last.wait()


def local(spectrum, pupils, offsets, measured):
    vmem = pl.BlockSpec(memory_space=pltpu.VMEM)
    patch, mark = pl.pallas_call(
        extract,
        out_shape=(jax.ShapeDtypeStruct((N, 2 * N), BF16), jax.ShapeDtypeStruct((2, 8, 128), F32)),
        in_specs=[pl.BlockSpec(memory_space=pltpu.SMEM), pl.BlockSpec(memory_space=pl.ANY)],
        out_specs=(vmem, vmem),
        scratch_shapes=[
            pltpu.VMEM((2, N + 16, N + 128), BF16),
            pltpu.VMEM((2, N + 24, N), F32),
            pltpu.SemaphoreType.DMA((2,)),
        ],
        compiler_params=pltpu.CompilerParams(vmem_limit_bytes=16 * 2**20),
    )(offsets, spectrum)
    half, half_t, swap = (jnp.asarray(table) for table in tables())
    scratch = [
        pltpu.VMEM((2, N, N), BF16),
        pltpu.VMEM((2, MODES, N, N), F32),
        pltpu.VMEM((N, N), F32),
        pltpu.VMEM((N, N), BF16),
        pltpu.VMEM((2, N, N), BF16),
        pltpu.VMEM((2, N, N), F32),
        pltpu.VMEM((2, N, N), F32),
        pltpu.VMEM((N, 2 * N), BF16),
        pltpu.VMEM((2 * N, N), BF16),
        pltpu.VMEM((2 * N, N), BF16),
        pltpu.VMEM((N, 2 * N), BF16),
        pltpu.VMEM((N, N), F32),
        pltpu.VMEM((2, 8, 128), F32),
        pltpu.VMEM((MODES, N, N), F32),
        pltpu.VMEM((MODES, 32, 128), F32),
        pltpu.VMEM((2, 8, SPEC), F32),
    ]
    scratch += [pltpu.VMEM((count, 64, 8, 128), F32) for count in COUNTS]
    scratch += [pltpu.VMEM((count, 63, 8, 128), F32) for count in COUNTS]
    scratch += [pltpu.SemaphoreType.DMA((6,)), pltpu.SemaphoreType.DMA((6,))]
    scratch += [pltpu.SemaphoreType.DMA((len(PIECES), STREAMS)), pltpu.SemaphoreType.DMA((len(PIECES), STREAMS))]
    scratch += [pltpu.SemaphoreType.DMA((len(PHASES), STREAMS, 6)), pltpu.SemaphoreType.DMA((len(PHASES), STREAMS, 6))]
    scratch += [pltpu.SemaphoreType.DMA((8,)), pltpu.SemaphoreType.DMA((8,))]
    return tuple(pl.pallas_call(
        kernel,
        out_shape=(
            jax.ShapeDtypeStruct((1, 8, 2 * SPEC), F32),
            jax.ShapeDtypeStruct((MODES, 16, 2 * N), F32),
        ),
        in_specs=[vmem] * 7,
        out_specs=(vmem, vmem),
        scratch_shapes=scratch,
        compiler_params=pltpu.CompilerParams(
            collective_id=0, has_side_effects=True, vmem_limit_bytes=60 * 2**20),
    )(mark, patch, pupils, measured, half, half_t, swap))


def solution(mesh):
    return jax.shard_map(
        local,
        mesh=mesh,
        in_specs=(P(), P(), P(("led", "tile"), None), P(("led", "tile"), None, None)),
        out_specs=(P("tile", "led", None), P(None, "led", None)),
        check_vma=False,
    )
```

```python
import math

import jax
import jax.numpy as jnp
import numpy as np
from jax import lax
from jax.experimental import pallas as pl
from jax.experimental.pallas import tpu as pltpu
from jax.sharding import PartitionSpec as P

MESH = pl.DeviceIdType.MESH
N = 512
H = 256
MODES = 4
SPEC = 1024
F32 = jnp.float32
BF16 = jnp.bfloat16

ORDERS = (("y", 0, "x", "z"), ("x", 0, "z", "y"), ("z", 0, "y", "x"),
          ("y", 1, "z", "x"), ("x", 1, "y", "z"), ("z", 1, "x", "y"))
LEVELS = 4

STREAMS = 6
PIECES = (
    (0, 1, 2, 3),
    (4, 5, 0, 1),
    (2, 3, 4, 5),
    (0, 1, 2, 3),
    (0, 1, 2, 3, 4, 4, 5, 5, 0, 1, 2, 2, 3, 3, 4, 5),
)
CANVAS = 4
PHASES = ((0, 1), (2, 3), (4,))
BEFORE = ((0, 1), (1, 0), (2, 0), (0, 2), (1, 1), (2, 1), (0, 3), (1, 2), (2, 2), (1, 3))
AFTER = ((2, 3),)


def plan():
    counts = [0] * STREAMS
    place, pieces, phases = {}, {}, {}
    for number, streams in enumerate(PIECES):
        first = list(counts)
        for unit, stream in enumerate(streams):
            place[number, unit] = (stream, counts[stream])
            counts[stream] += 1
        for stream in range(STREAMS):
            if counts[stream] > first[stream]:
                pieces[number, stream] = (first[stream], counts[stream])
    for number, members in enumerate(PHASES):
        for stream in range(STREAMS):
            spans = [pieces[member, stream] for member in members if (member, stream) in pieces]
            if spans:
                phases[number, stream] = (spans[0][0], spans[-1][1])
    return counts, place, pieces, phases


COUNTS, PLACE, PIECE_SPANS, PHASE_SPANS = plan()


def tables():
    positions = np.arange(N, dtype=np.int64)
    angles = (positions[:, None] * positions[None, :] % N).astype(np.float32) * np.float32(2.0 * math.pi / N)
    factor = np.float32(1.0 / math.sqrt(N))
    cosine = (np.cos(angles) * factor).astype(BF16)
    sine = (np.sin(angles) * factor).astype(BF16)
    half = np.concatenate([cosine[:H], sine[:H]], axis=0)
    half[H] = cosine[H]
    swap = np.zeros((H, H), np.float32)
    swap[(H - np.arange(H)) % H, np.arange(H)] = 1.0
    return half, np.ascontiguousarray(half.T), swap.astype(BF16)


def low_bit(position):
    return ((position + 1) // 2) % 2


def high_bit(position):
    return position // 2


def slot_of(at, stream):
    axis, bit, second, third = ORDERS[stream]
    bits = low_bit(at[axis]), high_bit(at[axis])
    return ((bits[bit] * 2 + bits[1 - bit]) * 4 + at[second]) * 4 + at[third]


def dot(a, b):
    return jnp.dot(a, b, preferred_element_type=F32)


def extract(offs, spectrum, patch, mark, window, aligned, sem):
    row, col = offs[0, 0], offs[0, 1]
    row_from = pl.multiple_of(jnp.minimum(row // 16 * 16, N - 16), 16)
    col_from = pl.multiple_of(jnp.minimum(col // 128 * 128, N - 128), 128)
    copies = [
        pltpu.make_async_copy(
            spectrum.at[pl.ds(row_from, N + 16), pl.ds(part * SPEC + col_from, N + 128)],
            window.at[part], sem.at[part])
        for part in range(2)
    ]
    for copy in copies:
        copy.start()
    mark[0] = jnp.full((8, 128), row, jnp.int32).astype(F32)
    mark[1] = jnp.full((8, 128), col, jnp.int32).astype(F32)
    down = row - row_from
    up = (24 - down % 8) % 24
    turn = (N + 128 - (col - col_from)) % (N + 128)
    for part in range(2):
        copies[part].wait()

        def turn_rows(i, carry):
            rows = pl.ds(pl.multiple_of(i * 16, 16), 16)
            aligned[part, rows, :] = pltpu.roll(window[part, rows, :].astype(F32), turn, 1)[:, :N]
            return carry

        lax.fori_loop(0, N // 16 + 1, turn_rows, 0, unroll=3)

        def move_rows(i, carry):
            rows = pl.ds(pl.multiple_of(i * 16, 16), 16)
            source = pl.ds(pl.multiple_of((i * 2 + down // 8) * 8, 8), 24)
            patch[rows, part * N:(part + 1) * N] = pltpu.roll(aligned[part, source, :], up, 0)[:16].astype(BF16)
            return carry

        lax.fori_loop(0, N // 16, move_rows, 0, unroll=4)


def kernel(mark, patch, pupils, meas, tab, tabt, swap, out_spec, out_pup, *scratch):
    (half_s, field, inten, measp, xs, grads, folded, shift_rows, shift_cols, parts, parts_t, peer_grad, part_mark,
     peer, pupil_src, canvas_src, pup) = scratch[:17]
    own = scratch[17:23]
    landed = scratch[23:29]
    (core_send, core_recv, send0, recv0, send, recv, gather_send, gather_recv, load) = scratch[29:]

    def pupil_load(m):
        return pltpu.make_async_copy(pupils.at[m], pup.at[m], load.at[m])

    for m in range(MODES):
        pupil_load(m).start()


    led = lax.axis_index("led")
    z = lax.axis_index("tile")
    core = led % 2
    x = (led // 2) % 4
    y = led // 8
    other = 1 - core

    def device(yy, xx, cc, zz):
        return ((yy * 4 + xx) * 2 + cc, zz)

    def low(p):
        return p + 1 - 2 * (p % 2)

    def high(p):
        return 3 - p

    here = {"y": y, "x": x, "z": z}

    def moved(axis, position):
        there = dict(here, **{axis: position})
        return device(there["y"], there["x"], core, there["z"])

    partner = device(y, x, other, z)
    column = [(c, d) for d in range(4) for c in range(2) if (c, d) != (0, 0)]

    barrier = pltpu.get_barrier_semaphore()
    greeted = [moved(axis, (here[axis] + k) % 4) for axis in ("y", "x") for k in range(1, 4)]
    greeted += [device(y, x, (core + c) % 2, (z + d) % 4) for c, d in column]
    for target in greeted:
        pl.semaphore_signal(barrier, inc=1, device_id=target, device_id_type=MESH)

    measp[:, :H] = meas[0, :, :H]
    measp[:, H:] = dot(meas[0, :, H:], swap[...]).astype(BF16)
    measp[H:, :] = dot(swap[...], measp[H:, :]).astype(BF16)
    inten[...] = jnp.zeros_like(inten)

    lane0 = lax.broadcasted_iota(jnp.int32, (1, 128), 1) == 0
    row0 = lax.broadcasted_iota(jnp.int32, (16, 1), 0) == 0

    def forward(m, carry):
        pupil_load(m).wait()
        for c in range(2):
            cols = slice(c * H, (c + 1) * H)
            cols_i = slice(N + c * H, N + (c + 1) * H)
            pr = patch[:, cols].astype(F32)
            pi = patch[:, cols_i].astype(F32)
            qr = pup[m, :, cols].astype(F32)
            qi = pup[m, :, cols_i].astype(F32)
            er = (pr * qr - pi * qi).astype(BF16)
            ei = (pr * qi + pi * qr).astype(BF16)
            u = dot(tab[...], er)
            v = dot(tab[...], ei)
            half_s[0, :H, cols] = (u[:H] - v[H:]).astype(BF16)
            half_s[0, H:, cols] = (u[:H] + v[H:]).astype(BF16)
            half_s[1, :H, cols] = (v[:H] + u[H:]).astype(BF16)
            half_s[1, H:, cols] = (v[:H] - u[H:]).astype(BF16)
            ut, ub, vt, vb = u[:16], u[H:H + 16], v[:16], v[H:H + 16]
            half_s[0, :16, cols] = jnp.where(row0, ut, ut - vb).astype(BF16)
            half_s[0, H:H + 16, cols] = jnp.where(row0, ub, ut + vb).astype(BF16)
            half_s[1, :16, cols] = jnp.where(row0, vt, vt + ub).astype(BF16)
            half_s[1, H:H + 16, cols] = jnp.where(row0, vb, vt - ub).astype(BF16)
        for r in range(2):
            rows = slice(r * H, (r + 1) * H)
            u = dot(half_s[0, rows, :], tabt[...])
            v = dot(half_s[1, rows, :], tabt[...])
            for b in range(2):
                left = slice(b * 128, (b + 1) * 128)
                right = slice(H + b * 128, H + (b + 1) * 128)
                uc, us, vc, vs = u[:, left], u[:, right], v[:, left], v[:, right]
                rl, il, rr, ir = uc - vs, vc + us, uc + vs, vc - us
                if b == 0:
                    rl = jnp.where(lane0, uc, rl)
                    il = jnp.where(lane0, vc, il)
                    rr = jnp.where(lane0, us, rr)
                    ir = jnp.where(lane0, vs, ir)
                field[0, m, rows, left] = rl
                field[1, m, rows, left] = il
                field[0, m, rows, right] = rr
                field[1, m, rows, right] = ir
                inten[rows, left] += rl * rl + il * il
                inten[rows, right] += rr * rr + ir * ir
        return carry

    lax.fori_loop(0, MODES, forward, 0)

    def weigh(i, carry):
        rows = pl.ds(pl.multiple_of(i * 64, 64), 64)
        level = measp[rows, :].astype(F32)
        inten[rows, :] = 1.0 - level * lax.rsqrt(level * jnp.maximum(inten[rows, :], 0.1))
        return carry

    lax.fori_loop(0, N // 64, weigh, 0)

    def weigh_fold(m):
        def fold(i, carry):
            top = pl.ds(pl.multiple_of(i * 32, 32), 32)
            bottom = pl.ds(pl.multiple_of(H + i * 32, 32), 32)
            wt, wb = inten[top, :], inten[bottom, :]
            rt, rb = wt * field[0, m, top, :], wb * field[0, m, bottom, :]
            it, ib = wt * field[1, m, top, :], wb * field[1, m, bottom, :]
            xs[0, top, :] = (rt + rb).astype(BF16)
            xs[0, bottom, :] = (it - ib).astype(BF16)
            xs[1, top, :] = (it + ib).astype(BF16)
            xs[1, bottom, :] = (rb - rt).astype(BF16)
            return carry

        lax.fori_loop(0, H // 32, fold, 0)
        wt, wb = inten[:16, :], inten[H:H + 16, :]
        rt, rb = wt * field[0, m, :16, :], wb * field[0, m, H:H + 16, :]
        it, ib = wt * field[1, m, :16, :], wb * field[1, m, H:H + 16, :]
        xs[0, :16, :] = jnp.where(row0, rt, rt + rb).astype(BF16)
        xs[0, H:H + 16, :] = jnp.where(row0, rb, it - ib).astype(BF16)
        xs[1, :16, :] = jnp.where(row0, it, it + ib).astype(BF16)
        xs[1, H:H + 16, :] = jnp.where(row0, ib, rb - rt).astype(BF16)

    def transform(m, i):
        rows = slice(i * H, (i + 1) * H)
        fr = dot(tabt[rows, :], xs[0])
        fi = dot(tabt[rows, :], xs[1])
        for b in range(2):
            left = slice(b * 128, (b + 1) * 128)
            right = slice(H + b * 128, H + (b + 1) * 128)
            rl, rr, il, ir = fr[:, left], fr[:, right], fi[:, left], fi[:, right]
            pr, mi, p_i, mr = rl + rr, il - ir, il + ir, rr - rl
            if b == 0:
                pr = jnp.where(lane0, rl, pr)
                mi = jnp.where(lane0, rr, mi)
                p_i = jnp.where(lane0, il, p_i)
                mr = jnp.where(lane0, ir, mr)
            half_s[0, rows, left] = pr.astype(BF16)
            half_s[0, rows, right] = mi.astype(BF16)
            half_s[1, rows, left] = p_i.astype(BF16)
            half_s[1, rows, right] = mr.astype(BF16)
        gr = dot(half_s[0, rows, :], tab[...])
        gi = dot(half_s[1, rows, :], tab[...])
        qr, qi = pup[m, rows, :N].astype(F32), pup[m, rows, N:].astype(F32)
        sr = qr * gr + qi * gi
        si = qr * gi - qi * gr
        if m == 0:
            grads[0, rows, :] = sr
            grads[1, rows, :] = si
        else:
            grads[0, rows, :] += sr
            grads[1, rows, :] += si
        pr, pi = patch[rows, :N].astype(F32), patch[rows, N:].astype(F32)
        field[0, m, rows, :] = pr * gr + pi * gi
        field[1, m, rows, :] = pr * gi - pi * gr

    def core_copy(m, i):
        rows = pl.ds(i * H, H)
        return pltpu.make_async_remote_copy(
            src_ref=field.at[other, m, rows], dst_ref=peer.at[m, rows], send_sem=core_send.at[2 * m + i],
            recv_sem=core_recv.at[2 * m + i], device_id=partner, device_id_type=MESH)

    def copy_tiles(stream, span, away, length, offset, sems, target):
        units = pl.ds(span[0], span[1] - span[0])
        return pltpu.make_async_remote_copy(
            src_ref=own[stream].at[units, pl.ds(away, length)],
            dst_ref=landed[stream].at[units, pl.ds(offset, length)],
            send_sem=sems[0], recv_sem=sems[1], device_id=target, device_id_type=MESH)

    def halves(stream):
        axis, bit, second, third = ORDERS[stream]
        bits = low_bit(here[axis]), high_bit(here[axis])
        one = bits[bit] * 32
        return axis, bit, bits, one, one + bits[1 - bit] * 16

    def first_hop(piece, stream):
        axis, bit, bits, _, _ = halves(stream)
        return copy_tiles(stream, PIECE_SPANS[piece, stream], (1 - bits[bit]) * 32, 32, 0,
                          (send0.at[piece, stream], recv0.at[piece, stream]),
                          moved(axis, (low, high)[bit](here[axis])))

    def hops(phase, stream, step):
        span = PHASE_SPANS[phase, stream]
        axis, bit, bits, one, two = halves(stream)

        def sems(number):
            return send.at[phase, stream, number], recv.at[phase, stream, number]

        if step == 1:
            return [copy_tiles(stream, span, one + (1 - bits[1 - bit]) * 16, 16, 32, sems(0),
                               moved(axis, (low, high)[1 - bit](here[axis])))]
        ring = ORDERS[stream][step]
        out = []
        for k in (2, 1, 3):
            to = (here[ring] + k) % 4
            if step == 2:
                away, length, offset = two + to * 4, 4, 48 + 4 * (k - 1)
            else:
                away, length, offset = two + here[ORDERS[stream][2]] * 4 + to, 1, 60 + (k - 1)
            out.append(copy_tiles(stream, span, away, length, offset, sems(3 * step - 6 + k), moved(ring, to)))
        return out

    def final_slot(stream):
        return slot_of(here, stream)

    def launch(piece):
        for stream in range(STREAMS):
            if (piece, stream) in PIECE_SPANS:
                first_hop(piece, stream).start()

    def add_landed(stream, span, step):
        _, _, _, one, two = halves(stream)
        second, third = (here[axis] for axis in ORDERS[stream][2:])
        keep, length, offset, count = (
            (one, 32, 0, 1), (two, 16, 32, 1), (two + second * 4, 4, 48, 3),
            (two + second * 4 + third, 1, 60, 3))[step]
        for unit in range(*span):
            total = own[stream][unit, pl.ds(keep, length)]
            for k in range(count):
                total += landed[stream][unit, pl.ds(offset + k * length, length)]
            own[stream][unit, pl.ds(keep, length)] = total

    def advance(phase, step):
        for stream in range(STREAMS):
            if (phase, stream) not in PHASE_SPANS:
                continue
            if step == 0:
                for piece in PHASES[phase]:
                    if (piece, stream) in PIECE_SPANS:
                        first_hop(piece, stream).wait()
                        add_landed(stream, PIECE_SPANS[piece, stream], 0)
            else:
                for copy in hops(phase, stream, step):
                    copy.wait()
                add_landed(stream, PHASE_SPANS[phase, stream], step)
            if step < LEVELS - 1:
                for copy in hops(phase, stream, step + 1):
                    copy.start()

    def spread_pupil(m):
        core_copy(m, 0).wait()
        core_copy(m, 1).wait()

        def body(yx, carry):
            for zz in range(4):
                at = {"y": yx // 4, "x": yx % 4, "z": zz}
                cols = slice(zz * 128, (zz + 1) * 128)
                for g in range(4):
                    stream, unit = PLACE[m, g]
                    rows = pl.ds(pl.multiple_of(yx * 32 + g * 8, 8), 8)
                    own[stream][unit, slot_of(at, stream)] = field[core, m, rows, cols] + peer[m, rows, cols]
            return carry

        lax.fori_loop(0, 16, body, 0)
        launch(m)

    def grad_copy(i):
        rows = pl.ds(i * H, H)
        return pltpu.make_async_remote_copy(
            src_ref=grads.at[other, rows], dst_ref=peer_grad.at[rows],
            send_sem=(core_send.at[8], core_send.at[10])[i], recv_sem=(core_recv.at[8], core_recv.at[10])[i],
            device_id=partner, device_id_type=MESH)

    mark_copy = pltpu.make_async_remote_copy(
        src_ref=mark, dst_ref=part_mark, send_sem=core_send.at[9],
        recv_sem=core_recv.at[9], device_id=partner, device_id_type=MESH)

    def backward(m, between=()):
        weigh_fold(m)
        for i in range(2):
            transform(m, i)
            if m == 0 and i == 0:
                pl.semaphore_wait(barrier, len(greeted))
            if m == MODES - 1:
                grad_copy(i).start()
            core_copy(m, i).start()
            if i == 0:
                for task, *values in between:
                    task(*values)

    along = lax.broadcasted_iota(jnp.int32, (N, 128), 1).astype(F32)
    down = lax.broadcasted_iota(jnp.int32, (N, 128), 0).astype(F32)

    def wrap(value):
        return jnp.where(value >= float(N), value - float(N), value)

    def one_hots(shifts):
        for b in range(4):
            at = slice(b * 128, (b + 1) * 128)
            to = wrap(along[:1] + float(b * 128) + shifts[0, :1, :])
            hit = (down == wrap(to)).astype(F32).astype(BF16)
            shift_rows[:, at] = hit
            shift_rows[:, N + b * 128:N + (b + 1) * 128] = hit
            to = wrap(down + shifts[1, :1, :])
            hit = (along + float(b * 128) == wrap(to)).astype(F32).astype(BF16)
            shift_cols[:N, at] = hit
            shift_cols[N:, at] = hit

    def roll(whole, shifts, number):
        one_hots(shifts)
        coarse = whole.astype(BF16)
        parts[:N, :] = coarse
        parts[N:, :] = (whole - coarse.astype(F32)).astype(BF16)
        whole = dot(shift_rows[...], parts[...])
        coarse = whole.astype(BF16)
        parts_t[:, :N] = coarse
        parts_t[:, N:] = (whole - coarse.astype(F32)).astype(BF16)
        folded[number] = dot(parts_t[...], shift_cols[...])

    backward(0)
    mark_copy.start()
    backward(1, ((spread_pupil, 0),))
    backward(2, ((spread_pupil, 1),))
    backward(3, ((spread_pupil, 2),))
    mark_copy.wait()
    roll(grads[core], mark, 0)
    advance(0, 0)
    grad_copy(0).wait()
    grad_copy(1).wait()
    roll(peer_grad[...], part_mark, 1)
    spread_pupil(3)

    iota_r = lax.broadcasted_iota(jnp.int32, (8, 128), 0).astype(F32)
    iota_c = lax.broadcasted_iota(jnp.int32, (8, 128), 1).astype(F32)

    def window(yx, carry):
        for zz in range(2):
            for g in range(2):
                base = 256 * zz + yx * 16 + g * 8
                rows = pl.ds(pl.multiple_of(base, 8), 8)
                row_no = iota_r + base.astype(F32)
                row_a = row_no < mark[0]
                row_b = row_no < part_mark[0]
                for block in range(4):
                    cols = slice(block * 128, (block + 1) * 128)
                    col_no = iota_c + float(block * 128)
                    col_a = col_no < mark[1]
                    col_b = col_no < part_mark[1]
                    value_a = folded[0, rows, cols]
                    value_b = folded[1, rows, cols]
                    ra1 = jnp.where(row_a, value_a, 0.0)
                    ra0 = value_a - ra1
                    rb1 = jnp.where(row_b, value_b, 0.0)
                    rb0 = value_b - rb1
                    for upper, (va, vb) in enumerate(((ra0, rb0), (ra1, rb1))):
                        va1 = jnp.where(col_a, va, 0.0)
                        vb1 = jnp.where(col_b, vb, 0.0)
                        tiles = ((va - va1) + (vb - vb1), va1 + vb1)
                        at = {"y": yx // 4, "x": yx % 4, "z": 2 * upper + zz}
                        for later in range(2):
                            stream, unit = PLACE[CANVAS, g * 8 + later * 4 + block]
                            own[stream][unit, slot_of(at, stream)] = tiles[later]
        return carry

    lax.fori_loop(0, 16, window, 0)
    launch(CANVAS)

    for phase, step in BEFORE:
        advance(phase, step)

    for m in range(MODES):
        for g in range(4):
            stream, unit = PLACE[m, g]
            pupil_src[m, g * 8:(g + 1) * 8, :] = own[stream][unit, final_slot(stream)]
    block = pl.ds(pl.multiple_of((core * 4 + z) * 128, 128), 128)
    copies = []
    for number, (c, d) in enumerate(column):
        to_core = (core + c) % 2
        copies.append(pltpu.make_async_remote_copy(
            src_ref=pupil_src.at[:, pl.ds(pl.multiple_of(to_core * 16, 16), 16), :],
            dst_ref=out_pup.at[:, :, block],
            send_sem=gather_send.at[number], recv_sem=gather_recv.at[number],
            device_id=device(y, x, to_core, (z + d) % 4), device_id_type=MESH))
        copies[-1].start()
    out_pup[:, :, block] = pupil_src[:, pl.ds(pl.multiple_of(core * 16, 16), 16), :]

    for phase, step in AFTER:
        advance(phase, step)

    for g in range(2):
        for b in range(8):
            stream, unit = PLACE[CANVAS, g * 8 + b]
            canvas_src[g, :, b * 128:(b + 1) * 128] = own[stream][unit, final_slot(stream)]
    half_cols = pl.ds(pl.multiple_of(core * SPEC, SPEC), SPEC)
    last = pltpu.make_async_remote_copy(
        src_ref=canvas_src.at[other], dst_ref=out_spec.at[0, :, half_cols],
        send_sem=gather_send.at[7], recv_sem=gather_recv.at[7], device_id=partner, device_id_type=MESH)
    last.start()
    out_spec[0, :, half_cols] = canvas_src[core]
    for copy in copies:
        copy.wait()
    last.wait()


def local(spectrum, pupils, offsets, measured):
    vmem = pl.BlockSpec(memory_space=pltpu.VMEM)
    patch, mark = pl.pallas_call(
        extract,
        out_shape=(jax.ShapeDtypeStruct((N, 2 * N), BF16), jax.ShapeDtypeStruct((2, 8, 128), F32)),
        in_specs=[pl.BlockSpec(memory_space=pltpu.SMEM), pl.BlockSpec(memory_space=pl.ANY)],
        out_specs=(vmem, vmem),
        scratch_shapes=[
            pltpu.VMEM((2, N + 16, N + 128), BF16),
            pltpu.VMEM((2, N + 24, N), F32),
            pltpu.SemaphoreType.DMA((2,)),
        ],
        compiler_params=pltpu.CompilerParams(vmem_limit_bytes=60 * 2**20),
    )(offsets, spectrum)
    half, half_t, swap = (jnp.asarray(table) for table in tables())
    scratch = [
        pltpu.VMEM((2, N, N), BF16),
        pltpu.VMEM((2, MODES, N, N), F32),
        pltpu.VMEM((N, N), F32),
        pltpu.VMEM((N, N), BF16),
        pltpu.VMEM((2, N, N), BF16),
        pltpu.VMEM((2, N, N), F32),
        pltpu.VMEM((2, N, N), F32),
        pltpu.VMEM((N, 2 * N), BF16),
        pltpu.VMEM((2 * N, N), BF16),
        pltpu.VMEM((2 * N, N), BF16),
        pltpu.VMEM((N, 2 * N), BF16),
        pltpu.VMEM((N, N), F32),
        pltpu.VMEM((2, 8, 128), F32),
        pltpu.VMEM((MODES, N, N), F32),
        pltpu.VMEM((MODES, 32, 128), F32),
        pltpu.VMEM((2, 8, SPEC), F32),
        pltpu.VMEM((MODES, N, 2 * N), BF16),
    ]
    scratch += [pltpu.VMEM((count, 64, 8, 128), F32) for count in COUNTS]
    scratch += [pltpu.VMEM((count, 63, 8, 128), F32) for count in COUNTS]
    scratch += [pltpu.SemaphoreType.DMA((11,)), pltpu.SemaphoreType.DMA((11,))]
    scratch += [pltpu.SemaphoreType.DMA((len(PIECES), STREAMS)), pltpu.SemaphoreType.DMA((len(PIECES), STREAMS))]
    scratch += [pltpu.SemaphoreType.DMA((len(PHASES), STREAMS, 7)), pltpu.SemaphoreType.DMA((len(PHASES), STREAMS, 7))]
    scratch += [pltpu.SemaphoreType.DMA((8,)), pltpu.SemaphoreType.DMA((8,)), pltpu.SemaphoreType.DMA((MODES,))]
    return tuple(pl.pallas_call(
        kernel,
        out_shape=(
            jax.ShapeDtypeStruct((1, 8, 2 * SPEC), F32),
            jax.ShapeDtypeStruct((MODES, 16, 2 * N), F32),
        ),
        in_specs=[vmem] * 2 + [pl.BlockSpec(memory_space=pl.ANY)] + [vmem] * 4,
        out_specs=(vmem, vmem),
        scratch_shapes=scratch,
        compiler_params=pltpu.CompilerParams(
            collective_id=0, has_side_effects=True, vmem_limit_bytes=60 * 2**20),
    )(mark, patch, pupils, measured, half, half_t, swap))


def solution(mesh):
    return jax.shard_map(
        local,
        mesh=mesh,
        in_specs=(P(), P(), P(("led", "tile"), None), P(("led", "tile"), None, None)),
        out_specs=(P("tile", "led", None), P(None, "led", None)),
        check_vma=False,
    )
```

```python
import math

import jax
import jax.numpy as jnp
import numpy as np
from jax import lax
from jax.experimental import pallas as pl
from jax.experimental.pallas import tpu as pltpu
from jax.sharding import PartitionSpec as P

MESH = pl.DeviceIdType.MESH
N = 512
H = 256
MODES = 4
SPEC = 1024
F32 = jnp.float32
BF16 = jnp.bfloat16

ORDERS = (("y", 0, "x", "z"), ("x", 0, "z", "y"), ("z", 0, "y", "x"),
          ("y", 1, "z", "x"), ("x", 1, "y", "z"), ("z", 1, "x", "y"))
LEVELS = 4

STREAMS = 6
PIECES = (
    (0, 1, 2, 3),
    (4, 5, 0, 1),
    (2, 3, 4, 5),
    (0, 1, 2, 3),
    (0, 1, 2, 3, 4, 4, 5, 5, 0, 1, 2, 2, 3, 3, 4, 5),
)
CANVAS = 4
PHASES = ((0, 1), (2, 3), (4,))
BEFORE = ((0, 1), (1, 0), (2, 0), (0, 2), (1, 1), (2, 1), (0, 3), (1, 2), (2, 2), (1, 3))
AFTER = ((2, 3),)


def plan():
    counts = [0] * STREAMS
    place, pieces, phases = {}, {}, {}
    for number, streams in enumerate(PIECES):
        first = list(counts)
        for unit, stream in enumerate(streams):
            place[number, unit] = (stream, counts[stream])
            counts[stream] += 1
        for stream in range(STREAMS):
            if counts[stream] > first[stream]:
                pieces[number, stream] = (first[stream], counts[stream])
    for number, members in enumerate(PHASES):
        for stream in range(STREAMS):
            spans = [pieces[member, stream] for member in members if (member, stream) in pieces]
            if spans:
                phases[number, stream] = (spans[0][0], spans[-1][1])
    return counts, place, pieces, phases


COUNTS, PLACE, PIECE_SPANS, PHASE_SPANS = plan()


def tables():
    positions = np.arange(N, dtype=np.int64)
    angles = (positions[:, None] * positions[None, :] % N).astype(np.float32) * np.float32(2.0 * math.pi / N)
    factor = np.float32(1.0 / math.sqrt(N))
    cosine = (np.cos(angles) * factor).astype(BF16)
    sine = (np.sin(angles) * factor).astype(BF16)
    half = np.concatenate([cosine[:H], sine[:H]], axis=0)
    half[H] = cosine[H]
    swap = np.zeros((H, H), np.float32)
    swap[(H - np.arange(H)) % H, np.arange(H)] = 1.0
    return half, np.ascontiguousarray(half.T), swap.astype(BF16)


def low_bit(position):
    return ((position + 1) // 2) % 2


def high_bit(position):
    return position // 2


def slot_of(at, stream):
    axis, bit, second, third = ORDERS[stream]
    bits = low_bit(at[axis]), high_bit(at[axis])
    return ((bits[bit] * 2 + bits[1 - bit]) * 4 + at[second]) * 4 + at[third]


def dot(a, b):
    return jnp.dot(a, b, preferred_element_type=F32)


def kernel(offs, spectrum, pupils, measured, table, table_t, swap_in, out_spec, out_pup, *scratch):
    (half_s, field, inten, measp, folds, grads, folded, shift_rows, shift_cols, parts, parts_t, peer_grad, part_mark,
     peer, pupil_src, canvas_src, pup, mark, patch, whole, meas, tab, tabt, swap, pick_row, pick_col) = scratch[:26]
    own = scratch[26:32]
    landed = scratch[32:38]
    (core_send, core_recv, send0, recv0, send, recv, gather_send, gather_recv, load) = scratch[38:]

    def pupil_load(m):
        return pltpu.make_async_copy(pupils.at[m], pup.at[m], load.at[m])

    loads = [
        pltpu.make_async_copy(source, target, load.at[MODES + number])
        for number, (source, target) in enumerate((
            (spectrum.at[:, :SPEC], whole.at[:, :SPEC]), (table, tab), (table_t, tabt), (measured, meas), (swap_in, swap),
            (spectrum.at[:, SPEC:], whole.at[:, SPEC:])))
    ]
    loads[0].start()
    loads[5].start()
    loads[1].start()
    pupil_load(0).start()
    for copy in loads[2:5]:
        copy.start()
    for m in range(1, MODES):
        pupil_load(m).start()


    led = lax.axis_index("led")
    z = lax.axis_index("tile")
    core = led % 2
    x = (led // 2) % 4
    y = led // 8
    other = 1 - core

    def device(yy, xx, cc, zz):
        return ((yy * 4 + xx) * 2 + cc, zz)

    def low(p):
        return p + 1 - 2 * (p % 2)

    def high(p):
        return 3 - p

    here = {"y": y, "x": x, "z": z}

    def moved(axis, position):
        there = dict(here, **{axis: position})
        return device(there["y"], there["x"], core, there["z"])

    partner = device(y, x, other, z)
    column = [(c, d) for d in range(4) for c in range(2) if (c, d) != (0, 0)]

    barrier = pltpu.get_barrier_semaphore()
    greeted = [moved(axis, (here[axis] + k) % 4) for axis in ("y", "x") for k in range(1, 4)]
    greeted += [device(y, x, (core + c) % 2, (z + d) % 4) for c, d in column]
    for target in greeted:
        pl.semaphore_signal(barrier, inc=1, device_id=target, device_id_type=MESH)

    mark[0] = jnp.broadcast_to(offs[:, 0:1], (8, 128)).astype(F32)
    mark[1] = jnp.broadcast_to(offs[:, 1:2], (8, 128)).astype(F32)
    rise = lax.broadcasted_iota(jnp.int32, (N, 128), 1) - lax.broadcasted_iota(jnp.int32, (N, 128), 0)
    fall = lax.broadcasted_iota(jnp.int32, (SPEC, 128), 0) - lax.broadcasted_iota(jnp.int32, (SPEC, 128), 1)
    for b in range(8):
        pick_row[:, b * 128:(b + 1) * 128] = (
            rise.astype(F32) == mark[0, :1, :] - float(b * 128)).astype(F32).astype(BF16)
    for b in range(4):
        pick_col[:, b * 128:(b + 1) * 128] = (
            fall.astype(F32) == mark[1, :1, :] + float(b * 128)).astype(F32).astype(BF16)
    for number in range(2):
        loads[5 * number].wait()
        window = dot(pick_row[...], whole[:, number * SPEC:(number + 1) * SPEC]).astype(BF16)
        patch[:, number * N:(number + 1) * N] = dot(window, pick_col[...]).astype(BF16)

    inten[...] = jnp.zeros_like(inten)
    for copy in loads[1:3]:
        copy.wait()

    lane0 = lax.broadcasted_iota(jnp.int32, (1, 128), 1) == 0
    row0 = lax.broadcasted_iota(jnp.int32, (16, 1), 0) == 0

    def forward(m, carry):
        pupil_load(m).wait()
        for c in range(2):
            cols = slice(c * H, (c + 1) * H)
            cols_i = slice(N + c * H, N + (c + 1) * H)
            pr = patch[:, cols].astype(F32)
            pi = patch[:, cols_i].astype(F32)
            qr = pup[m, :, cols].astype(F32)
            qi = pup[m, :, cols_i].astype(F32)
            er = (pr * qr - pi * qi).astype(BF16)
            ei = (pr * qi + pi * qr).astype(BF16)
            u = dot(tab[...], er)
            v = dot(tab[...], ei)
            half_s[0, :H, cols] = (u[:H] - v[H:]).astype(BF16)
            half_s[0, H:, cols] = (u[:H] + v[H:]).astype(BF16)
            half_s[1, :H, cols] = (v[:H] + u[H:]).astype(BF16)
            half_s[1, H:, cols] = (v[:H] - u[H:]).astype(BF16)
            ut, ub, vt, vb = u[:16], u[H:H + 16], v[:16], v[H:H + 16]
            half_s[0, :16, cols] = jnp.where(row0, ut, ut - vb).astype(BF16)
            half_s[0, H:H + 16, cols] = jnp.where(row0, ub, ut + vb).astype(BF16)
            half_s[1, :16, cols] = jnp.where(row0, vt, vt + ub).astype(BF16)
            half_s[1, H:H + 16, cols] = jnp.where(row0, vb, vt - ub).astype(BF16)
        for r in range(2):
            rows = slice(r * H, (r + 1) * H)
            u = dot(half_s[0, rows, :], tabt[...])
            v = dot(half_s[1, rows, :], tabt[...])
            for b in range(2):
                left = slice(b * 128, (b + 1) * 128)
                right = slice(H + b * 128, H + (b + 1) * 128)
                uc, us, vc, vs = u[:, left], u[:, right], v[:, left], v[:, right]
                rl, il, rr, ir = uc - vs, vc + us, uc + vs, vc - us
                if b == 0:
                    rl = jnp.where(lane0, uc, rl)
                    il = jnp.where(lane0, vc, il)
                    rr = jnp.where(lane0, us, rr)
                    ir = jnp.where(lane0, vs, ir)
                field[0, m, rows, left] = rl
                field[1, m, rows, left] = il
                field[0, m, rows, right] = rr
                field[1, m, rows, right] = ir
                inten[rows, left] += rl * rl + il * il
                inten[rows, right] += rr * rr + ir * ir
        return carry

    lax.fori_loop(0, MODES, forward, 0)

    for copy in loads[3:5]:
        copy.wait()
    measp[:, :H] = meas[0, :, :H]
    measp[:, H:] = dot(meas[0, :, H:], swap[...]).astype(BF16)
    measp[H:, :] = dot(swap[...], measp[H:, :]).astype(BF16)

    def weigh(i, carry):
        rows = pl.ds(pl.multiple_of(i * 64, 64), 64)
        level = measp[rows, :].astype(F32)
        inten[rows, :] = 1.0 - level * lax.rsqrt(level * jnp.maximum(inten[rows, :], 0.1))
        return carry

    lax.fori_loop(0, N // 64, weigh, 0)

    def weigh_fold(m):
        xs = folds.at[m % 2]
        for i in range(H // 32):
            top = slice(i * 32, i * 32 + 32)
            bottom = slice(H + i * 32, H + i * 32 + 32)
            wt, wb = inten[top, :], inten[bottom, :]
            rt, rb = wt * field[0, m, top, :], wb * field[0, m, bottom, :]
            it, ib = wt * field[1, m, top, :], wb * field[1, m, bottom, :]
            xs[0, top, :] = (rt + rb).astype(BF16)
            xs[0, bottom, :] = (it - ib).astype(BF16)
            xs[1, top, :] = (it + ib).astype(BF16)
            xs[1, bottom, :] = (rb - rt).astype(BF16)
        wt, wb = inten[:16, :], inten[H:H + 16, :]
        rt, rb = wt * field[0, m, :16, :], wb * field[0, m, H:H + 16, :]
        it, ib = wt * field[1, m, :16, :], wb * field[1, m, H:H + 16, :]
        xs[0, :16, :] = jnp.where(row0, rt, rt + rb).astype(BF16)
        xs[0, H:H + 16, :] = jnp.where(row0, rb, it - ib).astype(BF16)
        xs[1, :16, :] = jnp.where(row0, it, it + ib).astype(BF16)
        xs[1, H:H + 16, :] = jnp.where(row0, ib, rb - rt).astype(BF16)

    def transform(m, i):
        xs = folds.at[m % 2]
        rows = slice(i * H, (i + 1) * H)
        fr = dot(tabt[rows, :], xs[0])
        fi = dot(tabt[rows, :], xs[1])
        for b in range(2):
            left = slice(b * 128, (b + 1) * 128)
            right = slice(H + b * 128, H + (b + 1) * 128)
            rl, rr, il, ir = fr[:, left], fr[:, right], fi[:, left], fi[:, right]
            pr, mi, p_i, mr = rl + rr, il - ir, il + ir, rr - rl
            if b == 0:
                pr = jnp.where(lane0, rl, pr)
                mi = jnp.where(lane0, rr, mi)
                p_i = jnp.where(lane0, il, p_i)
                mr = jnp.where(lane0, ir, mr)
            half_s[0, rows, left] = pr.astype(BF16)
            half_s[0, rows, right] = mi.astype(BF16)
            half_s[1, rows, left] = p_i.astype(BF16)
            half_s[1, rows, right] = mr.astype(BF16)
        gr = dot(half_s[0, rows, :], tab[...])
        gi = dot(half_s[1, rows, :], tab[...])
        qr, qi = pup[m, rows, :N].astype(F32), pup[m, rows, N:].astype(F32)
        sr = qr * gr + qi * gi
        si = qr * gi - qi * gr
        if m == 0:
            grads[0, rows, :] = sr
            grads[1, rows, :] = si
        else:
            grads[0, rows, :] += sr
            grads[1, rows, :] += si
        pr, pi = patch[rows, :N].astype(F32), patch[rows, N:].astype(F32)
        field[0, m, rows, :] = pr * gr + pi * gi
        field[1, m, rows, :] = pr * gi - pi * gr

    def core_copy(m, i):
        rows = pl.ds(i * H, H)
        return pltpu.make_async_remote_copy(
            src_ref=field.at[other, m, rows], dst_ref=peer.at[m, rows], send_sem=core_send.at[2 * m + i],
            recv_sem=core_recv.at[2 * m + i], device_id=partner, device_id_type=MESH)

    def copy_tiles(stream, span, away, length, offset, sems, target):
        units = pl.ds(span[0], span[1] - span[0])
        return pltpu.make_async_remote_copy(
            src_ref=own[stream].at[units, pl.ds(away, length)],
            dst_ref=landed[stream].at[units, pl.ds(offset, length)],
            send_sem=sems[0], recv_sem=sems[1], device_id=target, device_id_type=MESH)

    def halves(stream):
        axis, bit, second, third = ORDERS[stream]
        bits = low_bit(here[axis]), high_bit(here[axis])
        one = bits[bit] * 32
        return axis, bit, bits, one, one + bits[1 - bit] * 16

    def first_hop(piece, stream):
        axis, bit, bits, _, _ = halves(stream)
        return copy_tiles(stream, PIECE_SPANS[piece, stream], (1 - bits[bit]) * 32, 32, 0,
                          (send0.at[piece, stream], recv0.at[piece, stream]),
                          moved(axis, (low, high)[bit](here[axis])))

    def hops(phase, stream, step):
        span = PHASE_SPANS[phase, stream]
        axis, bit, bits, one, two = halves(stream)

        def sems(number):
            return send.at[phase, stream, number], recv.at[phase, stream, number]

        if step == 1:
            return [copy_tiles(stream, span, one + (1 - bits[1 - bit]) * 16, 16, 32, sems(0),
                               moved(axis, (low, high)[1 - bit](here[axis])))]
        ring = ORDERS[stream][step]
        out = []
        for k in (2, 1, 3):
            to = (here[ring] + k) % 4
            if step == 2:
                away, length, offset = two + to * 4, 4, 48 + 4 * (k - 1)
            else:
                away, length, offset = two + here[ORDERS[stream][2]] * 4 + to, 1, 60 + (k - 1)
            out.append(copy_tiles(stream, span, away, length, offset, sems(3 * step - 6 + k), moved(ring, to)))
        return out

    def final_slot(stream):
        return slot_of(here, stream)

    def launch(piece):
        for stream in range(STREAMS):
            if (piece, stream) in PIECE_SPANS:
                first_hop(piece, stream).start()

    def add_landed(stream, span, step):
        _, _, _, one, two = halves(stream)
        second, third = (here[axis] for axis in ORDERS[stream][2:])
        keep, length, offset, count = (
            (one, 32, 0, 1), (two, 16, 32, 1), (two + second * 4, 4, 48, 3),
            (two + second * 4 + third, 1, 60, 3))[step]
        for unit in range(*span):
            total = own[stream][unit, pl.ds(keep, length)]
            for k in range(count):
                total += landed[stream][unit, pl.ds(offset + k * length, length)]
            own[stream][unit, pl.ds(keep, length)] = total

    def advance(phase, step):
        for stream in range(STREAMS):
            if (phase, stream) not in PHASE_SPANS:
                continue
            if step == 0:
                for piece in PHASES[phase]:
                    if (piece, stream) in PIECE_SPANS:
                        first_hop(piece, stream).wait()
                        add_landed(stream, PIECE_SPANS[piece, stream], 0)
            else:
                for copy in hops(phase, stream, step):
                    copy.wait()
                add_landed(stream, PHASE_SPANS[phase, stream], step)
            if step < LEVELS - 1:
                for copy in hops(phase, stream, step + 1):
                    copy.start()

    def spread_pupil(m):
        core_copy(m, 0).wait()
        core_copy(m, 1).wait()

        def body(yx, carry):
            for zz in range(4):
                at = {"y": yx // 4, "x": yx % 4, "z": zz}
                cols = slice(zz * 128, (zz + 1) * 128)
                for g in range(4):
                    stream, unit = PLACE[m, g]
                    rows = pl.ds(pl.multiple_of(yx * 32 + g * 8, 8), 8)
                    own[stream][unit, slot_of(at, stream)] = field[core, m, rows, cols] + peer[m, rows, cols]
            return carry

        lax.fori_loop(0, 16, body, 0)
        launch(m)

    def grad_copy(i):
        rows = pl.ds(i * H, H)
        return pltpu.make_async_remote_copy(
            src_ref=grads.at[other, rows], dst_ref=peer_grad.at[rows],
            send_sem=(core_send.at[8], core_send.at[10])[i], recv_sem=(core_recv.at[8], core_recv.at[10])[i],
            device_id=partner, device_id_type=MESH)

    mark_copy = pltpu.make_async_remote_copy(
        src_ref=mark, dst_ref=part_mark, send_sem=core_send.at[9],
        recv_sem=core_recv.at[9], device_id=partner, device_id_type=MESH)

    def backward(m, between=()):
        weigh_fold(m)
        for i in range(2):
            transform(m, i)
            if m == 0 and i == 0:
                pl.semaphore_wait(barrier, len(greeted))
            if m == MODES - 1:
                grad_copy(i).start()
            core_copy(m, i).start()
            if i == 0:
                for task, *values in between:
                    task(*values)

    along = lax.broadcasted_iota(jnp.int32, (N, 128), 1).astype(F32)
    down = lax.broadcasted_iota(jnp.int32, (N, 128), 0).astype(F32)

    def wrap(value):
        return jnp.where(value >= float(N), value - float(N), value)

    def one_hots(shifts):
        for b in range(4):
            at = slice(b * 128, (b + 1) * 128)
            to = wrap(along[:1] + float(b * 128) + shifts[0, :1, :])
            hit = (down == wrap(to)).astype(F32).astype(BF16)
            shift_rows[:, at] = hit
            shift_rows[:, N + b * 128:N + (b + 1) * 128] = hit
            to = wrap(down + shifts[1, :1, :])
            hit = (along + float(b * 128) == wrap(to)).astype(F32).astype(BF16)
            shift_cols[:N, at] = hit
            shift_cols[N:, at] = hit

    def roll(whole, shifts, number):
        one_hots(shifts)
        coarse = whole.astype(BF16)
        parts[:N, :] = coarse
        parts[N:, :] = (whole - coarse.astype(F32)).astype(BF16)
        whole = dot(shift_rows[...], parts[...])
        coarse = whole.astype(BF16)
        parts_t[:, :N] = coarse
        parts_t[:, N:] = (whole - coarse.astype(F32)).astype(BF16)
        folded[number] = dot(parts_t[...], shift_cols[...])

    backward(0)
    mark_copy.start()
    backward(1, ((spread_pupil, 0),))
    backward(2, ((spread_pupil, 1),))
    backward(3, ((spread_pupil, 2),))
    mark_copy.wait()
    roll(grads[core], mark, 0)
    advance(0, 0)
    grad_copy(0).wait()
    grad_copy(1).wait()
    roll(peer_grad[...], part_mark, 1)
    spread_pupil(3)

    iota_r = lax.broadcasted_iota(jnp.int32, (8, 128), 0).astype(F32)
    iota_c = lax.broadcasted_iota(jnp.int32, (8, 128), 1).astype(F32)

    def window(yx, carry):
        for zz in range(2):
            for g in range(2):
                base = 256 * zz + yx * 16 + g * 8
                rows = pl.ds(pl.multiple_of(base, 8), 8)
                row_no = iota_r + base.astype(F32)
                row_a = row_no < mark[0]
                row_b = row_no < part_mark[0]
                for block in range(4):
                    cols = slice(block * 128, (block + 1) * 128)
                    col_no = iota_c + float(block * 128)
                    col_a = col_no < mark[1]
                    col_b = col_no < part_mark[1]
                    value_a = folded[0, rows, cols]
                    value_b = folded[1, rows, cols]
                    ra1 = jnp.where(row_a, value_a, 0.0)
                    ra0 = value_a - ra1
                    rb1 = jnp.where(row_b, value_b, 0.0)
                    rb0 = value_b - rb1
                    for upper, (va, vb) in enumerate(((ra0, rb0), (ra1, rb1))):
                        va1 = jnp.where(col_a, va, 0.0)
                        vb1 = jnp.where(col_b, vb, 0.0)
                        tiles = ((va - va1) + (vb - vb1), va1 + vb1)
                        at = {"y": yx // 4, "x": yx % 4, "z": 2 * upper + zz}
                        for later in range(2):
                            stream, unit = PLACE[CANVAS, g * 8 + later * 4 + block]
                            own[stream][unit, slot_of(at, stream)] = tiles[later]
        return carry

    lax.fori_loop(0, 16, window, 0)
    launch(CANVAS)

    for phase, step in BEFORE:
        advance(phase, step)

    for m in range(MODES):
        for g in range(4):
            stream, unit = PLACE[m, g]
            pupil_src[m, g * 8:(g + 1) * 8, :] = own[stream][unit, final_slot(stream)]
    block = pl.ds(pl.multiple_of((core * 4 + z) * 128, 128), 128)
    copies = []
    for number, (c, d) in enumerate(column):
        to_core = (core + c) % 2
        copies.append(pltpu.make_async_remote_copy(
            src_ref=pupil_src.at[:, pl.ds(pl.multiple_of(to_core * 16, 16), 16), :],
            dst_ref=out_pup.at[:, :, block],
            send_sem=gather_send.at[number], recv_sem=gather_recv.at[number],
            device_id=device(y, x, to_core, (z + d) % 4), device_id_type=MESH))
        copies[-1].start()
    out_pup[:, :, block] = pupil_src[:, pl.ds(pl.multiple_of(core * 16, 16), 16), :]

    for phase, step in AFTER:
        advance(phase, step)

    for g in range(2):
        for b in range(8):
            stream, unit = PLACE[CANVAS, g * 8 + b]
            canvas_src[g, :, b * 128:(b + 1) * 128] = own[stream][unit, final_slot(stream)]
    half_cols = pl.ds(pl.multiple_of(core * SPEC, SPEC), SPEC)
    last = pltpu.make_async_remote_copy(
        src_ref=canvas_src.at[other], dst_ref=out_spec.at[0, :, half_cols],
        send_sem=gather_send.at[7], recv_sem=gather_recv.at[7], device_id=partner, device_id_type=MESH)
    last.start()
    out_spec[0, :, half_cols] = canvas_src[core]
    for copy in copies:
        copy.wait()
    last.wait()


def local(spectrum, pupils, offsets, measured):
    vmem = pl.BlockSpec(memory_space=pltpu.VMEM)
    half, half_t, swap = (jnp.asarray(table) for table in tables())
    scratch = [
        pltpu.VMEM((2, N, N), BF16),
        pltpu.VMEM((2, MODES, N, N), F32),
        pltpu.VMEM((N, N), F32),
        pltpu.VMEM((N, N), BF16),
        pltpu.VMEM((2, 2, N, N), BF16),
        pltpu.VMEM((2, N, N), F32),
        pltpu.VMEM((2, N, N), F32),
        pltpu.VMEM((N, 2 * N), BF16),
        pltpu.VMEM((2 * N, N), BF16),
        pltpu.VMEM((2 * N, N), BF16),
        pltpu.VMEM((N, 2 * N), BF16),
        pltpu.VMEM((N, N), F32),
        pltpu.VMEM((2, 8, 128), F32),
        pltpu.VMEM((MODES, N, N), F32),
        pltpu.VMEM((MODES, 32, 128), F32),
        pltpu.VMEM((2, 8, SPEC), F32),
        pltpu.VMEM((MODES, N, 2 * N), BF16),
        pltpu.VMEM((2, 8, 128), F32),
        pltpu.VMEM((N, 2 * N), BF16),
        pltpu.VMEM((SPEC, 2 * SPEC), BF16),
        pltpu.VMEM((1, N, N), BF16),
        pltpu.VMEM((N, N), BF16),
        pltpu.VMEM((N, N), BF16),
        pltpu.VMEM((H, H), BF16),
        pltpu.VMEM((N, SPEC), BF16),
        pltpu.VMEM((SPEC, N), BF16),
    ]
    scratch += [pltpu.VMEM((count, 64, 8, 128), F32) for count in COUNTS]
    scratch += [pltpu.VMEM((count, 63, 8, 128), F32) for count in COUNTS]
    scratch += [pltpu.SemaphoreType.DMA((11,)), pltpu.SemaphoreType.DMA((11,))]
    scratch += [pltpu.SemaphoreType.DMA((len(PIECES), STREAMS)), pltpu.SemaphoreType.DMA((len(PIECES), STREAMS))]
    scratch += [pltpu.SemaphoreType.DMA((len(PHASES), STREAMS, 7)), pltpu.SemaphoreType.DMA((len(PHASES), STREAMS, 7))]
    scratch += [pltpu.SemaphoreType.DMA((8,)), pltpu.SemaphoreType.DMA((8,)), pltpu.SemaphoreType.DMA((MODES + 6,))]
    return tuple(pl.pallas_call(
        kernel,
        out_shape=(
            jax.ShapeDtypeStruct((1, 8, 2 * SPEC), F32),
            jax.ShapeDtypeStruct((MODES, 16, 2 * N), F32),
        ),
        in_specs=[vmem] + [pl.BlockSpec(memory_space=pl.ANY)] * 6,
        out_specs=(vmem, vmem),
        scratch_shapes=scratch,
        compiler_params=pltpu.CompilerParams(
            collective_id=0, has_side_effects=True, vmem_limit_bytes=60 * 2**20),
    )(offsets, spectrum, pupils, measured, half, half_t, swap))


def solution(mesh):
    return jax.shard_map(
        local,
        mesh=mesh,
        in_specs=(P(), P(), P(("led", "tile"), None), P(("led", "tile"), None, None)),
        out_specs=(P("tile", "led", None), P(None, "led", None)),
        check_vma=False,
    )
```

```python
import math

import jax
import jax.numpy as jnp
import numpy as np
from jax import lax
from jax.experimental import pallas as pl
from jax.experimental.pallas import tpu as pltpu
from jax.sharding import PartitionSpec as P

MESH = pl.DeviceIdType.MESH
N = 512
H = 256
MODES = 4
SPEC = 1024
F32 = jnp.float32
BF16 = jnp.bfloat16

ORDERS = (("y", 0, "x", "z"), ("x", 0, "z", "y"), ("z", 0, "y", "x"),
          ("y", 1, "z", "x"), ("x", 1, "y", "z"), ("z", 1, "x", "y"))
LEVELS = 4

STREAMS = 6
PIECES = (
    (3, 4, 4, 5),
    (0, 1, 2, 5),
    (0, 2, 3, 5),
    (3, 4, 4, 5),
    (0, 0, 0, 1, 1, 1, 2, 2, 2, 3, 3, 4, 4, 5, 5, 5),
)
CANVAS = 4
PHASES = ((0, 1), (2, 3), (4,))
BEFORE = ((0, 1), (1, 0), (2, 0), (0, 2), (1, 1), (2, 1), (0, 3), (1, 2), (2, 2), (1, 3))
AFTER = ((2, 3),)


def plan():
    counts = [0] * STREAMS
    place, pieces, phases = {}, {}, {}
    for number, streams in enumerate(PIECES):
        first = list(counts)
        for unit, stream in enumerate(streams):
            place[number, unit] = (stream, counts[stream])
            counts[stream] += 1
        for stream in range(STREAMS):
            if counts[stream] > first[stream]:
                pieces[number, stream] = (first[stream], counts[stream])
    for number, members in enumerate(PHASES):
        for stream in range(STREAMS):
            spans = [pieces[member, stream] for member in members if (member, stream) in pieces]
            if spans:
                phases[number, stream] = (spans[0][0], spans[-1][1])
    return counts, place, pieces, phases


COUNTS, PLACE, PIECE_SPANS, PHASE_SPANS = plan()


def tables():
    positions = np.arange(N, dtype=np.int64)
    angles = (positions[:, None] * positions[None, :] % N).astype(np.float32) * np.float32(2.0 * math.pi / N)
    factor = np.float32(1.0 / math.sqrt(N))
    cosine = (np.cos(angles) * factor).astype(BF16)
    sine = (np.sin(angles) * factor).astype(BF16)
    half = np.concatenate([cosine[:H], sine[:H]], axis=0)
    half[H] = cosine[H]
    swap = np.zeros((H, H), np.float32)
    swap[(H - np.arange(H)) % H, np.arange(H)] = 1.0
    return half, np.ascontiguousarray(half.T), swap.astype(BF16)


def low_bit(position):
    return ((position + 1) // 2) % 2


def high_bit(position):
    return position // 2


def slot_of(at, stream):
    axis, bit, second, third = ORDERS[stream]
    bits = low_bit(at[axis]), high_bit(at[axis])
    return ((bits[bit] * 2 + bits[1 - bit]) * 4 + at[second]) * 4 + at[third]


def dot(a, b):
    return jnp.dot(a, b, preferred_element_type=F32)


def kernel(offs, spectrum, pupils, measured, table, table_t, swap_in, out_spec, out_pup, *scratch):
    (half_s, field, inten, measp, folds, grads, folded, shift_rows, shift_cols, parts, parts_t, peer_grad, part_mark,
     peer, pupil_src, canvas_src, pup, mark, patch, whole, meas, tab, tabt, swap, pick_row, pick_col) = scratch[:26]
    own = scratch[26:32]
    landed = scratch[32:38]
    (core_send, core_recv, send0, recv0, send, recv, gather_send, gather_recv, load) = scratch[38:]

    def pupil_load(m):
        return pltpu.make_async_copy(pupils.at[m], pup.at[m], load.at[m])

    loads = [
        pltpu.make_async_copy(source, target, load.at[MODES + number])
        for number, (source, target) in enumerate((
            (spectrum.at[:, :SPEC], whole.at[:, :SPEC]), (table, tab), (table_t, tabt), (measured, meas), (swap_in, swap),
            (spectrum.at[:, SPEC:], whole.at[:, SPEC:])))
    ]
    loads[0].start()
    loads[5].start()
    loads[1].start()
    pupil_load(0).start()
    for copy in loads[2:5]:
        copy.start()
    for m in range(1, MODES):
        pupil_load(m).start()


    led = lax.axis_index("led")
    z = lax.axis_index("tile")
    core = led % 2
    x = (led // 2) % 4
    y = led // 8
    other = 1 - core

    def device(yy, xx, cc, zz):
        return ((yy * 4 + xx) * 2 + cc, zz)

    def low(p):
        return p + 1 - 2 * (p % 2)

    def high(p):
        return 3 - p

    here = {"y": y, "x": x, "z": z}

    def moved(axis, position):
        there = dict(here, **{axis: position})
        return device(there["y"], there["x"], core, there["z"])

    partner = device(y, x, other, z)
    column = [(c, d) for d in range(4) for c in range(2) if (c, d) != (0, 0)]

    barrier = pltpu.get_barrier_semaphore()
    greeted = [moved(axis, (here[axis] + k) % 4) for axis in ("y", "x") for k in range(1, 4)]
    greeted += [device(y, x, (core + c) % 2, (z + d) % 4) for c, d in column]
    for target in greeted:
        pl.semaphore_signal(barrier, inc=1, device_id=target, device_id_type=MESH)

    mark[0] = jnp.broadcast_to(offs[:, 0:1], (8, 128)).astype(F32)
    mark[1] = jnp.broadcast_to(offs[:, 1:2], (8, 128)).astype(F32)
    rise = lax.broadcasted_iota(jnp.int32, (N, 128), 1) - lax.broadcasted_iota(jnp.int32, (N, 128), 0)
    fall = lax.broadcasted_iota(jnp.int32, (SPEC, 128), 0) - lax.broadcasted_iota(jnp.int32, (SPEC, 128), 1)
    for b in range(8):
        pick_row[:, b * 128:(b + 1) * 128] = (
            rise.astype(F32) == mark[0, :1, :] - float(b * 128)).astype(F32).astype(BF16)
    for b in range(4):
        pick_col[:, b * 128:(b + 1) * 128] = (
            fall.astype(F32) == mark[1, :1, :] + float(b * 128)).astype(F32).astype(BF16)
    for number in range(2):
        loads[5 * number].wait()
        window = dot(pick_row[...], whole[:, number * SPEC:(number + 1) * SPEC]).astype(BF16)
        patch[:, number * N:(number + 1) * N] = dot(window, pick_col[...]).astype(BF16)

    inten[...] = jnp.zeros_like(inten)
    for copy in loads[1:3]:
        copy.wait()

    lane0 = lax.broadcasted_iota(jnp.int32, (1, 128), 1) == 0
    row0 = lax.broadcasted_iota(jnp.int32, (16, 1), 0) == 0

    def forward(m, carry):
        pupil_load(m).wait()
        for c in range(2):
            cols = slice(c * H, (c + 1) * H)
            cols_i = slice(N + c * H, N + (c + 1) * H)
            pr = patch[:, cols].astype(F32)
            pi = patch[:, cols_i].astype(F32)
            qr = pup[m, :, cols].astype(F32)
            qi = pup[m, :, cols_i].astype(F32)
            er = (pr * qr - pi * qi).astype(BF16)
            ei = (pr * qi + pi * qr).astype(BF16)
            u = dot(tab[...], er)
            v = dot(tab[...], ei)
            half_s[0, :H, cols] = (u[:H] - v[H:]).astype(BF16)
            half_s[0, H:, cols] = (u[:H] + v[H:]).astype(BF16)
            half_s[1, :H, cols] = (v[:H] + u[H:]).astype(BF16)
            half_s[1, H:, cols] = (v[:H] - u[H:]).astype(BF16)
            ut, ub, vt, vb = u[:16], u[H:H + 16], v[:16], v[H:H + 16]
            half_s[0, :16, cols] = jnp.where(row0, ut, ut - vb).astype(BF16)
            half_s[0, H:H + 16, cols] = jnp.where(row0, ub, ut + vb).astype(BF16)
            half_s[1, :16, cols] = jnp.where(row0, vt, vt + ub).astype(BF16)
            half_s[1, H:H + 16, cols] = jnp.where(row0, vb, vt - ub).astype(BF16)
        for r in range(2):
            rows = slice(r * H, (r + 1) * H)
            u = dot(half_s[0, rows, :], tabt[...])
            v = dot(half_s[1, rows, :], tabt[...])
            for b in range(2):
                left = slice(b * 128, (b + 1) * 128)
                right = slice(H + b * 128, H + (b + 1) * 128)
                uc, us, vc, vs = u[:, left], u[:, right], v[:, left], v[:, right]
                rl, il, rr, ir = uc - vs, vc + us, uc + vs, vc - us
                if b == 0:
                    rl = jnp.where(lane0, uc, rl)
                    il = jnp.where(lane0, vc, il)
                    rr = jnp.where(lane0, us, rr)
                    ir = jnp.where(lane0, vs, ir)
                field[0, m, rows, left] = rl
                field[1, m, rows, left] = il
                field[0, m, rows, right] = rr
                field[1, m, rows, right] = ir
                inten[rows, left] += rl * rl + il * il
                inten[rows, right] += rr * rr + ir * ir
        return carry

    lax.fori_loop(0, MODES, forward, 0)

    for copy in loads[3:5]:
        copy.wait()
    measp[:, :H] = meas[0, :, :H]
    measp[:, H:] = dot(meas[0, :, H:], swap[...]).astype(BF16)
    measp[H:, :] = dot(swap[...], measp[H:, :]).astype(BF16)

    def weigh(i, carry):
        rows = pl.ds(pl.multiple_of(i * 64, 64), 64)
        level = measp[rows, :].astype(F32)
        inten[rows, :] = 1.0 - level * lax.rsqrt(level * jnp.maximum(inten[rows, :], 0.1))
        return carry

    lax.fori_loop(0, N // 64, weigh, 0)

    def weigh_fold(m):
        xs = folds.at[m % 2]
        for i in range(H // 32):
            top = slice(i * 32, i * 32 + 32)
            bottom = slice(H + i * 32, H + i * 32 + 32)
            wt, wb = inten[top, :], inten[bottom, :]
            rt, rb = wt * field[0, m, top, :], wb * field[0, m, bottom, :]
            it, ib = wt * field[1, m, top, :], wb * field[1, m, bottom, :]
            xs[0, top, :] = (rt + rb).astype(BF16)
            xs[0, bottom, :] = (it - ib).astype(BF16)
            xs[1, top, :] = (it + ib).astype(BF16)
            xs[1, bottom, :] = (rb - rt).astype(BF16)
        wt, wb = inten[:16, :], inten[H:H + 16, :]
        rt, rb = wt * field[0, m, :16, :], wb * field[0, m, H:H + 16, :]
        it, ib = wt * field[1, m, :16, :], wb * field[1, m, H:H + 16, :]
        xs[0, :16, :] = jnp.where(row0, rt, rt + rb).astype(BF16)
        xs[0, H:H + 16, :] = jnp.where(row0, rb, it - ib).astype(BF16)
        xs[1, :16, :] = jnp.where(row0, it, it + ib).astype(BF16)
        xs[1, H:H + 16, :] = jnp.where(row0, ib, rb - rt).astype(BF16)

    def transform(m, i):
        xs = folds.at[m % 2]
        rows = slice(i * H, (i + 1) * H)
        fr = dot(tabt[rows, :], xs[0])
        fi = dot(tabt[rows, :], xs[1])
        for b in range(2):
            left = slice(b * 128, (b + 1) * 128)
            right = slice(H + b * 128, H + (b + 1) * 128)
            rl, rr, il, ir = fr[:, left], fr[:, right], fi[:, left], fi[:, right]
            pr, mi, p_i, mr = rl + rr, il - ir, il + ir, rr - rl
            if b == 0:
                pr = jnp.where(lane0, rl, pr)
                mi = jnp.where(lane0, rr, mi)
                p_i = jnp.where(lane0, il, p_i)
                mr = jnp.where(lane0, ir, mr)
            half_s[0, rows, left] = pr.astype(BF16)
            half_s[0, rows, right] = mi.astype(BF16)
            half_s[1, rows, left] = p_i.astype(BF16)
            half_s[1, rows, right] = mr.astype(BF16)
        gr = dot(half_s[0, rows, :], tab[...])
        gi = dot(half_s[1, rows, :], tab[...])
        qr, qi = pup[m, rows, :N].astype(F32), pup[m, rows, N:].astype(F32)
        sr = qr * gr + qi * gi
        si = qr * gi - qi * gr
        if m == 0:
            grads[0, rows, :] = sr
            grads[1, rows, :] = si
        else:
            grads[0, rows, :] += sr
            grads[1, rows, :] += si
        pr, pi = patch[rows, :N].astype(F32), patch[rows, N:].astype(F32)
        field[0, m, rows, :] = pr * gr + pi * gi
        field[1, m, rows, :] = pr * gi - pi * gr

    def core_copy(m, i):
        rows = pl.ds(i * H, H)
        return pltpu.make_async_remote_copy(
            src_ref=field.at[other, m, rows], dst_ref=peer.at[m, rows], send_sem=core_send.at[2 * m + i],
            recv_sem=core_recv.at[2 * m + i], device_id=partner, device_id_type=MESH)

    def copy_tiles(stream, span, away, length, offset, sems, target):
        units = pl.ds(span[0], span[1] - span[0])
        return pltpu.make_async_remote_copy(
            src_ref=own[stream].at[units, pl.ds(away, length)],
            dst_ref=landed[stream].at[units, pl.ds(offset, length)],
            send_sem=sems[0], recv_sem=sems[1], device_id=target, device_id_type=MESH)

    def halves(stream):
        axis, bit, second, third = ORDERS[stream]
        bits = low_bit(here[axis]), high_bit(here[axis])
        one = bits[bit] * 32
        return axis, bit, bits, one, one + bits[1 - bit] * 16

    def first_hop(piece, stream):
        axis, bit, bits, _, _ = halves(stream)
        return copy_tiles(stream, PIECE_SPANS[piece, stream], (1 - bits[bit]) * 32, 32, 0,
                          (send0.at[piece, stream], recv0.at[piece, stream]),
                          moved(axis, (low, high)[bit](here[axis])))

    def hops(phase, stream, step):
        span = PHASE_SPANS[phase, stream]
        axis, bit, bits, one, two = halves(stream)

        def sems(number):
            return send.at[phase, stream, number], recv.at[phase, stream, number]

        if step == 1:
            return [copy_tiles(stream, span, one + (1 - bits[1 - bit]) * 16, 16, 32, sems(0),
                               moved(axis, (low, high)[1 - bit](here[axis])))]
        ring = ORDERS[stream][step]
        out = []
        for k in (2, 1, 3):
            to = (here[ring] + k) % 4
            if step == 2:
                away, length, offset = two + to * 4, 4, 48 + 4 * (k - 1)
            else:
                away, length, offset = two + here[ORDERS[stream][2]] * 4 + to, 1, 60 + (k - 1)
            out.append(copy_tiles(stream, span, away, length, offset, sems(3 * step - 6 + k), moved(ring, to)))
        return out

    def final_slot(stream):
        return slot_of(here, stream)

    def launch(piece):
        for stream in range(STREAMS):
            if (piece, stream) in PIECE_SPANS:
                first_hop(piece, stream).start()

    def add_landed(stream, span, step):
        _, _, _, one, two = halves(stream)
        second, third = (here[axis] for axis in ORDERS[stream][2:])
        keep, length, offset, count = (
            (one, 32, 0, 1), (two, 16, 32, 1), (two + second * 4, 4, 48, 3),
            (two + second * 4 + third, 1, 60, 3))[step]
        for unit in range(*span):
            total = own[stream][unit, pl.ds(keep, length)]
            for k in range(count):
                total += landed[stream][unit, pl.ds(offset + k * length, length)]
            own[stream][unit, pl.ds(keep, length)] = total

    def advance(phase, step):
        for stream in range(STREAMS):
            if (phase, stream) not in PHASE_SPANS:
                continue
            if step == 0:
                for piece in PHASES[phase]:
                    if (piece, stream) in PIECE_SPANS:
                        first_hop(piece, stream).wait()
                        add_landed(stream, PIECE_SPANS[piece, stream], 0)
            else:
                for copy in hops(phase, stream, step):
                    copy.wait()
                add_landed(stream, PHASE_SPANS[phase, stream], step)
            if step < LEVELS - 1:
                for copy in hops(phase, stream, step + 1):
                    copy.start()

    def spread_pupil(m):
        core_copy(m, 0).wait()
        core_copy(m, 1).wait()

        def body(yx, carry):
            for zz in range(4):
                at = {"y": yx // 4, "x": yx % 4, "z": zz}
                cols = slice(zz * 128, (zz + 1) * 128)
                for g in range(4):
                    stream, unit = PLACE[m, g]
                    rows = pl.ds(pl.multiple_of(yx * 32 + g * 8, 8), 8)
                    own[stream][unit, slot_of(at, stream)] = field[core, m, rows, cols] + peer[m, rows, cols]
            return carry

        lax.fori_loop(0, 16, body, 0)
        launch(m)

    def grad_copy(i):
        rows = pl.ds(i * H, H)
        return pltpu.make_async_remote_copy(
            src_ref=grads.at[other, rows], dst_ref=peer_grad.at[rows],
            send_sem=(core_send.at[8], core_send.at[10])[i], recv_sem=(core_recv.at[8], core_recv.at[10])[i],
            device_id=partner, device_id_type=MESH)

    mark_copy = pltpu.make_async_remote_copy(
        src_ref=mark, dst_ref=part_mark, send_sem=core_send.at[9],
        recv_sem=core_recv.at[9], device_id=partner, device_id_type=MESH)

    def backward(m, between=()):
        weigh_fold(m)
        for i in range(2):
            transform(m, i)
            if m == 0 and i == 0:
                pl.semaphore_wait(barrier, len(greeted))
            if m == MODES - 1:
                grad_copy(i).start()
            core_copy(m, i).start()
            if i == 0:
                for task, *values in between:
                    task(*values)

    along = lax.broadcasted_iota(jnp.int32, (N, 128), 1).astype(F32)
    down = lax.broadcasted_iota(jnp.int32, (N, 128), 0).astype(F32)

    def wrap(value):
        return jnp.where(value >= float(N), value - float(N), value)

    def one_hots(shifts):
        for b in range(4):
            at = slice(b * 128, (b + 1) * 128)
            to = wrap(along[:1] + float(b * 128) + shifts[0, :1, :])
            hit = (down == wrap(to)).astype(F32).astype(BF16)
            shift_rows[:, at] = hit
            shift_rows[:, N + b * 128:N + (b + 1) * 128] = hit
            to = wrap(down + shifts[1, :1, :])
            hit = (along + float(b * 128) == wrap(to)).astype(F32).astype(BF16)
            shift_cols[:N, at] = hit
            shift_cols[N:, at] = hit

    def roll(whole, shifts, number):
        one_hots(shifts)
        coarse = whole.astype(BF16)
        parts[:N, :] = coarse
        parts[N:, :] = (whole - coarse.astype(F32)).astype(BF16)
        whole = dot(shift_rows[...], parts[...])
        coarse = whole.astype(BF16)
        parts_t[:, :N] = coarse
        parts_t[:, N:] = (whole - coarse.astype(F32)).astype(BF16)
        folded[number] = dot(parts_t[...], shift_cols[...])

    backward(0)
    mark_copy.start()
    backward(1, ((spread_pupil, 0),))
    backward(2, ((spread_pupil, 1),))
    backward(3, ((spread_pupil, 2),))
    mark_copy.wait()
    roll(grads[core], mark, 0)
    advance(0, 0)
    grad_copy(0).wait()
    grad_copy(1).wait()
    roll(peer_grad[...], part_mark, 1)
    spread_pupil(3)

    iota_r = lax.broadcasted_iota(jnp.int32, (8, 128), 0).astype(F32)
    iota_c = lax.broadcasted_iota(jnp.int32, (8, 128), 1).astype(F32)

    def window(yx, carry):
        for zz in range(2):
            for g in range(2):
                base = 256 * zz + yx * 16 + g * 8
                rows = pl.ds(pl.multiple_of(base, 8), 8)
                row_no = iota_r + base.astype(F32)
                row_a = row_no < mark[0]
                row_b = row_no < part_mark[0]
                for block in range(4):
                    cols = slice(block * 128, (block + 1) * 128)
                    col_no = iota_c + float(block * 128)
                    col_a = col_no < mark[1]
                    col_b = col_no < part_mark[1]
                    value_a = folded[0, rows, cols]
                    value_b = folded[1, rows, cols]
                    ra1 = jnp.where(row_a, value_a, 0.0)
                    ra0 = value_a - ra1
                    rb1 = jnp.where(row_b, value_b, 0.0)
                    rb0 = value_b - rb1
                    for upper, (va, vb) in enumerate(((ra0, rb0), (ra1, rb1))):
                        va1 = jnp.where(col_a, va, 0.0)
                        vb1 = jnp.where(col_b, vb, 0.0)
                        tiles = ((va - va1) + (vb - vb1), va1 + vb1)
                        at = {"y": yx // 4, "x": yx % 4, "z": 2 * upper + zz}
                        for later in range(2):
                            stream, unit = PLACE[CANVAS, g * 8 + later * 4 + block]
                            own[stream][unit, slot_of(at, stream)] = tiles[later]
        return carry

    lax.fori_loop(0, 16, window, 0)
    launch(CANVAS)

    for phase, step in BEFORE:
        advance(phase, step)

    for m in range(MODES):
        for g in range(4):
            stream, unit = PLACE[m, g]
            pupil_src[m, g * 8:(g + 1) * 8, :] = own[stream][unit, final_slot(stream)]
    block = pl.ds(pl.multiple_of((core * 4 + z) * 128, 128), 128)
    copies = []
    for number, (c, d) in enumerate(column):
        to_core = (core + c) % 2
        copies.append(pltpu.make_async_remote_copy(
            src_ref=pupil_src.at[:, pl.ds(pl.multiple_of(to_core * 16, 16), 16), :],
            dst_ref=out_pup.at[:, :, block],
            send_sem=gather_send.at[number], recv_sem=gather_recv.at[number],
            device_id=device(y, x, to_core, (z + d) % 4), device_id_type=MESH))
        copies[-1].start()
    out_pup[:, :, block] = pupil_src[:, pl.ds(pl.multiple_of(core * 16, 16), 16), :]

    for phase, step in AFTER:
        advance(phase, step)

    for g in range(2):
        for b in range(8):
            stream, unit = PLACE[CANVAS, g * 8 + b]
            canvas_src[g, :, b * 128:(b + 1) * 128] = own[stream][unit, final_slot(stream)]
    half_cols = pl.ds(pl.multiple_of(core * SPEC, SPEC), SPEC)
    last = pltpu.make_async_remote_copy(
        src_ref=canvas_src.at[other], dst_ref=out_spec.at[0, :, half_cols],
        send_sem=gather_send.at[7], recv_sem=gather_recv.at[7], device_id=partner, device_id_type=MESH)
    last.start()
    out_spec[0, :, half_cols] = canvas_src[core]
    for copy in copies:
        copy.wait()
    last.wait()


def hand_over(spec_in, pup_in, spec_out, pup_out):
    spec_out[...] = spec_in[...]
    pup_out[...] = pup_in[...]


def local(spectrum, pupils, offsets, measured):
    vmem = pl.BlockSpec(memory_space=pltpu.VMEM)
    half, half_t, swap = (jnp.asarray(table) for table in tables())
    scratch = [
        pltpu.VMEM((2, N, N), BF16),
        pltpu.VMEM((2, MODES, N, N), F32),
        pltpu.VMEM((N, N), F32),
        pltpu.VMEM((N, N), BF16),
        pltpu.VMEM((2, 2, N, N), BF16),
        pltpu.VMEM((2, N, N), F32),
        pltpu.VMEM((2, N, N), F32),
        pltpu.VMEM((N, 2 * N), BF16),
        pltpu.VMEM((2 * N, N), BF16),
        pltpu.VMEM((2 * N, N), BF16),
        pltpu.VMEM((N, 2 * N), BF16),
        pltpu.VMEM((N, N), F32),
        pltpu.VMEM((2, 8, 128), F32),
        pltpu.VMEM((MODES, N, N), F32),
        pltpu.VMEM((MODES, 32, 128), F32),
        pltpu.VMEM((2, 8, SPEC), F32),
        pltpu.VMEM((MODES, N, 2 * N), BF16),
        pltpu.VMEM((2, 8, 128), F32),
        pltpu.VMEM((N, 2 * N), BF16),
        pltpu.VMEM((SPEC, 2 * SPEC), BF16),
        pltpu.VMEM((1, N, N), BF16),
        pltpu.VMEM((N, N), BF16),
        pltpu.VMEM((N, N), BF16),
        pltpu.VMEM((H, H), BF16),
        pltpu.VMEM((N, SPEC), BF16),
        pltpu.VMEM((SPEC, N), BF16),
    ]
    scratch += [pltpu.VMEM((count, 64, 8, 128), F32) for count in COUNTS]
    scratch += [pltpu.VMEM((count, 63, 8, 128), F32) for count in COUNTS]
    scratch += [pltpu.SemaphoreType.DMA((11,)), pltpu.SemaphoreType.DMA((11,))]
    scratch += [pltpu.SemaphoreType.DMA((len(PIECES), STREAMS)), pltpu.SemaphoreType.DMA((len(PIECES), STREAMS))]
    scratch += [pltpu.SemaphoreType.DMA((len(PHASES), STREAMS, 7)), pltpu.SemaphoreType.DMA((len(PHASES), STREAMS, 7))]
    scratch += [pltpu.SemaphoreType.DMA((8,)), pltpu.SemaphoreType.DMA((8,)), pltpu.SemaphoreType.DMA((MODES + 6,))]
    outs = tuple(pl.pallas_call(
        kernel,
        out_shape=(
            jax.ShapeDtypeStruct((1, 8, 2 * SPEC), F32),
            jax.ShapeDtypeStruct((MODES, 16, 2 * N), F32),
        ),
        in_specs=[vmem] + [pl.BlockSpec(memory_space=pl.ANY)] * 6,
        out_specs=(vmem, vmem),
        scratch_shapes=scratch,
        compiler_params=pltpu.CompilerParams(
            collective_id=0, has_side_effects=True, vmem_limit_bytes=60 * 2**20),
    )(offsets, spectrum, pupils, measured, half, half_t, swap))
    return tuple(pl.pallas_call(
        hand_over,
        out_shape=tuple(jax.ShapeDtypeStruct(out.shape, F32) for out in outs),
        in_specs=[vmem] * 2,
        out_specs=(vmem, vmem),
    )(*outs))


def solution(mesh):
    return jax.shard_map(
        local,
        mesh=mesh,
        in_specs=(P(), P(), P(("led", "tile"), None), P(("led", "tile"), None, None)),
        out_specs=(P("tile", "led", None), P(None, "led", None)),
        check_vma=False,
    )
```

```python
import math

import jax
import jax.numpy as jnp
import numpy as np
from jax import lax
from jax.experimental import pallas as pl
from jax.experimental.pallas import tpu as pltpu
from jax.sharding import PartitionSpec as P

MESH = pl.DeviceIdType.MESH
N = 512
H = 256
MODES = 4
SPEC = 1024
F32 = jnp.float32
BF16 = jnp.bfloat16

ORDERS = (("y", 0, "x", "z"), ("x", 0, "z", "y"), ("z", 0, "y", "x"),
          ("y", 1, "z", "x"), ("x", 1, "y", "z"), ("z", 1, "x", "y"))
LEVELS = 4

STREAMS = 6
PIECES = (
    (3, 4, 4, 5),
    (0, 1, 2, 5),
    (0, 2, 3, 5),
    (3, 4, 4, 5),
    (0, 0, 0, 1, 1, 1, 2, 2, 2, 3, 3, 4, 4, 5, 5, 5),
)
CANVAS = 4
PHASES = ((0, 1), (2, 3), (4,))
BEFORE = ((0, 1), (1, 0), (2, 0), (0, 2), (1, 1), (2, 1), (0, 3), (1, 2), (2, 2), (1, 3))
AFTER = ((2, 3),)


def plan():
    counts = [0] * STREAMS
    place, pieces, phases = {}, {}, {}
    for number, streams in enumerate(PIECES):
        first = list(counts)
        for unit, stream in enumerate(streams):
            place[number, unit] = (stream, counts[stream])
            counts[stream] += 1
        for stream in range(STREAMS):
            if counts[stream] > first[stream]:
                pieces[number, stream] = (first[stream], counts[stream])
    for number, members in enumerate(PHASES):
        for stream in range(STREAMS):
            spans = [pieces[member, stream] for member in members if (member, stream) in pieces]
            if spans:
                phases[number, stream] = (spans[0][0], spans[-1][1])
    return counts, place, pieces, phases


COUNTS, PLACE, PIECE_SPANS, PHASE_SPANS = plan()


def tables():
    positions = np.arange(N, dtype=np.int64)
    angles = (positions[:, None] * positions[None, :] % N).astype(np.float32) * np.float32(2.0 * math.pi / N)
    factor = np.float32(1.0 / math.sqrt(N))
    cosine = (np.cos(angles) * factor).astype(BF16)
    sine = (np.sin(angles) * factor).astype(BF16)
    half = np.concatenate([cosine[:H], sine[:H]], axis=0)
    half[H] = cosine[H]
    swap = np.zeros((H, H), np.float32)
    swap[(H - np.arange(H)) % H, np.arange(H)] = 1.0
    return half, np.ascontiguousarray(half.T), swap.astype(BF16)


def low_bit(position):
    return ((position + 1) // 2) % 2


def high_bit(position):
    return position // 2


def slot_of(at, stream):
    axis, bit, second, third = ORDERS[stream]
    bits = low_bit(at[axis]), high_bit(at[axis])
    return ((bits[bit] * 2 + bits[1 - bit]) * 4 + at[second]) * 4 + at[third]


def dot(a, b):
    return jnp.dot(a, b, preferred_element_type=F32)


def kernel(offs, spectrum, pupils, measured, table, table_t, swap_in, out_spec, out_pup, *scratch):
    (half_s, field, inten, measp, folds, grads, folded, shift_rows, shift_cols, parts, parts_t, peer_grad, part_mark,
     peer, pupil_src, canvas_src, pup, mark, patch, whole, meas, tab, tabt, swap, pick_row, pick_col) = scratch[:26]
    own = scratch[26:32]
    landed = scratch[32:38]
    (core_send, core_recv, send0, recv0, send, recv, gather_send, gather_recv, load) = scratch[38:]

    def pupil_load(m):
        return pltpu.make_async_copy(pupils.at[m], pup.at[m], load.at[m])

    loads = [
        pltpu.make_async_copy(source, target, load.at[MODES + number])
        for number, (source, target) in enumerate((
            (spectrum.at[:, :SPEC], whole.at[:, :SPEC]), (table, tab), (table_t, tabt), (measured, meas), (swap_in, swap),
            (spectrum.at[:, SPEC:], whole.at[:, SPEC:])))
    ]
    loads[0].start()
    loads[5].start()
    loads[1].start()
    pupil_load(0).start()
    for copy in loads[2:5]:
        copy.start()
    for m in range(1, MODES):
        pupil_load(m).start()


    led = lax.axis_index("led")
    z = lax.axis_index("tile")
    core = led % 2
    x = (led // 2) % 4
    y = led // 8
    other = 1 - core

    def device(yy, xx, cc, zz):
        return ((yy * 4 + xx) * 2 + cc, zz)

    def low(p):
        return p + 1 - 2 * (p % 2)

    def high(p):
        return 3 - p

    here = {"y": y, "x": x, "z": z}

    def moved(axis, position):
        there = dict(here, **{axis: position})
        return device(there["y"], there["x"], core, there["z"])

    partner = device(y, x, other, z)
    column = [(c, d) for d in range(4) for c in range(2) if (c, d) != (0, 0)]

    barrier = pltpu.get_barrier_semaphore()
    greeted = [moved(axis, (here[axis] + k) % 4) for axis in ("y", "x") for k in range(1, 4)]
    greeted += [device(y, x, (core + c) % 2, (z + d) % 4) for c, d in column]
    for target in greeted:
        pl.semaphore_signal(barrier, inc=1, device_id=target, device_id_type=MESH)

    mark[0] = jnp.broadcast_to(offs[:, 0:1], (8, 128)).astype(F32)
    mark[1] = jnp.broadcast_to(offs[:, 1:2], (8, 128)).astype(F32)
    rise = lax.broadcasted_iota(jnp.int32, (N, 128), 1) - lax.broadcasted_iota(jnp.int32, (N, 128), 0)
    fall = lax.broadcasted_iota(jnp.int32, (SPEC, 128), 0) - lax.broadcasted_iota(jnp.int32, (SPEC, 128), 1)
    for b in range(8):
        pick_row[:, b * 128:(b + 1) * 128] = (
            rise.astype(F32) == mark[0, :1, :] - float(b * 128)).astype(F32).astype(BF16)
    for b in range(4):
        pick_col[:, b * 128:(b + 1) * 128] = (
            fall.astype(F32) == mark[1, :1, :] + float(b * 128)).astype(F32).astype(BF16)
    for number in range(2):
        loads[5 * number].wait()
        window = dot(pick_row[...], whole[:, number * SPEC:(number + 1) * SPEC]).astype(BF16)
        patch[:, number * N:(number + 1) * N] = dot(window, pick_col[...]).astype(BF16)

    inten[...] = jnp.zeros_like(inten)
    for copy in loads[1:3]:
        copy.wait()

    lane0 = lax.broadcasted_iota(jnp.int32, (1, 128), 1) == 0
    row0 = lax.broadcasted_iota(jnp.int32, (16, 1), 0) == 0

    def forward(m, carry):
        pupil_load(m).wait()
        for c in range(2):
            cols = slice(c * H, (c + 1) * H)
            cols_i = slice(N + c * H, N + (c + 1) * H)
            pr = patch[:, cols].astype(F32)
            pi = patch[:, cols_i].astype(F32)
            qr = pup[m, :, cols].astype(F32)
            qi = pup[m, :, cols_i].astype(F32)
            er = (pr * qr - pi * qi).astype(BF16)
            ei = (pr * qi + pi * qr).astype(BF16)
            u = dot(tab[...], er)
            v = dot(tab[...], ei)
            half_s[0, :H, cols] = (u[:H] - v[H:]).astype(BF16)
            half_s[0, H:, cols] = (u[:H] + v[H:]).astype(BF16)
            half_s[1, :H, cols] = (v[:H] + u[H:]).astype(BF16)
            half_s[1, H:, cols] = (v[:H] - u[H:]).astype(BF16)
            ut, ub, vt, vb = u[:16], u[H:H + 16], v[:16], v[H:H + 16]
            half_s[0, :16, cols] = jnp.where(row0, ut, ut - vb).astype(BF16)
            half_s[0, H:H + 16, cols] = jnp.where(row0, ub, ut + vb).astype(BF16)
            half_s[1, :16, cols] = jnp.where(row0, vt, vt + ub).astype(BF16)
            half_s[1, H:H + 16, cols] = jnp.where(row0, vb, vt - ub).astype(BF16)
        for r in range(2):
            rows = slice(r * H, (r + 1) * H)
            u = dot(half_s[0, rows, :], tabt[...])
            v = dot(half_s[1, rows, :], tabt[...])
            for b in range(2):
                left = slice(b * 128, (b + 1) * 128)
                right = slice(H + b * 128, H + (b + 1) * 128)
                uc, us, vc, vs = u[:, left], u[:, right], v[:, left], v[:, right]
                rl, il, rr, ir = uc - vs, vc + us, uc + vs, vc - us
                if b == 0:
                    rl = jnp.where(lane0, uc, rl)
                    il = jnp.where(lane0, vc, il)
                    rr = jnp.where(lane0, us, rr)
                    ir = jnp.where(lane0, vs, ir)
                field[0, m, rows, left] = rl
                field[1, m, rows, left] = il
                field[0, m, rows, right] = rr
                field[1, m, rows, right] = ir
                inten[rows, left] += rl * rl + il * il
                inten[rows, right] += rr * rr + ir * ir
        return carry

    lax.fori_loop(0, MODES, forward, 0)

    for copy in loads[3:5]:
        copy.wait()
    measp[:, :H] = meas[0, :, :H]
    measp[:, H:] = dot(meas[0, :, H:], swap[...]).astype(BF16)
    measp[H:, :] = dot(swap[...], measp[H:, :]).astype(BF16)

    def weigh(i, carry):
        rows = pl.ds(pl.multiple_of(i * 64, 64), 64)
        level = measp[rows, :].astype(F32)
        inten[rows, :] = 1.0 - level * lax.rsqrt(level * jnp.maximum(inten[rows, :], 0.1))
        return carry

    lax.fori_loop(0, N // 64, weigh, 0)

    def weigh_fold(m):
        xs = folds.at[m % 2]
        for i in range(H // 32):
            top = slice(i * 32, i * 32 + 32)
            bottom = slice(H + i * 32, H + i * 32 + 32)
            wt, wb = inten[top, :], inten[bottom, :]
            rt, rb = wt * field[0, m, top, :], wb * field[0, m, bottom, :]
            it, ib = wt * field[1, m, top, :], wb * field[1, m, bottom, :]
            xs[0, top, :] = (rt + rb).astype(BF16)
            xs[0, bottom, :] = (it - ib).astype(BF16)
            xs[1, top, :] = (it + ib).astype(BF16)
            xs[1, bottom, :] = (rb - rt).astype(BF16)
        wt, wb = inten[:16, :], inten[H:H + 16, :]
        rt, rb = wt * field[0, m, :16, :], wb * field[0, m, H:H + 16, :]
        it, ib = wt * field[1, m, :16, :], wb * field[1, m, H:H + 16, :]
        xs[0, :16, :] = jnp.where(row0, rt, rt + rb).astype(BF16)
        xs[0, H:H + 16, :] = jnp.where(row0, rb, it - ib).astype(BF16)
        xs[1, :16, :] = jnp.where(row0, it, it + ib).astype(BF16)
        xs[1, H:H + 16, :] = jnp.where(row0, ib, rb - rt).astype(BF16)

    def transform(m, i):
        xs = folds.at[m % 2]
        rows = slice(i * H, (i + 1) * H)
        fr = dot(tabt[rows, :], xs[0])
        fi = dot(tabt[rows, :], xs[1])
        for b in range(2):
            left = slice(b * 128, (b + 1) * 128)
            right = slice(H + b * 128, H + (b + 1) * 128)
            rl, rr, il, ir = fr[:, left], fr[:, right], fi[:, left], fi[:, right]
            pr, mi, p_i, mr = rl + rr, il - ir, il + ir, rr - rl
            if b == 0:
                pr = jnp.where(lane0, rl, pr)
                mi = jnp.where(lane0, rr, mi)
                p_i = jnp.where(lane0, il, p_i)
                mr = jnp.where(lane0, ir, mr)
            half_s[0, rows, left] = pr.astype(BF16)
            half_s[0, rows, right] = mi.astype(BF16)
            half_s[1, rows, left] = p_i.astype(BF16)
            half_s[1, rows, right] = mr.astype(BF16)
        gr = dot(half_s[0, rows, :], tab[...])
        gi = dot(half_s[1, rows, :], tab[...])
        qr, qi = pup[m, rows, :N].astype(F32), pup[m, rows, N:].astype(F32)
        sr = qr * gr + qi * gi
        si = qr * gi - qi * gr
        if m == 0:
            grads[0, rows, :] = sr
            grads[1, rows, :] = si
        else:
            grads[0, rows, :] += sr
            grads[1, rows, :] += si
        pr, pi = patch[rows, :N].astype(F32), patch[rows, N:].astype(F32)
        field[0, m, rows, :] = pr * gr + pi * gi
        field[1, m, rows, :] = pr * gi - pi * gr

    def core_copy(m, i):
        rows = pl.ds(i * H, H)
        return pltpu.make_async_remote_copy(
            src_ref=field.at[other, m, rows], dst_ref=peer.at[m, rows], send_sem=core_send.at[2 * m + i],
            recv_sem=core_recv.at[2 * m + i], device_id=partner, device_id_type=MESH)

    def copy_tiles(stream, span, away, length, offset, sems, target):
        units = pl.ds(span[0], span[1] - span[0])
        return pltpu.make_async_remote_copy(
            src_ref=own[stream].at[units, pl.ds(away, length)],
            dst_ref=landed[stream].at[units, pl.ds(offset, length)],
            send_sem=sems[0], recv_sem=sems[1], device_id=target, device_id_type=MESH)

    def halves(stream):
        axis, bit, second, third = ORDERS[stream]
        bits = low_bit(here[axis]), high_bit(here[axis])
        one = bits[bit] * 32
        return axis, bit, bits, one, one + bits[1 - bit] * 16

    def first_hop(piece, stream):
        axis, bit, bits, _, _ = halves(stream)
        return copy_tiles(stream, PIECE_SPANS[piece, stream], (1 - bits[bit]) * 32, 32, 0,
                          (send0.at[piece, stream], recv0.at[piece, stream]),
                          moved(axis, (low, high)[bit](here[axis])))

    def hops(phase, stream, step):
        span = PHASE_SPANS[phase, stream]
        axis, bit, bits, one, two = halves(stream)

        def sems(number):
            return send.at[phase, stream, number], recv.at[phase, stream, number]

        if step == 1:
            return [copy_tiles(stream, span, one + (1 - bits[1 - bit]) * 16, 16, 32, sems(0),
                               moved(axis, (low, high)[1 - bit](here[axis])))]
        ring = ORDERS[stream][step]
        out = []
        for k in (2, 1, 3):
            to = (here[ring] + k) % 4
            if step == 2:
                away, length, offset = two + to * 4, 4, 48 + 4 * (k - 1)
            else:
                away, length, offset = two + here[ORDERS[stream][2]] * 4 + to, 1, 60 + (k - 1)
            out.append(copy_tiles(stream, span, away, length, offset, sems(3 * step - 6 + k), moved(ring, to)))
        return out

    def final_slot(stream):
        return slot_of(here, stream)

    def launch(piece):
        for stream in range(STREAMS):
            if (piece, stream) in PIECE_SPANS:
                first_hop(piece, stream).start()

    def add_landed(stream, span, step):
        _, _, _, one, two = halves(stream)
        second, third = (here[axis] for axis in ORDERS[stream][2:])
        keep, length, offset, count = (
            (one, 32, 0, 1), (two, 16, 32, 1), (two + second * 4, 4, 48, 3),
            (two + second * 4 + third, 1, 60, 3))[step]
        for unit in range(*span):
            total = own[stream][unit, pl.ds(keep, length)]
            for k in range(count):
                total += landed[stream][unit, pl.ds(offset + k * length, length)]
            own[stream][unit, pl.ds(keep, length)] = total

    def advance(phase, step):
        for stream in range(STREAMS):
            if (phase, stream) not in PHASE_SPANS:
                continue
            if step == 0:
                for piece in PHASES[phase]:
                    if (piece, stream) in PIECE_SPANS:
                        first_hop(piece, stream).wait()
                        add_landed(stream, PIECE_SPANS[piece, stream], 0)
            else:
                for copy in hops(phase, stream, step):
                    copy.wait()
                add_landed(stream, PHASE_SPANS[phase, stream], step)
            if step < LEVELS - 1:
                for copy in hops(phase, stream, step + 1):
                    copy.start()

    def y_slots(yy):
        return [slot_of({"y": yy, "x": 0, "z": 0}, stream) for stream in range(STREAMS)]

    def spread_pupil(m):
        core_copy(m, 0).wait()
        core_copy(m, 1).wait()

        def body(yy, carry):
            begin = y_slots(yy)
            for xx in range(4):
                for zz in range(4):
                    at = {"y": 0, "x": xx, "z": zz}
                    cols = slice(zz * 128, (zz + 1) * 128)
                    for g in range(4):
                        stream, unit = PLACE[m, g]
                        rows = pl.ds(pl.multiple_of(yy * 128 + (xx * 32 + g * 8), 8), 8)
                        slot = begin[stream] + slot_of(at, stream)
                        own[stream][unit, slot] = field[core, m, rows, cols] + peer[m, rows, cols]
            return carry

        lax.fori_loop(0, 4, body, 0)
        launch(m)

    def grad_copy(i):
        rows = pl.ds(i * H, H)
        return pltpu.make_async_remote_copy(
            src_ref=grads.at[other, rows], dst_ref=peer_grad.at[rows],
            send_sem=(core_send.at[8], core_send.at[10])[i], recv_sem=(core_recv.at[8], core_recv.at[10])[i],
            device_id=partner, device_id_type=MESH)

    mark_copy = pltpu.make_async_remote_copy(
        src_ref=mark, dst_ref=part_mark, send_sem=core_send.at[9],
        recv_sem=core_recv.at[9], device_id=partner, device_id_type=MESH)

    def backward(m, between=()):
        weigh_fold(m)
        for i in range(2):
            transform(m, i)
            if m == 0 and i == 0:
                pl.semaphore_wait(barrier, len(greeted))
            if m == MODES - 1:
                grad_copy(i).start()
            core_copy(m, i).start()
            if i == 0:
                for task, *values in between:
                    task(*values)

    along = lax.broadcasted_iota(jnp.int32, (N, 128), 1).astype(F32)
    down = lax.broadcasted_iota(jnp.int32, (N, 128), 0).astype(F32)

    def wrap(value):
        return jnp.where(value >= float(N), value - float(N), value)

    def one_hots(shifts):
        for b in range(4):
            at = slice(b * 128, (b + 1) * 128)
            to = wrap(along[:1] + float(b * 128) + shifts[0, :1, :])
            hit = (down == wrap(to)).astype(F32).astype(BF16)
            shift_rows[:, at] = hit
            shift_rows[:, N + b * 128:N + (b + 1) * 128] = hit
            to = wrap(down + shifts[1, :1, :])
            hit = (along + float(b * 128) == wrap(to)).astype(F32).astype(BF16)
            shift_cols[:N, at] = hit
            shift_cols[N:, at] = hit

    def roll(whole, shifts, number):
        one_hots(shifts)
        coarse = whole.astype(BF16)
        parts[:N, :] = coarse
        parts[N:, :] = (whole - coarse.astype(F32)).astype(BF16)
        whole = dot(shift_rows[...], parts[...])
        coarse = whole.astype(BF16)
        parts_t[:, :N] = coarse
        parts_t[:, N:] = (whole - coarse.astype(F32)).astype(BF16)
        folded[number] = dot(parts_t[...], shift_cols[...])

    backward(0)
    mark_copy.start()
    backward(1, ((spread_pupil, 0),))
    backward(2, ((spread_pupil, 1),))
    backward(3, ((spread_pupil, 2),))
    mark_copy.wait()
    roll(grads[core], mark, 0)
    advance(0, 0)
    grad_copy(0).wait()
    grad_copy(1).wait()
    roll(peer_grad[...], part_mark, 1)
    spread_pupil(3)

    iota_r = lax.broadcasted_iota(jnp.int32, (8, 128), 0).astype(F32)
    iota_c = lax.broadcasted_iota(jnp.int32, (8, 128), 1).astype(F32)

    def window(yy, carry):
        begin = y_slots(yy)
        for xx in range(4):
            for zz in range(2):
                for g in range(2):
                    base = yy * 64 + (256 * zz + xx * 16 + g * 8)
                    rows = pl.ds(pl.multiple_of(base, 8), 8)
                    row_no = iota_r + base.astype(F32)
                    row_a = row_no < mark[0]
                    row_b = row_no < part_mark[0]
                    for block in range(4):
                        cols = slice(block * 128, (block + 1) * 128)
                        col_no = iota_c + float(block * 128)
                        col_a = col_no < mark[1]
                        col_b = col_no < part_mark[1]
                        value_a = folded[0, rows, cols]
                        value_b = folded[1, rows, cols]
                        ra1 = jnp.where(row_a, value_a, 0.0)
                        ra0 = value_a - ra1
                        rb1 = jnp.where(row_b, value_b, 0.0)
                        rb0 = value_b - rb1
                        for upper, (va, vb) in enumerate(((ra0, rb0), (ra1, rb1))):
                            va1 = jnp.where(col_a, va, 0.0)
                            vb1 = jnp.where(col_b, vb, 0.0)
                            tiles = ((va - va1) + (vb - vb1), va1 + vb1)
                            at = {"y": 0, "x": xx, "z": 2 * upper + zz}
                            for later in range(2):
                                stream, unit = PLACE[CANVAS, g * 8 + later * 4 + block]
                                own[stream][unit, begin[stream] + slot_of(at, stream)] = tiles[later]
        return carry

    lax.fori_loop(0, 4, window, 0)
    launch(CANVAS)

    for phase, step in BEFORE:
        advance(phase, step)

    for m in range(MODES):
        for g in range(4):
            stream, unit = PLACE[m, g]
            pupil_src[m, g * 8:(g + 1) * 8, :] = own[stream][unit, final_slot(stream)]
    block = pl.ds(pl.multiple_of((core * 4 + z) * 128, 128), 128)
    copies = []
    for number, (c, d) in enumerate(column):
        to_core = (core + c) % 2
        copies.append(pltpu.make_async_remote_copy(
            src_ref=pupil_src.at[:, pl.ds(pl.multiple_of(to_core * 16, 16), 16), :],
            dst_ref=out_pup.at[:, :, block],
            send_sem=gather_send.at[number], recv_sem=gather_recv.at[number],
            device_id=device(y, x, to_core, (z + d) % 4), device_id_type=MESH))
        copies[-1].start()
    out_pup[:, :, block] = pupil_src[:, pl.ds(pl.multiple_of(core * 16, 16), 16), :]

    for phase, step in AFTER:
        advance(phase, step)

    for g in range(2):
        for b in range(8):
            stream, unit = PLACE[CANVAS, g * 8 + b]
            canvas_src[g, :, b * 128:(b + 1) * 128] = own[stream][unit, final_slot(stream)]
    half_cols = pl.ds(pl.multiple_of(core * SPEC, SPEC), SPEC)
    last = pltpu.make_async_remote_copy(
        src_ref=canvas_src.at[other], dst_ref=out_spec.at[0, :, half_cols],
        send_sem=gather_send.at[7], recv_sem=gather_recv.at[7], device_id=partner, device_id_type=MESH)
    last.start()
    out_spec[0, :, half_cols] = canvas_src[core]
    for copy in copies:
        copy.wait()
    last.wait()


def hand_over(spec_in, pup_in, spec_out, pup_out):
    spec_out[...] = spec_in[...]
    pup_out[...] = pup_in[...]


def local(spectrum, pupils, offsets, measured):
    vmem = pl.BlockSpec(memory_space=pltpu.VMEM)
    half, half_t, swap = (jnp.asarray(table) for table in tables())
    scratch = [
        pltpu.VMEM((2, N, N), BF16),
        pltpu.VMEM((2, MODES, N, N), F32),
        pltpu.VMEM((N, N), F32),
        pltpu.VMEM((N, N), BF16),
        pltpu.VMEM((2, 2, N, N), BF16),
        pltpu.VMEM((2, N, N), F32),
        pltpu.VMEM((2, N, N), F32),
        pltpu.VMEM((N, 2 * N), BF16),
        pltpu.VMEM((2 * N, N), BF16),
        pltpu.VMEM((2 * N, N), BF16),
        pltpu.VMEM((N, 2 * N), BF16),
        pltpu.VMEM((N, N), F32),
        pltpu.VMEM((2, 8, 128), F32),
        pltpu.VMEM((MODES, N, N), F32),
        pltpu.VMEM((MODES, 32, 128), F32),
        pltpu.VMEM((2, 8, SPEC), F32),
        pltpu.VMEM((MODES, N, 2 * N), BF16),
        pltpu.VMEM((2, 8, 128), F32),
        pltpu.VMEM((N, 2 * N), BF16),
        pltpu.VMEM((SPEC, 2 * SPEC), BF16),
        pltpu.VMEM((1, N, N), BF16),
        pltpu.VMEM((N, N), BF16),
        pltpu.VMEM((N, N), BF16),
        pltpu.VMEM((H, H), BF16),
        pltpu.VMEM((N, SPEC), BF16),
        pltpu.VMEM((SPEC, N), BF16),
    ]
    scratch += [pltpu.VMEM((count, 64, 8, 128), F32) for count in COUNTS]
    scratch += [pltpu.VMEM((count, 63, 8, 128), F32) for count in COUNTS]
    scratch += [pltpu.SemaphoreType.DMA((11,)), pltpu.SemaphoreType.DMA((11,))]
    scratch += [pltpu.SemaphoreType.DMA((len(PIECES), STREAMS)), pltpu.SemaphoreType.DMA((len(PIECES), STREAMS))]
    scratch += [pltpu.SemaphoreType.DMA((len(PHASES), STREAMS, 7)), pltpu.SemaphoreType.DMA((len(PHASES), STREAMS, 7))]
    scratch += [pltpu.SemaphoreType.DMA((8,)), pltpu.SemaphoreType.DMA((8,)), pltpu.SemaphoreType.DMA((MODES + 6,))]
    outs = tuple(pl.pallas_call(
        kernel,
        out_shape=(
            jax.ShapeDtypeStruct((1, 8, 2 * SPEC), F32),
            jax.ShapeDtypeStruct((MODES, 16, 2 * N), F32),
        ),
        in_specs=[vmem] + [pl.BlockSpec(memory_space=pl.ANY)] * 6,
        out_specs=(vmem, vmem),
        scratch_shapes=scratch,
        compiler_params=pltpu.CompilerParams(
            collective_id=0, has_side_effects=True, vmem_limit_bytes=60 * 2**20),
    )(offsets, spectrum, pupils, measured, half, half_t, swap))
    return tuple(pl.pallas_call(
        hand_over,
        out_shape=tuple(jax.ShapeDtypeStruct(out.shape, F32) for out in outs),
        in_specs=[vmem] * 2,
        out_specs=(vmem, vmem),
    )(*outs))


def solution(mesh):
    return jax.shard_map(
        local,
        mesh=mesh,
        in_specs=(P(), P(), P(("led", "tile"), None), P(("led", "tile"), None, None)),
        out_specs=(P("tile", "led", None), P(None, "led", None)),
        check_vma=False,
    )
```

```python
import math

import jax
import jax.numpy as jnp
import numpy as np
from jax import lax
from jax.experimental import pallas as pl
from jax.experimental.pallas import tpu as pltpu
from jax.sharding import PartitionSpec as P

MESH = pl.DeviceIdType.MESH
N = 512
H = 256
MODES = 4
SPEC = 1024
F32 = jnp.float32
BF16 = jnp.bfloat16

ORDERS = (("y", 0, "x", "z"), ("x", 0, "z", "y"), ("z", 0, "y", "x"),
          ("y", 1, "z", "x"), ("x", 1, "y", "z"), ("z", 1, "x", "y"))
LEVELS = 4

STREAMS = 6
PIECES = (
    (3, 4, 4, 5),
    (0, 1, 2, 5),
    (0, 2, 3, 5),
    (3, 4, 4, 5),
    (0, 0, 0, 1, 1, 1, 2, 2, 2, 3, 3, 4, 4, 5, 5, 5),
)
CANVAS = 4
PHASES = ((0, 1), (2, 3), (4,))
BEFORE = ((1, 0), (0, 1), (2, 0), (0, 2), (1, 1), (2, 1), (0, 3), (1, 2), (2, 2), (1, 3))
AFTER = ((2, 3),)


def plan():
    counts = [0] * STREAMS
    place, pieces, phases = {}, {}, {}
    for number, streams in enumerate(PIECES):
        first = list(counts)
        for unit, stream in enumerate(streams):
            place[number, unit] = (stream, counts[stream])
            counts[stream] += 1
        for stream in range(STREAMS):
            if counts[stream] > first[stream]:
                pieces[number, stream] = (first[stream], counts[stream])
    for number, members in enumerate(PHASES):
        for stream in range(STREAMS):
            spans = [pieces[member, stream] for member in members if (member, stream) in pieces]
            if spans:
                phases[number, stream] = (spans[0][0], spans[-1][1])
    return counts, place, pieces, phases


COUNTS, PLACE, PIECE_SPANS, PHASE_SPANS = plan()


def tables():
    positions = np.arange(N, dtype=np.int64)
    angles = (positions[:, None] * positions[None, :] % N).astype(np.float32) * np.float32(2.0 * math.pi / N)
    factor = np.float32(1.0 / math.sqrt(N))
    cosine = (np.cos(angles) * factor).astype(BF16)
    sine = (np.sin(angles) * factor).astype(BF16)
    half = np.concatenate([cosine[:H], sine[:H]], axis=0)
    half[H] = cosine[H]
    swap = np.zeros((H, H), np.float32)
    swap[(H - np.arange(H)) % H, np.arange(H)] = 1.0
    return half, np.ascontiguousarray(half.T), swap.astype(BF16)


def low_bit(position):
    return ((position + 1) // 2) % 2


def high_bit(position):
    return position // 2


def slot_of(at, stream):
    axis, bit, second, third = ORDERS[stream]
    bits = low_bit(at[axis]), high_bit(at[axis])
    return ((bits[bit] * 2 + bits[1 - bit]) * 4 + at[second]) * 4 + at[third]


def dot(a, b):
    return jnp.dot(a, b, preferred_element_type=F32)


def kernel(offs, spectrum, pupils, measured, table, table_t, swap_in, out_spec, out_pup, *scratch):
    (half_s, field, inten, measp, folds, grads, folded, shift_rows, shift_cols, parts, parts_t, peer_grad, part_mark,
     peer, pupil_src, canvas_src, pup, mark, patch, whole, meas, tab, tabt, swap, pick_row, pick_col) = scratch[:26]
    own = scratch[26:32]
    landed = scratch[32:38]
    (core_send, core_recv, send0, recv0, send, recv, gather_send, gather_recv, load) = scratch[38:]

    def pupil_load(m):
        return pltpu.make_async_copy(pupils.at[m], pup.at[m], load.at[m])

    loads = [
        pltpu.make_async_copy(source, target, load.at[MODES + number])
        for number, (source, target) in enumerate((
            (spectrum.at[:, :SPEC], whole.at[:, :SPEC]), (table, tab), (table_t, tabt), (measured, meas), (swap_in, swap),
            (spectrum.at[:, SPEC:], whole.at[:, SPEC:])))
    ]
    loads[0].start()
    loads[5].start()
    loads[1].start()
    pupil_load(0).start()
    for copy in loads[2:5]:
        copy.start()
    for m in range(1, MODES):
        pupil_load(m).start()


    led = lax.axis_index("led")
    z = lax.axis_index("tile")
    core = led % 2
    x = (led // 2) % 4
    y = led // 8
    other = 1 - core

    def device(yy, xx, cc, zz):
        return ((yy * 4 + xx) * 2 + cc, zz)

    def low(p):
        return p + 1 - 2 * (p % 2)

    def high(p):
        return 3 - p

    here = {"y": y, "x": x, "z": z}

    def moved(axis, position):
        there = dict(here, **{axis: position})
        return device(there["y"], there["x"], core, there["z"])

    partner = device(y, x, other, z)
    column = [(c, d) for d in range(4) for c in range(2) if (c, d) != (0, 0)]

    barrier = pltpu.get_barrier_semaphore()
    greeted = [moved(axis, (here[axis] + k) % 4) for axis in ("y", "x") for k in range(1, 4)]
    greeted += [device(y, x, (core + c) % 2, (z + d) % 4) for c, d in column]
    for target in greeted:
        pl.semaphore_signal(barrier, inc=1, device_id=target, device_id_type=MESH)

    mark[0] = jnp.broadcast_to(offs[:, 0:1], (8, 128)).astype(F32)
    mark[1] = jnp.broadcast_to(offs[:, 1:2], (8, 128)).astype(F32)
    rise = lax.broadcasted_iota(jnp.int32, (N, 128), 1) - lax.broadcasted_iota(jnp.int32, (N, 128), 0)
    fall = lax.broadcasted_iota(jnp.int32, (SPEC, 128), 0) - lax.broadcasted_iota(jnp.int32, (SPEC, 128), 1)
    for b in range(8):
        pick_row[:, b * 128:(b + 1) * 128] = (
            rise.astype(F32) == mark[0, :1, :] - float(b * 128)).astype(F32).astype(BF16)
    for b in range(4):
        pick_col[:, b * 128:(b + 1) * 128] = (
            fall.astype(F32) == mark[1, :1, :] + float(b * 128)).astype(F32).astype(BF16)
    for number in range(2):
        loads[5 * number].wait()
        window = dot(pick_row[...], whole[:, number * SPEC:(number + 1) * SPEC]).astype(BF16)
        patch[:, number * N:(number + 1) * N] = dot(window, pick_col[...]).astype(BF16)

    inten[...] = jnp.zeros_like(inten)
    for copy in loads[1:3]:
        copy.wait()

    lane0 = lax.broadcasted_iota(jnp.int32, (1, 128), 1) == 0
    row0 = lax.broadcasted_iota(jnp.int32, (16, 1), 0) == 0

    def forward(m, carry):
        pupil_load(m).wait()
        for c in range(2):
            cols = slice(c * H, (c + 1) * H)
            cols_i = slice(N + c * H, N + (c + 1) * H)
            pr = patch[:, cols].astype(F32)
            pi = patch[:, cols_i].astype(F32)
            qr = pup[m, :, cols].astype(F32)
            qi = pup[m, :, cols_i].astype(F32)
            er = (pr * qr - pi * qi).astype(BF16)
            ei = (pr * qi + pi * qr).astype(BF16)
            u = dot(tab[...], er)
            v = dot(tab[...], ei)
            half_s[0, :H, cols] = (u[:H] - v[H:]).astype(BF16)
            half_s[0, H:, cols] = (u[:H] + v[H:]).astype(BF16)
            half_s[1, :H, cols] = (v[:H] + u[H:]).astype(BF16)
            half_s[1, H:, cols] = (v[:H] - u[H:]).astype(BF16)
            ut, ub, vt, vb = u[:16], u[H:H + 16], v[:16], v[H:H + 16]
            half_s[0, :16, cols] = jnp.where(row0, ut, ut - vb).astype(BF16)
            half_s[0, H:H + 16, cols] = jnp.where(row0, ub, ut + vb).astype(BF16)
            half_s[1, :16, cols] = jnp.where(row0, vt, vt + ub).astype(BF16)
            half_s[1, H:H + 16, cols] = jnp.where(row0, vb, vt - ub).astype(BF16)
        for r in range(2):
            rows = slice(r * H, (r + 1) * H)
            u = dot(half_s[0, rows, :], tabt[...])
            v = dot(half_s[1, rows, :], tabt[...])
            for b in range(2):
                left = slice(b * 128, (b + 1) * 128)
                right = slice(H + b * 128, H + (b + 1) * 128)
                uc, us, vc, vs = u[:, left], u[:, right], v[:, left], v[:, right]
                rl, il, rr, ir = uc - vs, vc + us, uc + vs, vc - us
                if b == 0:
                    rl = jnp.where(lane0, uc, rl)
                    il = jnp.where(lane0, vc, il)
                    rr = jnp.where(lane0, us, rr)
                    ir = jnp.where(lane0, vs, ir)
                field[0, m, rows, left] = rl
                field[1, m, rows, left] = il
                field[0, m, rows, right] = rr
                field[1, m, rows, right] = ir
                inten[rows, left] += rl * rl + il * il
                inten[rows, right] += rr * rr + ir * ir
        return carry

    lax.fori_loop(0, MODES, forward, 0)

    for copy in loads[3:5]:
        copy.wait()
    measp[:, :H] = meas[0, :, :H]
    measp[:, H:] = dot(meas[0, :, H:], swap[...]).astype(BF16)
    measp[H:, :] = dot(swap[...], measp[H:, :]).astype(BF16)

    def weigh(i, carry):
        rows = pl.ds(pl.multiple_of(i * 64, 64), 64)
        level = measp[rows, :].astype(F32)
        inten[rows, :] = 1.0 - level * lax.rsqrt(level * jnp.maximum(inten[rows, :], 0.1))
        return carry

    lax.fori_loop(0, N // 64, weigh, 0)

    def weigh_fold(m):
        xs = folds.at[m % 2]
        for i in range(H // 32):
            top = slice(i * 32, i * 32 + 32)
            bottom = slice(H + i * 32, H + i * 32 + 32)
            wt, wb = inten[top, :], inten[bottom, :]
            rt, rb = wt * field[0, m, top, :], wb * field[0, m, bottom, :]
            it, ib = wt * field[1, m, top, :], wb * field[1, m, bottom, :]
            xs[0, top, :] = (rt + rb).astype(BF16)
            xs[0, bottom, :] = (it - ib).astype(BF16)
            xs[1, top, :] = (it + ib).astype(BF16)
            xs[1, bottom, :] = (rb - rt).astype(BF16)
        wt, wb = inten[:16, :], inten[H:H + 16, :]
        rt, rb = wt * field[0, m, :16, :], wb * field[0, m, H:H + 16, :]
        it, ib = wt * field[1, m, :16, :], wb * field[1, m, H:H + 16, :]
        xs[0, :16, :] = jnp.where(row0, rt, rt + rb).astype(BF16)
        xs[0, H:H + 16, :] = jnp.where(row0, rb, it - ib).astype(BF16)
        xs[1, :16, :] = jnp.where(row0, it, it + ib).astype(BF16)
        xs[1, H:H + 16, :] = jnp.where(row0, ib, rb - rt).astype(BF16)

    def transform(m, i):
        xs = folds.at[m % 2]
        rows = slice(i * H, (i + 1) * H)
        fr = dot(tabt[rows, :], xs[0])
        fi = dot(tabt[rows, :], xs[1])
        for b in range(2):
            left = slice(b * 128, (b + 1) * 128)
            right = slice(H + b * 128, H + (b + 1) * 128)
            rl, rr, il, ir = fr[:, left], fr[:, right], fi[:, left], fi[:, right]
            pr, mi, p_i, mr = rl + rr, il - ir, il + ir, rr - rl
            if b == 0:
                pr = jnp.where(lane0, rl, pr)
                mi = jnp.where(lane0, rr, mi)
                p_i = jnp.where(lane0, il, p_i)
                mr = jnp.where(lane0, ir, mr)
            half_s[0, rows, left] = pr.astype(BF16)
            half_s[0, rows, right] = mi.astype(BF16)
            half_s[1, rows, left] = p_i.astype(BF16)
            half_s[1, rows, right] = mr.astype(BF16)
        gr = dot(half_s[0, rows, :], tab[...])
        gi = dot(half_s[1, rows, :], tab[...])
        qr, qi = pup[m, rows, :N].astype(F32), pup[m, rows, N:].astype(F32)
        sr = qr * gr + qi * gi
        si = qr * gi - qi * gr
        if m == 0:
            grads[0, rows, :] = sr
            grads[1, rows, :] = si
        else:
            grads[0, rows, :] += sr
            grads[1, rows, :] += si
        pr, pi = patch[rows, :N].astype(F32), patch[rows, N:].astype(F32)
        field[0, m, rows, :] = pr * gr + pi * gi
        field[1, m, rows, :] = pr * gi - pi * gr

    def core_copy(m, i):
        rows = pl.ds(i * H, H)
        return pltpu.make_async_remote_copy(
            src_ref=field.at[other, m, rows], dst_ref=peer.at[m, rows], send_sem=core_send.at[2 * m + i],
            recv_sem=core_recv.at[2 * m + i], device_id=partner, device_id_type=MESH)

    def copy_tiles(stream, span, away, length, offset, sems, target):
        units = pl.ds(span[0], span[1] - span[0])
        return pltpu.make_async_remote_copy(
            src_ref=own[stream].at[units, pl.ds(away, length)],
            dst_ref=landed[stream].at[units, pl.ds(offset, length)],
            send_sem=sems[0], recv_sem=sems[1], device_id=target, device_id_type=MESH)

    def halves(stream):
        axis, bit, second, third = ORDERS[stream]
        bits = low_bit(here[axis]), high_bit(here[axis])
        one = bits[bit] * 32
        return axis, bit, bits, one, one + bits[1 - bit] * 16

    def first_hop(piece, stream):
        axis, bit, bits, _, _ = halves(stream)
        return copy_tiles(stream, PIECE_SPANS[piece, stream], (1 - bits[bit]) * 32, 32, 0,
                          (send0.at[piece, stream], recv0.at[piece, stream]),
                          moved(axis, (low, high)[bit](here[axis])))

    def hops(phase, stream, step):
        span = PHASE_SPANS[phase, stream]
        axis, bit, bits, one, two = halves(stream)

        def sems(number):
            return send.at[phase, stream, number], recv.at[phase, stream, number]

        if step == 1:
            return [copy_tiles(stream, span, one + (1 - bits[1 - bit]) * 16, 16, 32, sems(0),
                               moved(axis, (low, high)[1 - bit](here[axis])))]
        ring = ORDERS[stream][step]
        out = []
        for k in (2, 1, 3):
            to = (here[ring] + k) % 4
            if step == 2:
                away, length, offset = two + to * 4, 4, 48 + 4 * (k - 1)
            else:
                away, length, offset = two + here[ORDERS[stream][2]] * 4 + to, 1, 60 + (k - 1)
            out.append(copy_tiles(stream, span, away, length, offset, sems(3 * step - 6 + k), moved(ring, to)))
        return out

    def final_slot(stream):
        return slot_of(here, stream)

    def launch(piece):
        for stream in range(STREAMS):
            if (piece, stream) in PIECE_SPANS:
                first_hop(piece, stream).start()

    def add_landed(stream, span, step):
        _, _, _, one, two = halves(stream)
        second, third = (here[axis] for axis in ORDERS[stream][2:])
        keep, length, offset, count = (
            (one, 32, 0, 1), (two, 16, 32, 1), (two + second * 4, 4, 48, 3),
            (two + second * 4 + third, 1, 60, 3))[step]
        for unit in range(*span):
            total = own[stream][unit, pl.ds(keep, length)]
            for k in range(count):
                total += landed[stream][unit, pl.ds(offset + k * length, length)]
            own[stream][unit, pl.ds(keep, length)] = total

    def advance(phase, step):
        for stream in range(STREAMS):
            if (phase, stream) not in PHASE_SPANS:
                continue
            if step == 0:
                for piece in PHASES[phase]:
                    if (piece, stream) in PIECE_SPANS:
                        first_hop(piece, stream).wait()
                        add_landed(stream, PIECE_SPANS[piece, stream], 0)
            else:
                for copy in hops(phase, stream, step):
                    copy.wait()
                add_landed(stream, PHASE_SPANS[phase, stream], step)
            if step < LEVELS - 1:
                for copy in hops(phase, stream, step + 1):
                    copy.start()

    def y_slots(yy):
        return [slot_of({"y": yy, "x": 0, "z": 0}, stream) for stream in range(STREAMS)]

    def spread_pupil(m):
        core_copy(m, 0).wait()
        core_copy(m, 1).wait()

        def body(yy, carry):
            begin = y_slots(yy)
            for xx in range(4):
                for zz in range(4):
                    at = {"y": 0, "x": xx, "z": zz}
                    cols = slice(zz * 128, (zz + 1) * 128)
                    for g in range(4):
                        stream, unit = PLACE[m, g]
                        rows = slice(yy * 128 + xx * 32 + g * 8, yy * 128 + xx * 32 + g * 8 + 8)
                        slot = begin[stream] + slot_of(at, stream)
                        own[stream][unit, slot] = field[core, m, rows, cols] + peer[m, rows, cols]
            return carry

        for yy in range(4):
            body(yy, 0)
        launch(m)

    def grad_copy(i):
        rows = pl.ds(i * H, H)
        return pltpu.make_async_remote_copy(
            src_ref=grads.at[other, rows], dst_ref=peer_grad.at[rows],
            send_sem=(core_send.at[8], core_send.at[10])[i], recv_sem=(core_recv.at[8], core_recv.at[10])[i],
            device_id=partner, device_id_type=MESH)

    mark_copy = pltpu.make_async_remote_copy(
        src_ref=mark, dst_ref=part_mark, send_sem=core_send.at[9],
        recv_sem=core_recv.at[9], device_id=partner, device_id_type=MESH)

    def backward(m, between=()):
        weigh_fold(m)
        for i in range(2):
            transform(m, i)
            if m == 0 and i == 0:
                pl.semaphore_wait(barrier, len(greeted))
            if m == MODES - 1:
                grad_copy(i).start()
            core_copy(m, i).start()
            if i == 0:
                for task, *values in between:
                    task(*values)

    along = lax.broadcasted_iota(jnp.int32, (N, 128), 1).astype(F32)
    down = lax.broadcasted_iota(jnp.int32, (N, 128), 0).astype(F32)

    def wrap(value):
        return jnp.where(value >= float(N), value - float(N), value)

    def one_hots(shifts):
        for b in range(4):
            at = slice(b * 128, (b + 1) * 128)
            to = wrap(along[:1] + float(b * 128) + shifts[0, :1, :])
            hit = (down == wrap(to)).astype(F32).astype(BF16)
            shift_rows[:, at] = hit
            shift_rows[:, N + b * 128:N + (b + 1) * 128] = hit
            to = wrap(down + shifts[1, :1, :])
            hit = (along + float(b * 128) == wrap(to)).astype(F32).astype(BF16)
            shift_cols[:N, at] = hit
            shift_cols[N:, at] = hit

    def roll(whole, shifts, number):
        one_hots(shifts)
        coarse = whole.astype(BF16)
        parts[:N, :] = coarse
        parts[N:, :] = (whole - coarse.astype(F32)).astype(BF16)
        whole = dot(shift_rows[...], parts[...])
        coarse = whole.astype(BF16)
        parts_t[:, :N] = coarse
        parts_t[:, N:] = (whole - coarse.astype(F32)).astype(BF16)
        folded[number] = dot(parts_t[...], shift_cols[...])

    backward(0)
    mark_copy.start()
    backward(1, ((spread_pupil, 0),))
    backward(2, ((spread_pupil, 1),))
    backward(3, ((spread_pupil, 2),))
    mark_copy.wait()
    roll(grads[core], mark, 0)
    advance(0, 0)
    grad_copy(0).wait()
    grad_copy(1).wait()
    roll(peer_grad[...], part_mark, 1)
    spread_pupil(3)

    iota_r = lax.broadcasted_iota(jnp.int32, (8, 128), 0).astype(F32)
    iota_c = lax.broadcasted_iota(jnp.int32, (8, 128), 1).astype(F32)

    def window(yy, carry):
        begin = y_slots(yy)
        for xx in range(4):
            for zz in range(2):
                for g in range(2):
                    base = yy * 64 + (256 * zz + xx * 16 + g * 8)
                    rows = slice(base, base + 8)
                    row_no = iota_r + float(base)
                    row_a = row_no < mark[0]
                    row_b = row_no < part_mark[0]
                    for block in range(4):
                        cols = slice(block * 128, (block + 1) * 128)
                        col_no = iota_c + float(block * 128)
                        col_a = col_no < mark[1]
                        col_b = col_no < part_mark[1]
                        value_a = folded[0, rows, cols]
                        value_b = folded[1, rows, cols]
                        ra1 = jnp.where(row_a, value_a, 0.0)
                        ra0 = value_a - ra1
                        rb1 = jnp.where(row_b, value_b, 0.0)
                        rb0 = value_b - rb1
                        for upper, (va, vb) in enumerate(((ra0, rb0), (ra1, rb1))):
                            va1 = jnp.where(col_a, va, 0.0)
                            vb1 = jnp.where(col_b, vb, 0.0)
                            tiles = ((va - va1) + (vb - vb1), va1 + vb1)
                            at = {"y": 0, "x": xx, "z": 2 * upper + zz}
                            for later in range(2):
                                stream, unit = PLACE[CANVAS, g * 8 + later * 4 + block]
                                own[stream][unit, begin[stream] + slot_of(at, stream)] = tiles[later]
        return carry

    for yy in range(4):
        window(yy, 0)
    launch(CANVAS)

    for phase, step in BEFORE:
        advance(phase, step)

    for m in range(MODES):
        for g in range(4):
            stream, unit = PLACE[m, g]
            pupil_src[m, g * 8:(g + 1) * 8, :] = own[stream][unit, final_slot(stream)]
    block = pl.ds(pl.multiple_of((core * 4 + z) * 128, 128), 128)
    copies = []
    for number, (c, d) in enumerate(column):
        to_core = (core + c) % 2
        copies.append(pltpu.make_async_remote_copy(
            src_ref=pupil_src.at[:, pl.ds(pl.multiple_of(to_core * 16, 16), 16), :],
            dst_ref=out_pup.at[:, :, block],
            send_sem=gather_send.at[number], recv_sem=gather_recv.at[number],
            device_id=device(y, x, to_core, (z + d) % 4), device_id_type=MESH))
        copies[-1].start()
    out_pup[:, :, block] = pupil_src[:, pl.ds(pl.multiple_of(core * 16, 16), 16), :]

    for phase, step in AFTER:
        advance(phase, step)

    for g in range(2):
        for b in range(8):
            stream, unit = PLACE[CANVAS, g * 8 + b]
            canvas_src[g, :, b * 128:(b + 1) * 128] = own[stream][unit, final_slot(stream)]
    half_cols = pl.ds(pl.multiple_of(core * SPEC, SPEC), SPEC)
    last = pltpu.make_async_remote_copy(
        src_ref=canvas_src.at[other], dst_ref=out_spec.at[0, :, half_cols],
        send_sem=gather_send.at[7], recv_sem=gather_recv.at[7], device_id=partner, device_id_type=MESH)
    last.start()
    out_spec[0, :, half_cols] = canvas_src[core]
    for copy in copies:
        copy.wait()
    last.wait()


def hand_over(spec_in, pup_in, spec_out, pup_out):
    spec_out[...] = spec_in[...]
    pup_out[...] = pup_in[...]


def local(spectrum, pupils, offsets, measured):
    vmem = pl.BlockSpec(memory_space=pltpu.VMEM)
    half, half_t, swap = (jnp.asarray(table) for table in tables())
    scratch = [
        pltpu.VMEM((2, N, N), BF16),
        pltpu.VMEM((2, MODES, N, N), F32),
        pltpu.VMEM((N, N), F32),
        pltpu.VMEM((N, N), BF16),
        pltpu.VMEM((2, 2, N, N), BF16),
        pltpu.VMEM((2, N, N), F32),
        pltpu.VMEM((2, N, N), F32),
        pltpu.VMEM((N, 2 * N), BF16),
        pltpu.VMEM((2 * N, N), BF16),
        pltpu.VMEM((2 * N, N), BF16),
        pltpu.VMEM((N, 2 * N), BF16),
        pltpu.VMEM((N, N), F32),
        pltpu.VMEM((2, 8, 128), F32),
        pltpu.VMEM((MODES, N, N), F32),
        pltpu.VMEM((MODES, 32, 128), F32),
        pltpu.VMEM((2, 8, SPEC), F32),
        pltpu.VMEM((MODES, N, 2 * N), BF16),
        pltpu.VMEM((2, 8, 128), F32),
        pltpu.VMEM((N, 2 * N), BF16),
        pltpu.VMEM((SPEC, 2 * SPEC), BF16),
        pltpu.VMEM((1, N, N), BF16),
        pltpu.VMEM((N, N), BF16),
        pltpu.VMEM((N, N), BF16),
        pltpu.VMEM((H, H), BF16),
        pltpu.VMEM((N, SPEC), BF16),
        pltpu.VMEM((SPEC, N), BF16),
    ]
    scratch += [pltpu.VMEM((count, 64, 8, 128), F32) for count in COUNTS]
    scratch += [pltpu.VMEM((count, 63, 8, 128), F32) for count in COUNTS]
    scratch += [pltpu.SemaphoreType.DMA((11,)), pltpu.SemaphoreType.DMA((11,))]
    scratch += [pltpu.SemaphoreType.DMA((len(PIECES), STREAMS)), pltpu.SemaphoreType.DMA((len(PIECES), STREAMS))]
    scratch += [pltpu.SemaphoreType.DMA((len(PHASES), STREAMS, 7)), pltpu.SemaphoreType.DMA((len(PHASES), STREAMS, 7))]
    scratch += [pltpu.SemaphoreType.DMA((8,)), pltpu.SemaphoreType.DMA((8,)), pltpu.SemaphoreType.DMA((MODES + 6,))]
    outs = tuple(pl.pallas_call(
        kernel,
        out_shape=(
            jax.ShapeDtypeStruct((1, 8, 2 * SPEC), F32),
            jax.ShapeDtypeStruct((MODES, 16, 2 * N), F32),
        ),
        in_specs=[vmem] + [pl.BlockSpec(memory_space=pl.ANY)] * 6,
        out_specs=(vmem, vmem),
        scratch_shapes=scratch,
        compiler_params=pltpu.CompilerParams(
            collective_id=0, has_side_effects=True, vmem_limit_bytes=60 * 2**20),
    )(offsets, spectrum, pupils, measured, half, half_t, swap))
    return tuple(pl.pallas_call(
        hand_over,
        out_shape=tuple(jax.ShapeDtypeStruct(out.shape, F32) for out in outs),
        in_specs=[vmem] * 2,
        out_specs=(vmem, vmem),
    )(*outs))


def solution(mesh):
    return jax.shard_map(
        local,
        mesh=mesh,
        in_specs=(P(), P(), P(("led", "tile"), None), P(("led", "tile"), None, None)),
        out_specs=(P("tile", "led", None), P(None, "led", None)),
        check_vma=False,
    )
```

```python
import math

import jax
import jax.numpy as jnp
import numpy as np
from jax import lax
from jax.experimental import pallas as pl
from jax.experimental.pallas import tpu as pltpu
from jax.sharding import PartitionSpec as P

MESH = pl.DeviceIdType.MESH
N = 512
H = 256
MODES = 4
SPEC = 1024
F32 = jnp.float32
BF16 = jnp.bfloat16

ORDERS = (("y", 0, "x", "z"), ("x", 0, "z", "y"), ("z", 0, "y", "x"),
          ("y", 1, "z", "x"), ("x", 1, "y", "z"), ("z", 1, "x", "y"))
LEVELS = 4

STREAMS = 6
PIECES = (
    (3, 4, 4, 5),
    (0, 1, 2, 5),
    (0, 2, 3, 5),
    (3, 4, 4, 5),
    (0, 0, 0, 1, 1, 1, 2, 2, 2, 3, 3, 4, 4, 5, 5, 5),
)
CANVAS = 4
PHASES = ((0, 1), (2, 3), (4,))
BEFORE = ((1, 0), (0, 1), (2, 0), (0, 2), (1, 1), (2, 1), (0, 3), (1, 2), (2, 2), (1, 3))
AFTER = ((2, 3),)


def plan():
    counts = [0] * STREAMS
    place, pieces, phases = {}, {}, {}
    for number, streams in enumerate(PIECES):
        first = list(counts)
        for unit, stream in enumerate(streams):
            place[number, unit] = (stream, counts[stream])
            counts[stream] += 1
        for stream in range(STREAMS):
            if counts[stream] > first[stream]:
                pieces[number, stream] = (first[stream], counts[stream])
    for number, members in enumerate(PHASES):
        for stream in range(STREAMS):
            spans = [pieces[member, stream] for member in members if (member, stream) in pieces]
            if spans:
                phases[number, stream] = (spans[0][0], spans[-1][1])
    return counts, place, pieces, phases


COUNTS, PLACE, PIECE_SPANS, PHASE_SPANS = plan()


def tables():
    positions = np.arange(N, dtype=np.int64)
    angles = (positions[:, None] * positions[None, :] % N).astype(np.float32) * np.float32(2.0 * math.pi / N)
    factor = np.float32(1.0 / math.sqrt(N))
    cosine = (np.cos(angles) * factor).astype(BF16)
    sine = (np.sin(angles) * factor).astype(BF16)
    half = np.concatenate([cosine[:H], sine[:H]], axis=0)
    half[H] = cosine[H]
    swap = np.zeros((H, H), np.float32)
    swap[(H - np.arange(H)) % H, np.arange(H)] = 1.0
    return half, np.ascontiguousarray(half.T), swap.astype(BF16)


def low_bit(position):
    return ((position + 1) // 2) % 2


def high_bit(position):
    return position // 2


def slot_of(at, stream):
    axis, bit, second, third = ORDERS[stream]
    bits = low_bit(at[axis]), high_bit(at[axis])
    return ((bits[bit] * 2 + bits[1 - bit]) * 4 + at[second]) * 4 + at[third]


def dot(a, b):
    return jnp.dot(a, b, preferred_element_type=F32)


def kernel(offs, spectrum, pupils, measured, table, table_t, swap_in, out_spec, out_pup, *scratch):
    (half_s, field, inten, measp, folds, grads, folded, shift_rows, shift_cols, parts, parts_t, peer_grad, part_mark,
     peer, pupil_src, canvas_src, pup, mark, patch, whole, meas, tab, tabt, swap, pick_row, pick_col) = scratch[:26]
    own = scratch[26:32]
    landed = scratch[32:38]
    (core_send, core_recv, send0, recv0, send, recv, gather_send, gather_recv, load) = scratch[38:]

    def pupil_load(m):
        return pltpu.make_async_copy(pupils.at[m], pup.at[m], load.at[m])

    loads = [
        pltpu.make_async_copy(source, target, load.at[MODES + number])
        for number, (source, target) in enumerate((
            (spectrum.at[:, :SPEC], whole.at[:, :SPEC]), (table, tab), (table_t, tabt), (measured, meas), (swap_in, swap),
            (spectrum.at[:, SPEC:], whole.at[:, SPEC:])))
    ]
    loads[0].start()
    loads[5].start()
    loads[1].start()
    pupil_load(0).start()
    for copy in loads[2:5]:
        copy.start()
    for m in range(1, MODES):
        pupil_load(m).start()


    led = lax.axis_index("led")
    z = lax.axis_index("tile")
    core = led % 2
    x = (led // 2) % 4
    y = led // 8
    other = 1 - core

    def device(yy, xx, cc, zz):
        return ((yy * 4 + xx) * 2 + cc, zz)

    def low(p):
        return p + 1 - 2 * (p % 2)

    def high(p):
        return 3 - p

    here = {"y": y, "x": x, "z": z}

    def moved(axis, position):
        there = dict(here, **{axis: position})
        return device(there["y"], there["x"], core, there["z"])

    partner = device(y, x, other, z)
    column = [(c, d) for d in range(4) for c in range(2) if (c, d) != (0, 0)]

    barrier = pltpu.get_barrier_semaphore()
    greeted = [moved(axis, (here[axis] + k) % 4) for axis in ("y", "x") for k in range(1, 4)]
    greeted += [device(y, x, (core + c) % 2, (z + d) % 4) for c, d in column]
    for target in greeted:
        pl.semaphore_signal(barrier, inc=1, device_id=target, device_id_type=MESH)

    mark[0] = jnp.broadcast_to(offs[:, 0:1], (8, 128)).astype(F32)
    mark[1] = jnp.broadcast_to(offs[:, 1:2], (8, 128)).astype(F32)
    rise = lax.broadcasted_iota(jnp.int32, (N, 128), 1) - lax.broadcasted_iota(jnp.int32, (N, 128), 0)
    fall = lax.broadcasted_iota(jnp.int32, (SPEC, 128), 0) - lax.broadcasted_iota(jnp.int32, (SPEC, 128), 1)
    for b in range(8):
        pick_row[:, b * 128:(b + 1) * 128] = (
            rise.astype(F32) == mark[0, :1, :] - float(b * 128)).astype(F32).astype(BF16)
    for b in range(4):
        pick_col[:, b * 128:(b + 1) * 128] = (
            fall.astype(F32) == mark[1, :1, :] + float(b * 128)).astype(F32).astype(BF16)
    for number in range(2):
        loads[5 * number].wait()
        window = dot(pick_row[...], whole[:, number * SPEC:(number + 1) * SPEC]).astype(BF16)
        patch[:, number * N:(number + 1) * N] = dot(window, pick_col[...]).astype(BF16)

    inten[...] = jnp.zeros_like(inten)
    for copy in loads[1:3]:
        copy.wait()

    lane0 = lax.broadcasted_iota(jnp.int32, (1, 128), 1) == 0
    row0 = lax.broadcasted_iota(jnp.int32, (16, 1), 0) == 0

    def forward(m, carry):
        pupil_load(m).wait()
        for c in range(2):
            cols = slice(c * H, (c + 1) * H)
            cols_i = slice(N + c * H, N + (c + 1) * H)
            pr = patch[:, cols].astype(F32)
            pi = patch[:, cols_i].astype(F32)
            qr = pup[m, :, cols].astype(F32)
            qi = pup[m, :, cols_i].astype(F32)
            er = (pr * qr - pi * qi).astype(BF16)
            ei = (pr * qi + pi * qr).astype(BF16)
            u = dot(tab[...], er)
            v = dot(tab[...], ei)
            half_s[0, :H, cols] = (u[:H] - v[H:]).astype(BF16)
            half_s[0, H:, cols] = (u[:H] + v[H:]).astype(BF16)
            half_s[1, :H, cols] = (v[:H] + u[H:]).astype(BF16)
            half_s[1, H:, cols] = (v[:H] - u[H:]).astype(BF16)
            ut, ub, vt, vb = u[:16], u[H:H + 16], v[:16], v[H:H + 16]
            half_s[0, :16, cols] = jnp.where(row0, ut, ut - vb).astype(BF16)
            half_s[0, H:H + 16, cols] = jnp.where(row0, ub, ut + vb).astype(BF16)
            half_s[1, :16, cols] = jnp.where(row0, vt, vt + ub).astype(BF16)
            half_s[1, H:H + 16, cols] = jnp.where(row0, vb, vt - ub).astype(BF16)
        for r in range(2):
            rows = slice(r * H, (r + 1) * H)
            u = dot(half_s[0, rows, :], tabt[...])
            v = dot(half_s[1, rows, :], tabt[...])
            for b in range(2):
                left = slice(b * 128, (b + 1) * 128)
                right = slice(H + b * 128, H + (b + 1) * 128)
                uc, us, vc, vs = u[:, left], u[:, right], v[:, left], v[:, right]
                rl, il, rr, ir = uc - vs, vc + us, uc + vs, vc - us
                if b == 0:
                    rl = jnp.where(lane0, uc, rl)
                    il = jnp.where(lane0, vc, il)
                    rr = jnp.where(lane0, us, rr)
                    ir = jnp.where(lane0, vs, ir)
                field[0, m, rows, left] = rl
                field[1, m, rows, left] = il
                field[0, m, rows, right] = rr
                field[1, m, rows, right] = ir
                inten[rows, left] += rl * rl + il * il
                inten[rows, right] += rr * rr + ir * ir
        return carry

    lax.fori_loop(0, MODES, forward, 0, unroll=2)

    for copy in loads[3:5]:
        copy.wait()
    measp[:, :H] = meas[0, :, :H]
    measp[:, H:] = dot(meas[0, :, H:], swap[...]).astype(BF16)
    measp[H:, :] = dot(swap[...], measp[H:, :]).astype(BF16)

    def weigh(i, carry):
        rows = pl.ds(pl.multiple_of(i * 64, 64), 64)
        level = measp[rows, :].astype(F32)
        inten[rows, :] = 1.0 - level * lax.rsqrt(level * jnp.maximum(inten[rows, :], 0.1))
        return carry

    lax.fori_loop(0, N // 64, weigh, 0, unroll=8)

    def weigh_fold(m):
        xs = folds.at[m % 2]
        for i in range(H // 32):
            top = slice(i * 32, i * 32 + 32)
            bottom = slice(H + i * 32, H + i * 32 + 32)
            wt, wb = inten[top, :], inten[bottom, :]
            rt, rb = wt * field[0, m, top, :], wb * field[0, m, bottom, :]
            it, ib = wt * field[1, m, top, :], wb * field[1, m, bottom, :]
            xs[0, top, :] = (rt + rb).astype(BF16)
            xs[0, bottom, :] = (it - ib).astype(BF16)
            xs[1, top, :] = (it + ib).astype(BF16)
            xs[1, bottom, :] = (rb - rt).astype(BF16)
        wt, wb = inten[:16, :], inten[H:H + 16, :]
        rt, rb = wt * field[0, m, :16, :], wb * field[0, m, H:H + 16, :]
        it, ib = wt * field[1, m, :16, :], wb * field[1, m, H:H + 16, :]
        xs[0, :16, :] = jnp.where(row0, rt, rt + rb).astype(BF16)
        xs[0, H:H + 16, :] = jnp.where(row0, rb, it - ib).astype(BF16)
        xs[1, :16, :] = jnp.where(row0, it, it + ib).astype(BF16)
        xs[1, H:H + 16, :] = jnp.where(row0, ib, rb - rt).astype(BF16)

    def transform(m, i):
        xs = folds.at[m % 2]
        rows = slice(i * H, (i + 1) * H)
        fr = dot(tabt[rows, :], xs[0])
        fi = dot(tabt[rows, :], xs[1])
        for b in range(2):
            left = slice(b * 128, (b + 1) * 128)
            right = slice(H + b * 128, H + (b + 1) * 128)
            rl, rr, il, ir = fr[:, left], fr[:, right], fi[:, left], fi[:, right]
            pr, mi, p_i, mr = rl + rr, il - ir, il + ir, rr - rl
            if b == 0:
                pr = jnp.where(lane0, rl, pr)
                mi = jnp.where(lane0, rr, mi)
                p_i = jnp.where(lane0, il, p_i)
                mr = jnp.where(lane0, ir, mr)
            half_s[0, rows, left] = pr.astype(BF16)
            half_s[0, rows, right] = mi.astype(BF16)
            half_s[1, rows, left] = p_i.astype(BF16)
            half_s[1, rows, right] = mr.astype(BF16)
        gr = dot(half_s[0, rows, :], tab[...])
        gi = dot(half_s[1, rows, :], tab[...])
        qr, qi = pup[m, rows, :N].astype(F32), pup[m, rows, N:].astype(F32)
        sr = qr * gr + qi * gi
        si = qr * gi - qi * gr
        if m == 0:
            grads[0, rows, :] = sr
            grads[1, rows, :] = si
        else:
            grads[0, rows, :] += sr
            grads[1, rows, :] += si
        pr, pi = patch[rows, :N].astype(F32), patch[rows, N:].astype(F32)
        field[0, m, rows, :] = pr * gr + pi * gi
        field[1, m, rows, :] = pr * gi - pi * gr

    def core_copy(m, i):
        rows = pl.ds(i * H, H)
        return pltpu.make_async_remote_copy(
            src_ref=field.at[other, m, rows], dst_ref=peer.at[m, rows], send_sem=core_send.at[2 * m + i],
            recv_sem=core_recv.at[2 * m + i], device_id=partner, device_id_type=MESH)

    def copy_tiles(stream, span, away, length, offset, sems, target):
        units = pl.ds(span[0], span[1] - span[0])
        return pltpu.make_async_remote_copy(
            src_ref=own[stream].at[units, pl.ds(away, length)],
            dst_ref=landed[stream].at[units, pl.ds(offset, length)],
            send_sem=sems[0], recv_sem=sems[1], device_id=target, device_id_type=MESH)

    def halves(stream):
        axis, bit, second, third = ORDERS[stream]
        bits = low_bit(here[axis]), high_bit(here[axis])
        one = bits[bit] * 32
        return axis, bit, bits, one, one + bits[1 - bit] * 16

    def first_hop(piece, stream):
        axis, bit, bits, _, _ = halves(stream)
        return copy_tiles(stream, PIECE_SPANS[piece, stream], (1 - bits[bit]) * 32, 32, 0,
                          (send0.at[piece, stream], recv0.at[piece, stream]),
                          moved(axis, (low, high)[bit](here[axis])))

    def hops(phase, stream, step):
        span = PHASE_SPANS[phase, stream]
        axis, bit, bits, one, two = halves(stream)

        def sems(number):
            return send.at[phase, stream, number], recv.at[phase, stream, number]

        if step == 1:
            return [copy_tiles(stream, span, one + (1 - bits[1 - bit]) * 16, 16, 32, sems(0),
                               moved(axis, (low, high)[1 - bit](here[axis])))]
        ring = ORDERS[stream][step]
        out = []
        for k in (2, 1, 3):
            to = (here[ring] + k) % 4
            if step == 2:
                away, length, offset = two + to * 4, 4, 48 + 4 * (k - 1)
            else:
                away, length, offset = two + here[ORDERS[stream][2]] * 4 + to, 1, 60 + (k - 1)
            out.append(copy_tiles(stream, span, away, length, offset, sems(3 * step - 6 + k), moved(ring, to)))
        return out

    def final_slot(stream):
        return slot_of(here, stream)

    def launch(piece):
        for stream in range(STREAMS):
            if (piece, stream) in PIECE_SPANS:
                first_hop(piece, stream).start()

    def add_landed(stream, span, step):
        _, _, _, one, two = halves(stream)
        second, third = (here[axis] for axis in ORDERS[stream][2:])
        keep, length, offset, count = (
            (one, 32, 0, 1), (two, 16, 32, 1), (two + second * 4, 4, 48, 3),
            (two + second * 4 + third, 1, 60, 3))[step]
        for unit in range(*span):
            total = own[stream][unit, pl.ds(keep, length)]
            for k in range(count):
                total += landed[stream][unit, pl.ds(offset + k * length, length)]
            own[stream][unit, pl.ds(keep, length)] = total

    def advance(phase, step):
        for stream in range(STREAMS):
            if (phase, stream) not in PHASE_SPANS:
                continue
            if step == 0:
                for piece in PHASES[phase]:
                    if (piece, stream) in PIECE_SPANS:
                        first_hop(piece, stream).wait()
                        add_landed(stream, PIECE_SPANS[piece, stream], 0)
            else:
                for copy in hops(phase, stream, step):
                    copy.wait()
                add_landed(stream, PHASE_SPANS[phase, stream], step)
            if step < LEVELS - 1:
                for copy in hops(phase, stream, step + 1):
                    copy.start()

    def y_slots(yy):
        return [slot_of({"y": yy, "x": 0, "z": 0}, stream) for stream in range(STREAMS)]

    def spread_pupil(m):
        core_copy(m, 0).wait()
        core_copy(m, 1).wait()

        def body(yy, carry):
            begin = y_slots(yy)
            for xx in range(4):
                for zz in range(4):
                    at = {"y": 0, "x": xx, "z": zz}
                    cols = slice(zz * 128, (zz + 1) * 128)
                    for g in range(4):
                        stream, unit = PLACE[m, g]
                        rows = slice(yy * 128 + xx * 32 + g * 8, yy * 128 + xx * 32 + g * 8 + 8)
                        slot = begin[stream] + slot_of(at, stream)
                        own[stream][unit, slot] = field[core, m, rows, cols] + peer[m, rows, cols]
            return carry

        for yy in range(4):
            body(yy, 0)
        launch(m)

    def grad_copy(i):
        rows = pl.ds(i * H, H)
        return pltpu.make_async_remote_copy(
            src_ref=grads.at[other, rows], dst_ref=peer_grad.at[rows],
            send_sem=(core_send.at[8], core_send.at[10])[i], recv_sem=(core_recv.at[8], core_recv.at[10])[i],
            device_id=partner, device_id_type=MESH)

    mark_copy = pltpu.make_async_remote_copy(
        src_ref=mark, dst_ref=part_mark, send_sem=core_send.at[9],
        recv_sem=core_recv.at[9], device_id=partner, device_id_type=MESH)

    def backward(m, between=()):
        weigh_fold(m)
        for i in range(2):
            transform(m, i)
            if m == 0 and i == 0:
                pl.semaphore_wait(barrier, len(greeted))
            if m == MODES - 1:
                grad_copy(i).start()
            core_copy(m, i).start()
            if i == 0:
                for task, *values in between:
                    task(*values)

    along = lax.broadcasted_iota(jnp.int32, (N, 128), 1).astype(F32)
    down = lax.broadcasted_iota(jnp.int32, (N, 128), 0).astype(F32)

    def wrap(value):
        return jnp.where(value >= float(N), value - float(N), value)

    def one_hots(shifts):
        for b in range(4):
            at = slice(b * 128, (b + 1) * 128)
            to = wrap(along[:1] + float(b * 128) + shifts[0, :1, :])
            hit = (down == wrap(to)).astype(F32).astype(BF16)
            shift_rows[:, at] = hit
            shift_rows[:, N + b * 128:N + (b + 1) * 128] = hit
            to = wrap(down + shifts[1, :1, :])
            hit = (along + float(b * 128) == wrap(to)).astype(F32).astype(BF16)
            shift_cols[:N, at] = hit
            shift_cols[N:, at] = hit

    def roll(whole, shifts, number):
        one_hots(shifts)
        coarse = whole.astype(BF16)
        parts[:N, :] = coarse
        parts[N:, :] = (whole - coarse.astype(F32)).astype(BF16)
        whole = dot(shift_rows[...], parts[...])
        coarse = whole.astype(BF16)
        parts_t[:, :N] = coarse
        parts_t[:, N:] = (whole - coarse.astype(F32)).astype(BF16)
        folded[number] = dot(parts_t[...], shift_cols[...])

    backward(0)
    mark_copy.start()
    backward(1, ((spread_pupil, 0),))
    backward(2, ((spread_pupil, 1),))
    backward(3, ((spread_pupil, 2),))
    mark_copy.wait()
    roll(grads[core], mark, 0)
    advance(0, 0)
    grad_copy(0).wait()
    grad_copy(1).wait()
    roll(peer_grad[...], part_mark, 1)
    spread_pupil(3)

    iota_r = lax.broadcasted_iota(jnp.int32, (8, 128), 0).astype(F32)
    iota_c = lax.broadcasted_iota(jnp.int32, (8, 128), 1).astype(F32)

    def window(yy, carry):
        begin = y_slots(yy)
        for xx in range(4):
            for zz in range(2):
                for g in range(2):
                    base = yy * 64 + (256 * zz + xx * 16 + g * 8)
                    rows = slice(base, base + 8)
                    row_no = iota_r + float(base)
                    row_a = row_no < mark[0]
                    row_b = row_no < part_mark[0]
                    for block in range(4):
                        cols = slice(block * 128, (block + 1) * 128)
                        col_no = iota_c + float(block * 128)
                        col_a = col_no < mark[1]
                        col_b = col_no < part_mark[1]
                        value_a = folded[0, rows, cols]
                        value_b = folded[1, rows, cols]
                        ra1 = jnp.where(row_a, value_a, 0.0)
                        ra0 = value_a - ra1
                        rb1 = jnp.where(row_b, value_b, 0.0)
                        rb0 = value_b - rb1
                        for upper, (va, vb) in enumerate(((ra0, rb0), (ra1, rb1))):
                            va1 = jnp.where(col_a, va, 0.0)
                            vb1 = jnp.where(col_b, vb, 0.0)
                            tiles = ((va - va1) + (vb - vb1), va1 + vb1)
                            at = {"y": 0, "x": xx, "z": 2 * upper + zz}
                            for later in range(2):
                                stream, unit = PLACE[CANVAS, g * 8 + later * 4 + block]
                                own[stream][unit, begin[stream] + slot_of(at, stream)] = tiles[later]
        return carry

    for yy in range(4):
        window(yy, 0)
    launch(CANVAS)

    for phase, step in BEFORE:
        advance(phase, step)

    for m in range(MODES):
        for g in range(4):
            stream, unit = PLACE[m, g]
            pupil_src[m, g * 8:(g + 1) * 8, :] = own[stream][unit, final_slot(stream)]
    block = pl.ds(pl.multiple_of((core * 4 + z) * 128, 128), 128)
    copies = []
    for number, (c, d) in enumerate(column):
        to_core = (core + c) % 2
        copies.append(pltpu.make_async_remote_copy(
            src_ref=pupil_src.at[:, pl.ds(pl.multiple_of(to_core * 16, 16), 16), :],
            dst_ref=out_pup.at[:, :, block],
            send_sem=gather_send.at[number], recv_sem=gather_recv.at[number],
            device_id=device(y, x, to_core, (z + d) % 4), device_id_type=MESH))
        copies[-1].start()
    out_pup[:, :, block] = pupil_src[:, pl.ds(pl.multiple_of(core * 16, 16), 16), :]

    for phase, step in AFTER:
        advance(phase, step)

    for g in range(2):
        for b in range(8):
            stream, unit = PLACE[CANVAS, g * 8 + b]
            canvas_src[g, :, b * 128:(b + 1) * 128] = own[stream][unit, final_slot(stream)]
    half_cols = pl.ds(pl.multiple_of(core * SPEC, SPEC), SPEC)
    last = pltpu.make_async_remote_copy(
        src_ref=canvas_src.at[other], dst_ref=out_spec.at[0, :, half_cols],
        send_sem=gather_send.at[7], recv_sem=gather_recv.at[7], device_id=partner, device_id_type=MESH)
    last.start()
    out_spec[0, :, half_cols] = canvas_src[core]
    for copy in copies:
        copy.wait()
    last.wait()


def hand_over(spec_in, pup_in, spec_out, pup_out):
    spec_out[...] = spec_in[...]
    pup_out[...] = pup_in[...]


def local(spectrum, pupils, offsets, measured):
    vmem = pl.BlockSpec(memory_space=pltpu.VMEM)
    half, half_t, swap = (jnp.asarray(table) for table in tables())
    scratch = [
        pltpu.VMEM((2, N, N), BF16),
        pltpu.VMEM((2, MODES, N, N), F32),
        pltpu.VMEM((N, N), F32),
        pltpu.VMEM((N, N), BF16),
        pltpu.VMEM((2, 2, N, N), BF16),
        pltpu.VMEM((2, N, N), F32),
        pltpu.VMEM((2, N, N), F32),
        pltpu.VMEM((N, 2 * N), BF16),
        pltpu.VMEM((2 * N, N), BF16),
        pltpu.VMEM((2 * N, N), BF16),
        pltpu.VMEM((N, 2 * N), BF16),
        pltpu.VMEM((N, N), F32),
        pltpu.VMEM((2, 8, 128), F32),
        pltpu.VMEM((MODES, N, N), F32),
        pltpu.VMEM((MODES, 32, 128), F32),
        pltpu.VMEM((2, 8, SPEC), F32),
        pltpu.VMEM((MODES, N, 2 * N), BF16),
        pltpu.VMEM((2, 8, 128), F32),
        pltpu.VMEM((N, 2 * N), BF16),
        pltpu.VMEM((SPEC, 2 * SPEC), BF16),
        pltpu.VMEM((1, N, N), BF16),
        pltpu.VMEM((N, N), BF16),
        pltpu.VMEM((N, N), BF16),
        pltpu.VMEM((H, H), BF16),
        pltpu.VMEM((N, SPEC), BF16),
        pltpu.VMEM((SPEC, N), BF16),
    ]
    scratch += [pltpu.VMEM((count, 64, 8, 128), F32) for count in COUNTS]
    scratch += [pltpu.VMEM((count, 63, 8, 128), F32) for count in COUNTS]
    scratch += [pltpu.SemaphoreType.DMA((11,)), pltpu.SemaphoreType.DMA((11,))]
    scratch += [pltpu.SemaphoreType.DMA((len(PIECES), STREAMS)), pltpu.SemaphoreType.DMA((len(PIECES), STREAMS))]
    scratch += [pltpu.SemaphoreType.DMA((len(PHASES), STREAMS, 7)), pltpu.SemaphoreType.DMA((len(PHASES), STREAMS, 7))]
    scratch += [pltpu.SemaphoreType.DMA((8,)), pltpu.SemaphoreType.DMA((8,)), pltpu.SemaphoreType.DMA((MODES + 6,))]
    outs = tuple(pl.pallas_call(
        kernel,
        out_shape=(
            jax.ShapeDtypeStruct((1, 8, 2 * SPEC), F32),
            jax.ShapeDtypeStruct((MODES, 16, 2 * N), F32),
        ),
        in_specs=[vmem] + [pl.BlockSpec(memory_space=pl.ANY)] * 6,
        out_specs=(vmem, vmem),
        scratch_shapes=scratch,
        compiler_params=pltpu.CompilerParams(
            collective_id=0, has_side_effects=True, vmem_limit_bytes=60 * 2**20),
    )(offsets, spectrum, pupils, measured, half, half_t, swap))
    return tuple(pl.pallas_call(
        hand_over,
        out_shape=tuple(jax.ShapeDtypeStruct(out.shape, F32) for out in outs),
        in_specs=[vmem] * 2,
        out_specs=(vmem, vmem),
    )(*outs))


def solution(mesh):
    return jax.shard_map(
        local,
        mesh=mesh,
        in_specs=(P(), P(), P(("led", "tile"), None), P(("led", "tile"), None, None)),
        out_specs=(P("tile", "led", None), P(None, "led", None)),
        check_vma=False,
    )
```
